32 devices in a mesh: scene: 2 (over y), tok: 4 (over z), col: 2 (over x), rep: 2 (over core).
Axes of the slice: x: 2, y: 2, z: 4, core: 2. Of those that a mesh axis runs over, the one named last changes fastest.
Arguments:
- tokens: float32 [8192, 512], P(('scene', 'tok'), ('col', 'rep')), parts along dimension 0
- w_qkv: float32 [2, 3, 512, 512], P(None, None, None, ('col', 'rep'))
- w_out: float32 [2, 512, 512], P(None, ('col', 'rep')), may hold values from -0.25 to 0.25
- w_up: float32 [2, 512, 2048], P(None, None, ('col', 'rep')), may hold values from -0.25 to 0.25
- w_down: float32 [2, 2048, 512], P(None, ('col', 'rep')), may hold values from -0.125 to 0.125
- attn_gain: float32 [2, 512], replicated, may hold values from 0.1 to 1.9
- mlp_gain: float32 [2, 512], replicated, may hold values from 0.1 to 1.9
- dest_device: int32 [128], P(('scene', 'tok')), parts along dimension 0, may hold values from 0 to 3, as said below
- dest_slot: int32 [128], P(('scene', 'tok')), parts along dimension 0, may hold values from 0 to 15, as said below
- pillar: int32 [8192], P(('scene', 'tok')), parts along dimension 0, may hold values from -1 to 2047, as said below
- depth_weight: float32 [2, 3, 3, 512], replicated, may hold values from -2 to 2
- point_weight: float32 [2, 512, 1024], replicated, may hold values from -0.25 to 0.25
- raster_gain: float32 [2, 512], replicated, may hold values from 0.1 to 1.9
Outputs:
- raster: float32 [128, 32, 512], P(('scene', 'tok', 'rep'), 'col'), parts along dimension 0
The draws below stay inside these ranges and needn't reach their ends.
There are 2 independent parts, one for each index of `scene`. The reference program is written for one: setup_inputs(seed, part) draws one part's arguments, and reference() takes and returns one part's arrays. A program takes and returns all parts, laid end to end along the dimension named above; an argument that names none is the same for every part. Nothing has to cross between parts.
Inputs may be any that keep to these rules, and one draw needn't show every extreme that they name: `dest_device`: together with dest_slot the blocks fill every index of tok's 16 slots exactly once. At most 5 blocks of one index of tok go to one index, and every index sends exactly 5 blocks to some index. `dest_slot`: the slot of the block among the 16 of its destination. The token at Hilbert position t has a cell in raster rows i * 16 to (i + 1) * 16 - 1 with i = t // 1024, or -1 if it has no pillar; several tokens may share a cell.
All inputs are finite; a program needn't handle non-finite values.
Results may differ from the reference program's by a relative error of at most 0.00012.
Values sent between devices are 32-bit elements; how exact they have to be, the bound alone decides.
No kernel may reach another device: no remote copies, remote signals or barrier semaphores. Data moves between devices by JAX's collectives and lax.ppermute only.
A program may use at most 128 MiB of HBM per device.

```python
import jax
import jax.numpy as jnp
from jax import lax

D = 512
HEADS = 32
FF = 2048
PATCH = 1024
BLOCK = 64
TR = 16
TC = 16
HD = 16
TOK_DEV = 1024
TOKENS = 4096
BLK_DEV = 16
NB = 64
H = 64
W = 32
N_TOK = 4
N_COL = 2


def draw_tokens(key, part):
    first_key = jax.random.fold_in(jax.random.fold_in(key, 3), 0)
    values = jax.random.normal(first_key, (TOKENS, D), jnp.float32)
    return values


def draw_w_qkv(key, part):
    first_key = jax.random.fold_in(jax.random.fold_in(key, 5), 0)
    base = jax.random.normal(first_key, (2, 3, D, D), jnp.float32) * D ** (-0.5)
    return base


def route_tables(key):
    first_key, second_key, third_key, fourth_key = jax.random.split(jax.random.fold_in(key, 29), 4)
    owners = jax.random.permutation(first_key, N_TOK).astype(jnp.int32)
    spread = jax.random.permutation(second_key, BLK_DEV - 2).astype(jnp.int32)
    shifts = jnp.concatenate([jnp.zeros((2,), jnp.int32), 1 + spread % (N_TOK - 1)])

    def permute_single_block(subkey):
        return jax.random.permutation(subkey, BLK_DEV).astype(jnp.int32)
    order = jax.vmap(permute_single_block)(jax.random.split(third_key, N_TOK))
    arrival = jax.vmap(permute_single_block)(jax.random.split(fourth_key, N_TOK))
    source = jnp.arange(N_TOK, dtype=jnp.int32)[:, None]
    target = owners[(source + shifts[order]) % N_TOK]
    slots = arrival[target, order]
    return (target.reshape(-1).astype(jnp.int32), slots.reshape(-1).astype(jnp.int32))


def draw_dest_device(key, part):
    return route_tables(key)[0]


def draw_dest_slot(key, part):
    return route_tables(key)[1]


def draw_pillar(key, part):
    first_key, second_key, third_key = jax.random.split(jax.random.fold_in(key, 41), 3)
    full_width = TC * N_COL
    band = jnp.arange(TOKENS, dtype=jnp.int32) // TOK_DEV
    row_in = jax.random.randint(first_key, (TOKENS,), 0, TR, jnp.int32)
    col_in = jax.random.randint(second_key, (TOKENS,), 0, full_width, jnp.int32)
    present = jax.random.randint(third_key, (TOKENS,), 0, 8, jnp.int32) < 7
    return jnp.where(present, (band * TR + row_in) * full_width + col_in, -1).astype(jnp.int32)


def shard_levels(own_key, dims, pieces, low, high):
    gain = 1.0
    for axis_at, shards_of in pieces:
        draws = jax.random.uniform(jax.random.fold_in(jax.random.fold_in(own_key, 6), axis_at), (shards_of,), jnp.float32, low / len(pieces), high / len(pieces))
        gain = gain * jnp.repeat(jnp.exp(draws), dims[axis_at] // shards_of).reshape((-1,) + (1,) * (len(dims) - 1 - axis_at))
    return gain


def centred(rng, dims, deviation, limit, cuts=(), kind=jnp.bfloat16):
    gain = shard_levels(rng, dims, cuts, -0.22, 0.18) if cuts else 1.0
    array = jax.random.normal(rng, dims, jnp.float32) * deviation * gain
    return jnp.minimum(jnp.maximum(array, -limit), limit).astype(kind)


def setup_inputs(seed: int = 0, part: int = 0) -> dict:
    seeds = jax.random.split(jax.random.key(seed), 14)
    part_keys = jax.random.split(jax.random.fold_in(seeds[13], part), 14)
    tokens = draw_tokens(jax.random.fold_in(jax.random.fold_in(seeds[13], part), 71), part)
    w_qkv = draw_w_qkv(jax.random.fold_in(seeds[13], 71), part)
    w_out = centred(seeds[2], (2, D, D), D ** -0.5, 0.25, ((1, 4),), jnp.float32)
    w_up = centred(seeds[3], (2, D, FF), D ** -0.5, 0.25, ((2, 4),), jnp.float32)
    w_down = centred(seeds[4], (2, FF, D), FF ** -0.5, 0.125, ((1, 4),), jnp.float32)
    attn_gain = jnp.clip(1.0 + 0.18 * jax.random.normal(seeds[5], (2, D), jnp.float32), 0.1, 1.9)
    mlp_gain = jnp.clip(1.0 + 0.18 * jax.random.normal(seeds[6], (2, D), jnp.float32), 0.1, 1.9)
    dest_device = draw_dest_device(jax.random.fold_in(jax.random.fold_in(seeds[13], part), 71), part)
    dest_slot = draw_dest_slot(jax.random.fold_in(jax.random.fold_in(seeds[13], part), 71), part)
    pillar = draw_pillar(jax.random.fold_in(jax.random.fold_in(seeds[13], part), 71), part)
    depth_weight = centred(seeds[10], (2, 3, 3, D), 0.35, 2.0, (), jnp.float32)
    point_weight = centred(seeds[11], (2, D, 2 * D), D ** -0.5, 0.25, (), jnp.float32)
    raster_gain = jnp.clip(1.0 + 0.18 * jax.random.normal(seeds[12], (2, D), jnp.float32), 0.1, 1.9)
    return dict(tokens=tokens, w_qkv=w_qkv, w_out=w_out, w_up=w_up, w_down=w_down, attn_gain=attn_gain, mlp_gain=mlp_gain, dest_device=dest_device, dest_slot=dest_slot, pillar=pillar, depth_weight=depth_weight, point_weight=point_weight, raster_gain=raster_gain)


MATMUL_PRECISION = lax.Precision.HIGHEST
EPSILON = 1e-05

def layer_norm(values, gain_row):
    average = lax.optimization_barrier(jnp.mean(values, axis=-1, keepdims=True))
    centered = values - average
    variance = lax.optimization_barrier(jnp.mean(centered * centered, axis=-1, keepdims=True))
    return centered * lax.rsqrt(variance + EPSILON) * gain_row

def patch_attention(query_projection, key_proj, value_proj):
    scores = jnp.einsum('qhd,khd->hqk', query_projection, key_proj, precision=MATMUL_PRECISION) * HD ** (-0.5)
    scores = scores - lax.optimization_barrier(jnp.max(scores, axis=-1, keepdims=True))
    weights = jnp.exp(scores)
    weights = weights / lax.optimization_barrier(jnp.sum(weights, axis=-1, keepdims=True))
    return jnp.einsum('hqk,khd->qhd', weights, value_proj, precision=MATMUL_PRECISION)

def matmul(left, right):
    return jnp.dot(left, right, precision=MATMUL_PRECISION, preferred_element_type=jnp.float32)

def block_layer(stream, w_qkv, w_out, w_up, w_down, attn_gain, mlp_gain):
    row_count = stream.shape[0]
    normed = layer_norm(stream, attn_gain)
    shaped = tuple((matmul(normed, w_qkv[j]).reshape(row_count // PATCH, PATCH, HEADS, HD) for j in range(3)))

    def attend_patch(operands):
        return patch_attention(operands[0], operands[1], operands[2]).reshape(PATCH, D)
    attended = lax.map(attend_patch, shaped).reshape(row_count, D)
    stream = stream + matmul(attended, w_out)
    normed = layer_norm(stream, mlp_gain)
    hidden = jax.nn.gelu(matmul(normed, w_up), approximate=False)
    return stream + matmul(hidden, w_down)

def raster_layer(raster_grid, depth_weight, point_weight, gain_row):
    row_count, col_count, count_of_channels = raster_grid.shape
    normed = raster_grid * lax.rsqrt(lax.optimization_barrier(jnp.mean(raster_grid * raster_grid, axis=-1, keepdims=True)) + EPSILON) * gain_row
    padded = jnp.pad(normed, ((1, 1), (1, 1), (0, 0)))
    mixed_cells = jnp.zeros_like(raster_grid)
    for row_tap in range(3):
        for col_tap in range(3):
            mixed_cells = mixed_cells + padded[row_tap:row_tap + row_count, col_tap:col_tap + col_count] * depth_weight[row_tap, col_tap]
    combined = matmul(mixed_cells.reshape(row_count * col_count, count_of_channels), point_weight)
    combined = combined.reshape(row_count, col_count, 2 * count_of_channels)
    return raster_grid + combined[..., :count_of_channels] * jax.nn.sigmoid(combined[..., count_of_channels:])

def reference(tokens, w_qkv, w_out, w_up, w_down, attn_gain, mlp_gain, dest_device, dest_slot, pillar, depth_weight, point_weight, raster_gain):
    stream = block_layer(tokens, w_qkv[0], w_out[0], w_up[0], w_down[0], attn_gain[0], mlp_gain[0])
    block_list = stream.reshape(NB, BLOCK, D)
    position = (dest_device * BLK_DEV + dest_slot).astype(jnp.int32)
    reordered_tokens = jnp.zeros_like(block_list).at[position].set(block_list).reshape(TOKENS, D)
    stream = block_layer(reordered_tokens, w_qkv[1], w_out[1], w_up[1], w_down[1], attn_gain[1], mlp_gain[1])
    cell_ids = jnp.where(pillar < 0, H * W, pillar).astype(jnp.int32)
    pooled = jax.ops.segment_sum(stream, cell_ids, num_segments=H * W + 1)[:H * W]
    raster_grid = pooled.reshape(H, W, D)
    for layer_index in range(2):
        raster_grid = raster_layer(raster_grid, depth_weight[layer_index], point_weight[layer_index], raster_gain[layer_index])
    return raster_grid
```

```python
import functools

import jax
import jax.numpy as jnp
from jax import lax
from jax.experimental import pallas as pl
from jax.experimental.pallas import tpu as pltpu
from jax.sharding import PartitionSpec as P

PATCH = 1024
TR = 16
TC = 16
HD = 16
EPSILON = 1e-05
LOG2E = 1.4426950408889634
BF = jnp.bfloat16
F32 = jnp.float32
VMEM_LIMIT = 56 * 2**20
BORDER = 2


def vmem():
    return pl.BlockSpec(memory_space=pltpu.VMEM)


def smem():
    return pl.BlockSpec(memory_space=pltpu.SMEM)


def params():
    return pltpu.CompilerParams(vmem_limit_bytes=VMEM_LIMIT)


def split2(x):
    high = x.astype(BF)
    return high, (x - high.astype(F32)).astype(BF)


def split3(x):
    first = x.astype(BF)
    rest = x - first.astype(F32)
    second = rest.astype(BF)
    return first, second, (rest - second.astype(F32)).astype(BF)


def dot3(left, right, dims=(((1,), (0,)), ((), ()))):
    lh, ll = left
    rh, rl = right
    dot = functools.partial(lax.dot_general, dimension_numbers=dims, preferred_element_type=F32)
    return dot(lh, rh) + dot(lh, rl) + dot(ll, rh)


def layer_norm(values, gain_row):
    average = jnp.mean(values, axis=-1, keepdims=True)
    centered = values - average
    variance = jnp.mean(centered * centered, axis=-1, keepdims=True)
    return centered * lax.rsqrt(variance + EPSILON) * gain_row


def shift_by(k, count):
    return [(i, (i + k) % count) for i in range(count)]


def gather_slabs(piece):
    cols = lax.axis_size("col")
    reps = lax.axis_size("rep")
    far = [lax.ppermute(piece, "col", shift_by(k, cols)) for k in range(1, cols)]
    return [(p, lax.ppermute(p, "rep", shift_by(1, reps))) for p in [piece] + far]


def attention_kernel(cols, heads_per_step, place, *refs):
    slabs = refs[: 2 * cols]
    gain, wq0, wq1, wo0, wo1, keep_ref = refs[2 * cols : 2 * cols + 6]
    send_refs = refs[2 * cols + 6 : 2 * cols + 6 + cols - 1]
    x_all, q_t, k_t, v_t, attended = refs[2 * cols + 6 + cols - 1 :]
    col, rep = place[0], place[1]
    rows, width = x_all.shape
    slab = width // cols
    half = q_t.shape[1]
    step = pl.program_id(0)

    @pl.when(step == 0)
    def _():
        for k in range(cols):
            near, other = slabs[2 * k][...], slabs[2 * k + 1][...]
            low = jnp.where(rep == 0, near, other)
            high = jnp.where(rep == 0, other, near)
            at = pl.multiple_of(lax.rem(col + cols - k, cols) * slab, 128)
            x_all[:, pl.ds(at, slab)] = jnp.concatenate([low, high], axis=1)
        weights = [
            split2(jnp.concatenate([wq0[0, j], wq1[0, j]], axis=1)) for j in range(3)
        ]
        chunk = 256
        for start in range(0, rows, chunk):
            normed = split2(layer_norm(x_all[start : start + chunk, :], gain[...]))
            k_t[:, start : start + chunk] = dot3(normed, weights[1]).T
            v_t[:, start : start + chunk] = dot3(normed, weights[2]).T
        for start in range(0, half, chunk):
            at = pl.multiple_of(rep * half + start, chunk)
            normed = split2(layer_norm(x_all[pl.ds(at, chunk), :], gain[...]))
            q_t[:, start : start + chunk] = dot3(normed, weights[0]).T * (LOG2E * HD**-0.5)

    chunk = min(256, half)
    base = step * heads_per_step * HD

    def head_rows(h):
        return pl.ds(pl.multiple_of(base + h * HD, HD), HD)

    keys, values = [], []
    for h in range(heads_per_step):
        k1, k2, k3 = split3(k_t[head_rows(h), :])
        keys.append(jnp.concatenate([k1, k2, k1, k3, k2, k1], axis=0))
        v1, v2 = split2(v_t[head_rows(h), :])
        ones = jnp.ones_like(v1)
        values.append((jnp.concatenate([v1, v2, ones], axis=0), jnp.concatenate([v1, ones], axis=0)))

    def scores(h, at):
        q1, q2, q3 = split3(q_t[head_rows(h), at : at + chunk])
        queries = jnp.concatenate([q1, q1, q2, q1, q2, q3], axis=0)
        return lax.dot_general(
            keys[h], queries, (((0,), (0,)), ((), ())), preferred_element_type=F32
        )

    items = [(h, at) for h in range(heads_per_step) for at in range(0, half, chunk)]
    current = scores(*items[0])
    for i, (h, at) in enumerate(items):
        following = scores(*items[i + 1]) if i + 1 < len(items) else None
        weights = jnp.exp2(current - jnp.max(current, axis=0, keepdims=True))
        high, low = split2(weights)
        first = jnp.dot(values[h][0], high, preferred_element_type=F32)
        second = jnp.dot(values[h][1], low, preferred_element_type=F32)
        total = first[:HD] + first[HD : 2 * HD] + second[:HD]
        norm = first[2 * HD : 2 * HD + 1] + second[HD : HD + 1]
        attended[head_rows(h), at : at + chunk] = total / norm
        current = following

    @pl.when(step == pl.num_programs(0) - 1)
    def _():
        w_out = split2(jnp.concatenate([wo0[0], wo1[0]], axis=0))
        part = half // cols
        for k in range(cols):
            quarter = lax.rem(col + k, cols)
            at = pl.multiple_of(quarter * part, 128)
            mine = split2(attended[:, pl.ds(at, part)].T)
            result = dot3(mine, w_out)
            if k == 0:
                keep_ref[...] = result + x_all[pl.ds(rep * half + at, part), :]
            else:
                send_refs[k - 1][...] = result


def attention(place, slabs, gain, w_qkv, w_out, layer_index):
    cols = len(slabs)
    reps = lax.axis_size("rep")
    rows = slabs[0][0].shape[0]
    width = w_out[0].shape[-1]
    chip_width = 2 * w_qkv[0].shape[-1]
    half = rows // reps
    part = half // cols
    heads = chip_width // HD
    heads_per_step = 4
    local = w_qkv[0].shape[-1]
    fixed = lambda *block: pl.BlockSpec(
        (1,) + block, lambda h: (layer_index,) + (0,) * len(block)
    )
    out_block = pl.BlockSpec((part, width), lambda h: (0, 0))
    return pl.pallas_call(
        functools.partial(attention_kernel, cols, heads_per_step),
        grid=(heads // heads_per_step,),
        in_specs=[smem()]
        + [vmem()] * (2 * cols)
        + [vmem()]
        + [fixed(3, width, local)] * 2
        + [fixed(local, width)] * 2,
        out_specs=[out_block] * cols,
        out_shape=[jax.ShapeDtypeStruct((part, width), F32)] * cols,
        scratch_shapes=[
            pltpu.VMEM((rows, width), F32),
            pltpu.VMEM((chip_width, half), F32),
            pltpu.VMEM((chip_width, rows), F32),
            pltpu.VMEM((chip_width, rows), F32),
            pltpu.VMEM((chip_width, half), F32),
        ],
        compiler_params=params(),
        cost_estimate=pl.CostEstimate(
            flops=6 * 10**9, bytes_accessed=6 * 10**6, transcendentals=heads * rows * half
        ),
        name="attention",
    )(
        place,
        *[p for pair in slabs for p in pair],
        gain[layer_index][None],
        *w_qkv,
        *w_out,
    )


def mlp_rows(values, gain_row, up, down):
    normed = split2(layer_norm(values, gain_row))
    result = None
    for w_up, w_down in zip(up, down):
        hidden = dot3(normed, w_up)
        hidden = split2(hidden * (0.5 + 0.5 * lax.erf(hidden * 0.5**0.5)))
        term = dot3(hidden, w_down)
        result = term if result is None else result + term
    return result


def mlp_kernel(cols, place, *refs):
    pieces = refs[:cols]
    gain, wu0, wu1, wd0, wd1, keep_ref = refs[cols : cols + 6]
    send_refs = refs[cols + 6 : cols + 6 + cols - 1]
    partial, residual = refs[cols + 6 + cols - 1 :]
    col = place[0]
    part, width = pieces[0].shape
    slab = width // cols
    up = [split2(w[0]) for w in (wu0, wu1)]
    down = [split2(w[0]) for w in (wd0, wd1)]
    for k in range(cols):
        at = pl.multiple_of(lax.rem(col + cols - k, cols) * part, 128)
        values = pieces[k][...]
        partial[pl.ds(at, part), :] = mlp_rows(values, gain[...], up, down)
        residual[pl.ds(at, part), :] = values
    for k in range(cols):
        at = pl.multiple_of(lax.rem(col + k, cols) * slab, 128)
        if k == 0:
            keep_ref[...] = partial[:, pl.ds(at, slab)] + residual[:, pl.ds(at, slab)]
        else:
            send_refs[k - 1][...] = partial[:, pl.ds(at, slab)]


def mlp(place, pieces, gain, w_up, w_down, layer_index):
    cols = len(pieces)
    part, width = pieces[0].shape
    local = w_up[0].shape[-1]
    rows = part * cols
    slab = width // cols
    fixed = lambda *block: pl.BlockSpec(
        (1,) + block, lambda i: (layer_index,) + (0,) * len(block)
    )
    out_block = pl.BlockSpec((rows, slab), lambda i: (0, 0))
    return pl.pallas_call(
        functools.partial(mlp_kernel, cols),
        grid=(1,),
        in_specs=[smem()]
        + [vmem()] * (cols + 1)
        + [fixed(width, local)] * 2
        + [fixed(local, width)] * 2,
        out_specs=[out_block] * cols,
        out_shape=[jax.ShapeDtypeStruct((rows, slab), F32)] * cols,
        scratch_shapes=[pltpu.VMEM((rows, width), F32)] * 2,
        compiler_params=params(),
        cost_estimate=pl.CostEstimate(
            flops=4 * rows * width * 2 * local * 3, bytes_accessed=6 * 10**6, transcendentals=0
        ),
        name="mlp",
    )(place, *pieces, gain[layer_index][None], *w_up, *w_down)


def pooled_mlp_kernel(cols, place, *refs):
    pieces = refs[:cols]
    pillar, cells, gain, wu0, wu1, wd0, wd1 = refs[cols : cols + 7]
    own_refs = refs[cols + 7 : 2 * cols + 7]
    other_refs = refs[2 * cols + 7 :]
    col, rep = place[0], place[1]
    part = pieces[0].shape[0]
    up = [split2(w[0]) for w in (wu0, wu1)]
    down = [split2(w[0]) for w in (wd0, wd1)]
    totals = [None] * (2 * cols)
    for k in range(cols):
        source = lax.rem(col + cols - k, cols)
        at = pl.multiple_of(rep * part * cols + source * part, 128)
        tokens_cells = pillar[:, pl.ds(at, part)]
        values = pieces[k][...]
        result = mlp_rows(values, gain[...], up, down)
        if k == 0:
            result = result + values
        high, low = split2(result)
        for i in range(2 * cols):
            chosen = jnp.where(cells[i] == tokens_cells, 1.0, 0.0).astype(BF)
            term = jnp.dot(chosen, high, preferred_element_type=F32) + jnp.dot(
                chosen, low, preferred_element_type=F32
            )
            totals[i] = term if totals[i] is None else totals[i] + term
    for k in range(cols):
        own_refs[k][...] = totals[2 * k]
        other_refs[k][...] = totals[2 * k + 1]


def pooled_mlp(place, pieces, pillar, cells, gain, w_up, w_down, layer_index):
    cols = len(pieces)
    part, width = pieces[0].shape
    local = w_up[0].shape[-1]
    rows = part * cols
    count = cells.shape[1]
    fixed = lambda *block: pl.BlockSpec(
        (1,) + block, lambda i: (layer_index,) + (0,) * len(block)
    )
    out_block = pl.BlockSpec((count, width), lambda i: (0, 0))
    outs = pl.pallas_call(
        functools.partial(pooled_mlp_kernel, cols),
        grid=(1,),
        in_specs=[smem()]
        + [vmem()] * (cols + 3)
        + [fixed(width, local)] * 2
        + [fixed(local, width)] * 2,
        out_specs=[out_block] * (2 * cols),
        out_shape=[jax.ShapeDtypeStruct((count, width), F32)] * (2 * cols),
        compiler_params=params(),
        cost_estimate=pl.CostEstimate(
            flops=4 * rows * width * 2 * local * 3, bytes_accessed=6 * 10**6, transcendentals=0
        ),
        name="mlp_pool",
    )(place, *pieces, pillar, cells, gain[layer_index][None], *w_up, *w_down)
    return outs[:cols], outs[cols:]


def pick_blocks_kernel(outs, counts, index, *refs):
    sources = refs[: len(counts)]
    targets = refs[len(counts) : len(counts) + outs]
    blocks = refs[-1]
    start = 0
    for ref, count in zip(sources, counts):
        blocks[start : start + count] = ref[...]
        start += count
    each = targets[0].shape[0]
    for o in range(outs):
        for j in range(each):
            targets[o][j] = blocks[index[o * each + j]]


def pick_blocks(sources, index, outs, each):
    counts = [s.shape[0] for s in sources]
    shape = sources[0].shape[1:]
    return pl.pallas_call(
        functools.partial(pick_blocks_kernel, outs, counts),
        in_specs=[smem()] + [vmem()] * len(sources),
        out_specs=[vmem()] * outs,
        out_shape=[jax.ShapeDtypeStruct((each,) + shape, F32)] * outs,
        scratch_shapes=[pltpu.VMEM((sum(counts),) + shape, F32)],
        compiler_params=params(),
        name="pick_blocks",
    )(index, *sources)


def routes(dest_device, dest_slot):
    count = dest_device.shape[0]
    peers = lax.axis_size("tok")
    capacity = max(2, (count + peers - 4) // (peers - 1))
    order = jnp.arange(count, dtype=jnp.int32)
    earlier = (dest_device[:, None] == dest_device[None, :]) & (order[None, :] < order[:, None])
    rank = jnp.sum(earlier.astype(jnp.int32), axis=1)
    shifts = jnp.arange(peers, dtype=jnp.int32)
    targets = (lax.axis_index("tok") + shifts) % peers
    places = jnp.arange(capacity, dtype=jnp.int32)
    chosen = (
        (targets[:, None, None] == dest_device[None, None, :])
        & (places[None, :, None] == rank[None, None, :])
    ).astype(jnp.int32)
    blocks = jnp.sum(chosen * order, axis=-1)
    slots = jnp.sum(chosen * (dest_slot + 1), axis=-1)
    arrived = jnp.stack(
        [slots[0]]
        + [lax.ppermute(slots[k], "tok", shift_by(k, peers)) for k in range(1, peers)]
    ).reshape(-1)
    matches = (arrived[None, :] == order[:, None] + 1).astype(jnp.int32)
    sources = jnp.sum(matches * jnp.arange(peers * capacity, dtype=jnp.int32), axis=1)
    return blocks, sources


def raster_kernel(reps, place, tile, halo, depth, point, gain, out_ref, cells, normed):
    tok, col, rep, height, full_width = (place[i] for i in (2, 0, 1, 3, 4))
    tile_rows = out_ref.shape[0]
    tile_cols = out_ref.shape[1]
    width = out_ref.shape[2]
    wide = tile_cols + 2 * BORDER
    kept = tile_rows + BORDER
    padded = cells.shape[1]
    cells[...] = jnp.zeros_like(cells)
    normed[...] = jnp.zeros_like(normed)
    first = BORDER * (1 - rep)
    for i in range(kept):
        cells[first + i, 0:wide, :] = tile[i * wide : (i + 1) * wide, :]
    other = (tile_rows + BORDER) * rep
    for i in range(BORDER):
        cells[other + i, 0:wide, :] = halo[i * wide : (i + 1) * wide, :]
    lead = 8
    row_zero = tok * (tile_rows * reps) + rep * tile_rows - BORDER
    col_zero = col * tile_cols - BORDER
    for layer in range(2):
        rim = layer + 1
        grid_rows = tile_rows + 2 * BORDER - 2 * rim
        low_col, span = (0, padded) if layer == 0 else (BORDER, tile_cols)
        values = cells[...]
        mean = jnp.mean(values * values, axis=-1, keepdims=True)
        normed[:, lead : lead + padded, :] = values * lax.rsqrt(mean + EPSILON) * gain[layer : layer + 1]
        mixed = None
        for a in range(3):
            for b in range(3):
                start = lead + low_col + b - 1
                term = (
                    normed[rim - 1 + a : rim - 1 + a + grid_rows, start : start + span, :]
                    * depth[layer, a, b][None, None, :]
                )
                mixed = term if mixed is None else mixed + term
        left = split2(mixed.reshape(grid_rows * span, width))
        value = dot3(left, split2(point[layer, :, :width]))
        gate = dot3(left, split2(point[layer, :, width:]))
        change = (value * jax.nn.sigmoid(gate)).reshape(grid_rows, span, width)
        centre = cells[rim : rim + grid_rows, low_col : low_col + span, :]
        if layer == 0:
            row = row_zero + rim + lax.broadcasted_iota(jnp.int32, (grid_rows, span, 1), 0)
            column = col_zero + lax.broadcasted_iota(jnp.int32, (grid_rows, span, 1), 1)
            inside = (row >= 0) & (row < height) & (column >= 0) & (column < full_width)
            cells[rim : rim + grid_rows, :, :] = jnp.where(inside, centre + change, 0.0)
        else:
            out_ref[...] = centre + change


def raster_layers(place, tile, halo, depth_weight, point_weight, raster_gain, tile_rows):
    reps = lax.axis_size("rep")
    width = tile.shape[-1]
    padded = -(-(TC + 2 * BORDER) // 8) * 8
    return pl.pallas_call(
        functools.partial(raster_kernel, reps),
        in_specs=[smem()] + [vmem()] * 5,
        out_specs=vmem(),
        out_shape=jax.ShapeDtypeStruct((tile_rows, TC, width), F32),
        scratch_shapes=[
            pltpu.VMEM((tile_rows + 2 * BORDER, padded, width), F32),
            pltpu.VMEM((tile_rows + 2 * BORDER, padded + 16, width), F32),
        ],
        compiler_params=params(),
        name="raster",
    )(place, tile, halo, depth_weight, point_weight, raster_gain)


def tile_cells(tile_rows):
    cols = lax.axis_size("col")
    tok, col, rep = (lax.axis_index(a) for a in ("tok", "col", "rep"))
    full_width = TC * cols
    wide = TC + 2 * BORDER
    flat = jnp.arange((tile_rows + BORDER) * wide, dtype=jnp.int32)
    row, column = flat // wide, flat % wide
    tables = []
    for k in range(cols):
        for r in (rep, 1 - rep):
            x = ((col + k) % cols) * TC - BORDER + column
            y = tok * TR + r * (tile_rows - BORDER) + row
            tables.append(jnp.where((x >= 0) & (x < full_width), y * full_width + x, -2))
    return jnp.stack(tables)[:, :, None]


def on_device(
    tokens,
    w_qkv,
    w_out,
    w_up,
    w_down,
    attn_gain,
    mlp_gain,
    dest_device,
    dest_slot,
    pillar,
    depth_weight,
    point_weight,
    raster_gain,
):
    cols, reps, toks = (lax.axis_size(a) for a in ("col", "rep", "tok"))
    tok, col, rep = (lax.axis_index(a) for a in ("tok", "col", "rep"))
    swap = shift_by(1, reps)
    place = jnp.stack([col, rep, tok, jnp.int32(TR * toks), jnp.int32(TC * cols)]).astype(jnp.int32)
    slabs = gather_slabs(tokens)
    both = lambda w: (w, lax.ppermute(w, "rep", swap))
    w_qkv, w_out, w_up, w_down = (both(w) for w in (w_qkv, w_out, w_up, w_down))
    blocks_out, blocks_in = routes(dest_device, dest_slot)
    count = dest_device.shape[0]
    each = count // reps
    tile_rows = TR // reps
    cells = tile_cells(tile_rows)

    def attend(slabs, layer_index):
        keep, *sends = attention(place, slabs, attn_gain, w_qkv, w_out, layer_index)
        for k, part in enumerate(sends):
            keep = keep + lax.ppermute(part, "col", shift_by(k + 1, cols))
        return [keep] + [lax.ppermute(keep, "col", shift_by(k, cols)) for k in range(1, cols)]

    pieces = attend(slabs, 0)
    keep, *sends = mlp(place, pieces, mlp_gain, w_up, w_down, 0)
    for k, part in enumerate(sends):
        keep = keep + lax.ppermute(part, "col", shift_by(k + 1, cols))
    feature = keep.shape[1] // reps
    low, high = keep[:, :feature], keep[:, feature:]
    near = jnp.where(rep == 0, low, high)
    far = lax.ppermute(jnp.where(rep == 0, high, low), "rep", swap)
    in_blocks = lambda x: x.reshape(each, -1, feature)
    index = jnp.where(blocks_out // each == rep, blocks_out % each, each + blocks_out % each)
    capacity = index.shape[1]
    outgoing = pick_blocks([in_blocks(near), in_blocks(far)], index.reshape(-1), toks, capacity)
    incoming = [outgoing[0]] + [
        lax.ppermute(outgoing[k], "tok", shift_by(k, toks)) for k in range(1, toks)
    ]
    (moved,) = pick_blocks(incoming, blocks_in, 1, count)
    pieces = attend(gather_slabs(moved.reshape(-1, feature)), 1)

    own, other = pooled_mlp(place, pieces, pillar[None], cells, mlp_gain, w_up, w_down, 1)
    sums = [own[k] + lax.ppermute(other[k], "rep", swap) for k in range(cols)]
    tile = sums[0]
    for k in range(1, cols):
        tile = tile + lax.ppermute(sums[k], "col", shift_by(k, cols))
    edge = BORDER * (TC + 2 * BORDER)
    edge_rows = jnp.where(rep == 0, tile[:edge], tile[-edge:])
    pairs = [(i * reps + reps - 1, (i + 1) * reps) for i in range(toks - 1)]
    halo = lax.ppermute(edge_rows, ("tok", "rep"), pairs + [(b, a) for a, b in pairs])
    return raster_layers(place, tile, halo, depth_weight, point_weight, raster_gain, tile_rows)


def solution(mesh):
    placed = (
        P(("scene", "tok"), ("col", "rep")),
        P(None, None, None, ("col", "rep")),
        P(None, ("col", "rep"), None),
        P(None, None, ("col", "rep")),
        P(None, ("col", "rep"), None),
        P(),
        P(),
        P(("scene", "tok")),
        P(("scene", "tok")),
        P(("scene", "tok")),
        P(),
        P(),
        P(),
    )
    return jax.shard_map(
        on_device,
        mesh=mesh,
        in_specs=placed,
        out_specs=P(("scene", "tok", "rep"), "col", None),
        check_vma=False,
    )
```

```python
import functools

import jax
import jax.numpy as jnp
from jax import lax
from jax.experimental import pallas as pl
from jax.experimental.pallas import tpu as pltpu
from jax.sharding import PartitionSpec as P

PATCH = 1024
TR = 16
TC = 16
HD = 16
EPSILON = 1e-05
LOG2E = 1.4426950408889634
BF = jnp.bfloat16
F32 = jnp.float32
VMEM_LIMIT = 56 * 2**20
BORDER = 2


def vmem():
    return pl.BlockSpec(memory_space=pltpu.VMEM)


def smem():
    return pl.BlockSpec(memory_space=pltpu.SMEM)


def params():
    return pltpu.CompilerParams(vmem_limit_bytes=VMEM_LIMIT)


def split2(x):
    high = x.astype(BF)
    return high, (x - high.astype(F32)).astype(BF)


def split3(x):
    first = x.astype(BF)
    rest = x - first.astype(F32)
    second = rest.astype(BF)
    return first, second, (rest - second.astype(F32)).astype(BF)


def dot3(left, right, dims=(((1,), (0,)), ((), ()))):
    lh, ll = left
    rh, rl = right
    dot = functools.partial(lax.dot_general, dimension_numbers=dims, preferred_element_type=F32)
    return dot(lh, rh) + dot(lh, rl) + dot(ll, rh)


def layer_norm(values, gain_row):
    average = jnp.mean(values, axis=-1, keepdims=True)
    centered = values - average
    variance = jnp.mean(centered * centered, axis=-1, keepdims=True)
    return centered * lax.rsqrt(variance + EPSILON) * gain_row


def shift_by(k, count):
    return [(i, (i + k) % count) for i in range(count)]


def gather_slabs(piece):
    cols = lax.axis_size("col")
    reps = lax.axis_size("rep")
    far = [lax.ppermute(piece, "col", shift_by(k, cols)) for k in range(1, cols)]
    return [(p, lax.ppermute(p, "rep", shift_by(1, reps))) for p in [piece] + far]


def qkv_kernel(cols, units, halves, place, *refs):
    slabs = refs[: 2 * cols]
    gain = refs[2 * cols]
    pieces = refs[2 * cols + 1 : 2 * cols + 1 + units]
    q_t, k_t, v_t, x_half, x_all = refs[2 * cols + 1 + units :]
    col, rep = place[0], place[1]
    rows, width = x_all.shape
    slab = width // cols
    half = q_t.shape[1]
    for k in range(cols):
        near, other = slabs[2 * k][...], slabs[2 * k + 1][...]
        low = jnp.where(rep == 0, near, other)
        high = jnp.where(rep == 0, other, near)
        at = pl.multiple_of(lax.rem(col + cols - k, cols) * slab, 128)
        x_all[:, pl.ds(at, slab)] = jnp.concatenate([low, high], axis=1)
    weights = [split2(jnp.concatenate([u[j] for u in pieces], axis=0)) for j in range(3)]
    dims = (((1,), (1,)), ((), ()))
    chunk = 256
    for start in range(0, rows, chunk):
        normed = split2(layer_norm(x_all[start : start + chunk, :], gain[...]))
        k_t[:, start : start + chunk] = dot3(weights[1], normed, dims)
        v_t[:, start : start + chunk] = dot3(weights[2], normed, dims)
    first = (rep if halves == "rep" else col) * half
    chunk = min(chunk, half)
    for start in range(0, half, chunk):
        values = x_all[pl.ds(pl.multiple_of(first + start, chunk), chunk), :]
        x_half[start : start + chunk, :] = values
        normed = split2(layer_norm(values, gain[...]))
        q_t[:, start : start + chunk] = dot3(weights[0], normed, dims) * (LOG2E * HD**-0.5)


def project(place, slabs, gain, units, halves):
    cols = len(slabs)
    rows = slabs[0][0].shape[0]
    width = units[0].shape[-1]
    features = sum(u.shape[1] for u in units)
    half = rows // lax.axis_size(halves)
    shape = lambda *dims: jax.ShapeDtypeStruct(dims, F32)
    return pl.pallas_call(
        functools.partial(qkv_kernel, cols, len(units), halves),
        in_specs=[smem()] + [vmem()] * (2 * cols + 1 + len(units)),
        out_specs=[vmem()] * 4,
        out_shape=[
            shape(features, half),
            shape(features, rows),
            shape(features, rows),
            shape(half, width),
        ],
        scratch_shapes=[pltpu.VMEM((rows, width), F32)],
        compiler_params=params(),
        cost_estimate=pl.CostEstimate(
            flops=6 * rows * width * features * 3, bytes_accessed=8 * 10**6, transcendentals=0
        ),
        name="project",
    )(place, *[p for pair in slabs for p in pair], gain, *units)


def attention_kernel(parts, units, heads_per_step, scatter, place, *refs):
    q_t, k_t, v_t, x_half = refs[:4]
    pieces = refs[4 : 4 + units]
    outs = refs[4 + units : -1]
    attended = refs[-1]
    half = q_t.shape[1]
    step = pl.program_id(0)
    chunk = min(256, half)
    base = step * heads_per_step * HD

    def head_rows(h):
        return pl.ds(pl.multiple_of(base + h * HD, HD), HD)

    keys, values = [], []
    for h in range(heads_per_step):
        k1, k2, k3 = split3(k_t[head_rows(h), :])
        keys.append(jnp.concatenate([k1, k2, k1, k3, k2, k1], axis=0))
        v1, v2 = split2(v_t[head_rows(h), :])
        ones = jnp.ones_like(v1)
        values.append((jnp.concatenate([v1, v2, ones], axis=0), jnp.concatenate([v1, ones], axis=0)))

    def scores(h, at):
        q1, q2, q3 = split3(q_t[head_rows(h), at : at + chunk])
        queries = jnp.concatenate([q1, q1, q2, q1, q2, q3], axis=0)
        return lax.dot_general(
            keys[h], queries, (((0,), (0,)), ((), ())), preferred_element_type=F32
        )

    items = [(h, at) for h in range(heads_per_step) for at in range(0, half, chunk)]
    current = scores(*items[0])
    for i, (h, at) in enumerate(items):
        following = scores(*items[i + 1]) if i + 1 < len(items) else None
        weights = jnp.exp2(current - jnp.max(current, axis=0, keepdims=True))
        high, low = split2(weights)
        first = jnp.dot(values[h][0], high, preferred_element_type=F32)
        second = jnp.dot(values[h][1], low, preferred_element_type=F32)
        total = first[:HD] + first[HD : 2 * HD] + second[:HD]
        norm = first[2 * HD : 2 * HD + 1] + second[HD : HD + 1]
        attended[head_rows(h), at : at + chunk] = total / norm
        current = following

    @pl.when(step == pl.num_programs(0) - 1)
    def _():
        w_out = split2(jnp.concatenate([u[3] for u in pieces], axis=0))
        part = half // parts
        mine = place[0] if scatter else place[1]
        for k in range(parts):
            at = pl.multiple_of(lax.rem(mine + k, parts) * part, 128)
            result = dot3(split2(attended[:, pl.ds(at, part)].T), w_out)
            if k == 0:
                result = result + x_half[pl.ds(at, part), :]
            if scatter:
                outs[k][...] = result
            else:
                outs[0][pl.ds(at, part), :] = result


def attention(place, projected, units, scatter):
    parts = lax.axis_size("col" if scatter else "rep")
    features, half = projected[0].shape
    rows = projected[1].shape[1]
    width = units[0].shape[-1]
    heads = features // HD
    heads_per_step = 4
    shapes = [(half // parts, width)] * parts if scatter else [(half, width)]
    return pl.pallas_call(
        functools.partial(attention_kernel, parts, len(units), heads_per_step, scatter),
        grid=(heads // heads_per_step,),
        in_specs=[smem()] + [vmem()] * (4 + len(units)),
        out_specs=[pl.BlockSpec(s, lambda h: (0, 0)) for s in shapes],
        out_shape=[jax.ShapeDtypeStruct(s, F32) for s in shapes],
        scratch_shapes=[pltpu.VMEM((features, half), F32)],
        compiler_params=params(),
        cost_estimate=pl.CostEstimate(
            flops=16 * 10**9, bytes_accessed=6 * 10**6, transcendentals=heads * rows * half
        ),
        name="attention",
    )(place, *projected, *units)


def mlp_rows(values, gain_row, up, down):
    normed = split2(layer_norm(values, gain_row))
    hidden = dot3(normed, up, (((1,), (1,)), ((), ())))
    hidden = split2(hidden * (0.5 + 0.5 * lax.erf(hidden * 0.5**0.5)))
    return dot3(hidden, down)


def mlp_kernel(cols, reps, units, place, *refs):
    pieces = refs[:reps]
    gain = refs[reps]
    unit_refs = refs[reps + 1 : reps + 1 + units]
    outs = refs[reps + 1 + units : -1]
    partial = refs[-1]
    col, rep = place[0], place[1]
    part, width = pieces[0].shape
    feature = width // (cols * reps)
    up, down = (split2(jnp.concatenate([u[j] for u in unit_refs], axis=0)) for j in range(2))
    for k in range(reps):
        at = pl.multiple_of(lax.rem(rep + reps - k, reps) * part, 128)
        values = pieces[k][...]
        result = mlp_rows(values, gain[...], up, down)
        partial[pl.ds(at, part), :] = result + values if k == 0 else result
    aligned = feature % 128 == 0
    for k in range(cols):
        for j in range(reps):
            place_of = lax.rem(col + k, cols) * reps + lax.rem(rep + j, reps)
            if aligned:
                at = pl.multiple_of(place_of * feature, 128)
                outs[k * reps + j][...] = partial[:, pl.ds(at, feature)]
            else:
                at = pl.multiple_of(lax.rem(col + k, cols) * reps * feature, 128)
                slab = partial[:, pl.ds(at, reps * feature)]
                low, high = slab[:, :feature], slab[:, feature:]
                outs[k * reps + j][...] = jnp.where(lax.rem(rep + j, reps) == 0, low, high)


def mlp(place, pieces, gain, units):
    cols, reps = lax.axis_size("col"), len(pieces)
    part, width = pieces[0].shape
    rows = part * reps
    feature = width // (cols * reps)
    hidden = sum(u.shape[1] for u in units)
    return pl.pallas_call(
        functools.partial(mlp_kernel, cols, reps, len(units)),
        in_specs=[smem()] + [vmem()] * (reps + 1 + len(units)),
        out_specs=[vmem()] * (cols * reps),
        out_shape=[jax.ShapeDtypeStruct((rows, feature), F32)] * (cols * reps),
        scratch_shapes=[pltpu.VMEM((rows, width), F32)],
        compiler_params=params(),
        cost_estimate=pl.CostEstimate(
            flops=4 * rows * width * hidden * 3, bytes_accessed=6 * 10**6, transcendentals=0
        ),
        name="mlp",
    )(place, *pieces, gain, *units)


def pooled_mlp_kernel(cols, units, place, *refs):
    near, other, pillar, cells, gain = refs[:5]
    unit_refs = refs[5 : 5 + units]
    outs = refs[5 + units :]
    col, rep = place[0], place[1]
    half = near.shape[0]
    part = half // 2
    up, down = (split2(jnp.concatenate([u[j] for u in unit_refs], axis=0)) for j in range(2))
    totals = [None] * (2 * cols)
    for k in range(2):
        source = lax.rem(rep + k, 2) * part
        tokens_cells = pillar[:, pl.ds(pl.multiple_of(col * half + source, 128), part)]
        here = pl.ds(pl.multiple_of(source, 128), part)
        values = near[here, :] + other[here, :]
        result = mlp_rows(values, gain[...], up, down)
        if k == 0:
            result = result + values
        high, low = split2(result)
        for i in range(2 * cols):
            chosen = jnp.where(cells[i] == tokens_cells, 1.0, 0.0).astype(BF)
            term = jnp.dot(chosen, high, preferred_element_type=F32) + jnp.dot(
                chosen, low, preferred_element_type=F32
            )
            totals[i] = term if totals[i] is None else totals[i] + term
    for i in range(2 * cols):
        outs[i][...] = totals[i]


def pooled_mlp(place, near, other, pillar, cells, gain, units):
    cols = lax.axis_size("col")
    rows, width = near.shape
    count = cells.shape[1]
    hidden = sum(u.shape[1] for u in units)
    outs = pl.pallas_call(
        functools.partial(pooled_mlp_kernel, cols, len(units)),
        in_specs=[smem()] + [vmem()] * (5 + len(units)),
        out_specs=[vmem()] * (2 * cols),
        out_shape=[jax.ShapeDtypeStruct((count, width), F32)] * (2 * cols),
        compiler_params=params(),
        cost_estimate=pl.CostEstimate(
            flops=4 * rows * width * hidden * 3, bytes_accessed=6 * 10**6, transcendentals=0
        ),
        name="mlp_pool",
    )(place, near, other, pillar, cells, gain, *units)
    return outs[::2], outs[1::2]


def pick_blocks_kernel(outs, counts, index, *refs):
    sources = refs[: len(counts)]
    targets = refs[len(counts) : len(counts) + outs]
    blocks = refs[-1]
    start = 0
    for ref, count in zip(sources, counts):
        blocks[start : start + count] = ref[...]
        start += count
    each = targets[0].shape[0]
    for o in range(outs):
        for j in range(each):
            targets[o][j] = blocks[index[o * each + j]]


def pick_blocks(sources, index, outs, each):
    counts = [s.shape[0] for s in sources]
    shape = sources[0].shape[1:]
    return pl.pallas_call(
        functools.partial(pick_blocks_kernel, outs, counts),
        in_specs=[smem()] + [vmem()] * len(sources),
        out_specs=[vmem()] * outs,
        out_shape=[jax.ShapeDtypeStruct((each,) + shape, F32)] * outs,
        scratch_shapes=[pltpu.VMEM((sum(counts),) + shape, F32)],
        compiler_params=params(),
        name="pick_blocks",
    )(index, *sources)


def routes(dest_device, dest_slot):
    count = dest_device.shape[0]
    peers = lax.axis_size("tok")
    capacity = max(2, (count + peers - 4) // (peers - 1))
    order = jnp.arange(count, dtype=jnp.int32)
    earlier = (dest_device[:, None] == dest_device[None, :]) & (order[None, :] < order[:, None])
    rank = jnp.sum(earlier.astype(jnp.int32), axis=1)
    shifts = jnp.arange(peers, dtype=jnp.int32)
    targets = (lax.axis_index("tok") + shifts) % peers
    places = jnp.arange(capacity, dtype=jnp.int32)
    chosen = (
        (targets[:, None, None] == dest_device[None, None, :])
        & (places[None, :, None] == rank[None, None, :])
    ).astype(jnp.int32)
    blocks = jnp.sum(chosen * order, axis=-1)
    slots = jnp.sum(chosen * (dest_slot + 1), axis=-1)
    arrived = jnp.stack(
        [slots[0]]
        + [lax.ppermute(slots[k], "tok", shift_by(k, peers)) for k in range(1, peers)]
    ).reshape(-1)
    matches = (arrived[None, :] == order[:, None] + 1).astype(jnp.int32)
    sources = jnp.sum(matches * jnp.arange(peers * capacity, dtype=jnp.int32), axis=1)
    return blocks, sources


def raster_kernel(reps, place, tile, halo, depth, point, gain, out_ref, cells, normed):
    tok, col, rep, height, full_width = (place[i] for i in (2, 0, 1, 3, 4))
    tile_rows = out_ref.shape[0]
    tile_cols = out_ref.shape[1]
    width = out_ref.shape[2]
    wide = tile_cols + 2 * BORDER
    kept = tile_rows + BORDER
    padded = cells.shape[1]
    cells[...] = jnp.zeros_like(cells)
    normed[...] = jnp.zeros_like(normed)
    first = BORDER * (1 - rep)
    for i in range(kept):
        cells[first + i, 0:wide, :] = tile[i * wide : (i + 1) * wide, :]
    other = (tile_rows + BORDER) * rep
    for i in range(BORDER):
        cells[other + i, 0:wide, :] = halo[i * wide : (i + 1) * wide, :]
    lead = 8
    row_zero = tok * (tile_rows * reps) + rep * tile_rows - BORDER
    col_zero = col * tile_cols - BORDER
    for layer in range(2):
        rim = layer + 1
        grid_rows = tile_rows + 2 * BORDER - 2 * rim
        low_col, span = (0, padded) if layer == 0 else (BORDER, tile_cols)
        values = cells[...]
        mean = jnp.mean(values * values, axis=-1, keepdims=True)
        normed[:, lead : lead + padded, :] = values * lax.rsqrt(mean + EPSILON) * gain[layer : layer + 1]
        mixed = None
        for a in range(3):
            for b in range(3):
                start = lead + low_col + b - 1
                term = (
                    normed[rim - 1 + a : rim - 1 + a + grid_rows, start : start + span, :]
                    * depth[layer, a, b][None, None, :]
                )
                mixed = term if mixed is None else mixed + term
        left = split2(mixed.reshape(grid_rows * span, width))
        value = dot3(left, split2(point[layer, :, :width]))
        gate = dot3(left, split2(point[layer, :, width:]))
        change = (value * jax.nn.sigmoid(gate)).reshape(grid_rows, span, width)
        centre = cells[rim : rim + grid_rows, low_col : low_col + span, :]
        if layer == 0:
            row = row_zero + rim + lax.broadcasted_iota(jnp.int32, (grid_rows, span, 1), 0)
            column = col_zero + lax.broadcasted_iota(jnp.int32, (grid_rows, span, 1), 1)
            inside = (row >= 0) & (row < height) & (column >= 0) & (column < full_width)
            cells[rim : rim + grid_rows, :, :] = jnp.where(inside, centre + change, 0.0)
        else:
            out_ref[...] = centre + change


def raster_layers(place, tile, halo, depth_weight, point_weight, raster_gain, tile_rows):
    reps = lax.axis_size("rep")
    width = tile.shape[-1]
    padded = -(-(TC + 2 * BORDER) // 8) * 8
    return pl.pallas_call(
        functools.partial(raster_kernel, reps),
        in_specs=[smem()] + [vmem()] * 5,
        out_specs=vmem(),
        out_shape=jax.ShapeDtypeStruct((tile_rows, TC, width), F32),
        scratch_shapes=[
            pltpu.VMEM((tile_rows + 2 * BORDER, padded, width), F32),
            pltpu.VMEM((tile_rows + 2 * BORDER, padded + 16, width), F32),
        ],
        compiler_params=params(),
        name="raster",
    )(place, tile, halo, depth_weight, point_weight, raster_gain)


def tile_cells(tile_rows):
    cols = lax.axis_size("col")
    tok, col, rep = (lax.axis_index(a) for a in ("tok", "col", "rep"))
    full_width = TC * cols
    wide = TC + 2 * BORDER
    flat = jnp.arange((tile_rows + BORDER) * wide, dtype=jnp.int32)
    row, column = flat // wide, flat % wide
    tables = []
    for k in range(cols):
        for r in (rep, 1 - rep):
            x = ((col + k) % cols) * TC - BORDER + column
            y = tok * TR + r * (tile_rows - BORDER) + row
            tables.append(jnp.where((x >= 0) & (x < full_width), y * full_width + x, -2))
    return jnp.stack(tables)[:, :, None]


def on_device(
    tokens,
    w_qkv,
    w_out,
    w_up,
    w_down,
    attn_gain,
    mlp_gain,
    dest_device,
    dest_slot,
    pillar,
    depth_weight,
    point_weight,
    raster_gain,
):
    cols, reps, toks = (lax.axis_size(a) for a in ("col", "rep", "tok"))
    tok, col, rep = (lax.axis_index(a) for a in ("tok", "col", "rep"))
    swap = shift_by(1, reps)
    place = jnp.stack([col, rep, tok, jnp.int32(TR * toks), jnp.int32(TC * cols)]).astype(jnp.int32)
    slabs = gather_slabs(tokens)
    heads_unit = [
        jnp.concatenate([jnp.swapaxes(w_qkv[l], 1, 2), w_out[l][None]], axis=0) for l in range(2)
    ]
    hidden_unit = [jnp.stack([w_up[l].T, w_down[l]], axis=0) for l in range(2)]

    def far_units(unit, pieces, piece, after=None):
        scenes = lax.axis_size("scene")
        size = unit.shape[1] // (scenes * pieces)
        start = (lax.axis_index("scene") * pieces + piece) * size
        if after is not None:
            start = start + jnp.minimum(jnp.abs(after[0, 0]), 0.0).astype(jnp.int32)
        own = lax.dynamic_slice_in_dim(unit, start, size, 1)
        found = []
        for k in range(1, cols):
            direct = lax.ppermute(own, "col", shift_by(k, cols))
            found += [direct] + [
                lax.ppermute(direct, "scene", shift_by(j, scenes)) for j in range(1, scenes)
            ]
        return found

    blocks_out, blocks_in = routes(dest_device, dest_slot)
    count = dest_device.shape[0]
    tile_rows = TR // reps
    cells = tile_cells(tile_rows)

    units = [heads_unit[0], lax.ppermute(heads_unit[0], "rep", swap)]
    far_hidden = far_units(hidden_unit[0], 2, 0) + far_units(hidden_unit[0], 2, 1)
    projected = project(place, slabs, attn_gain[:1], units, "rep")
    keep, *sends = attention(place, projected, units, True)
    for k, part in enumerate(sends):
        keep = keep + lax.ppermute(part, "col", shift_by(k + 1, cols))
    far_heads = far_units(heads_unit[1], 1, 0, keep)
    pieces = [keep, lax.ppermute(keep, "rep", swap)]
    outs = mlp(place, pieces, mlp_gain[:1], [hidden_unit[0]] + far_hidden)
    parts = [outs[k * reps] + lax.ppermute(outs[k * reps + 1], "rep", swap) for k in range(cols)]
    gathered = [parts[0]] + [
        lax.ppermute(parts[k], "col", shift_by(k, cols)) for k in range(1, cols)
    ]
    far_hidden = far_units(hidden_unit[1], 1, 0, gathered[-1])
    feature = parts[0].shape[1]
    each = count // (reps * cols)
    of_rep, of_col = blocks_out // (each * cols), blocks_out // each % cols
    index = ((col - of_col) % cols * reps + of_rep) * each + blocks_out % each
    capacity = index.shape[1]
    outgoing = pick_blocks(
        [g.reshape(reps * each, -1, feature) for g in gathered], index.reshape(-1), toks, capacity
    )
    incoming = [outgoing[0]] + [
        lax.ppermute(outgoing[k], "tok", shift_by(k, toks)) for k in range(1, toks)
    ]
    (moved,) = pick_blocks(incoming, blocks_in, 1, count)

    units = [heads_unit[1]] + far_heads
    projected = project(place, gather_slabs(moved.reshape(-1, feature)), attn_gain[1:], units, "col")
    (near,) = attention(place, projected, units, False)
    own, other = pooled_mlp(
        place,
        near,
        lax.ppermute(near, "rep", swap),
        pillar[None],
        cells,
        mlp_gain[1:],
        [hidden_unit[1]] + far_hidden,
    )
    sums = [own[k] + lax.ppermute(other[k], "rep", swap) for k in range(cols)]
    tile = sums[0]
    for k in range(1, cols):
        tile = tile + lax.ppermute(sums[k], "col", shift_by(k, cols))
    edge = BORDER * (TC + 2 * BORDER)
    edge_rows = jnp.where(rep == 0, tile[:edge], tile[-edge:])
    pairs = [(i * reps + reps - 1, (i + 1) * reps) for i in range(toks - 1)]
    halo = lax.ppermute(edge_rows, ("tok", "rep"), pairs + [(b, a) for a, b in pairs])
    return raster_layers(place, tile, halo, depth_weight, point_weight, raster_gain, tile_rows)


def solution(mesh):
    placed = (
        P(("scene", "tok"), ("col", "rep")),
        P(None, None, None, ("col", "rep")),
        P(None, ("col", "rep"), None),
        P(None, None, ("col", "rep")),
        P(None, ("col", "rep"), None),
        P(),
        P(),
        P(("scene", "tok")),
        P(("scene", "tok")),
        P(("scene", "tok")),
        P(),
        P(),
        P(),
    )
    return jax.shard_map(
        on_device,
        mesh=mesh,
        in_specs=placed,
        out_specs=P(("scene", "tok", "rep"), "col", None),
        check_vma=False,
    )
```

```python
import functools

import jax
import jax.numpy as jnp
from jax import lax
from jax.experimental import pallas as pl
from jax.experimental.pallas import tpu as pltpu
from jax.sharding import PartitionSpec as P

PATCH = 1024
TR = 16
TC = 16
HD = 16
EPSILON = 1e-05
LOG2E = 1.4426950408889634
BF = jnp.bfloat16
F32 = jnp.float32
VMEM_LIMIT = 32 * 2**20
BORDER = 2


def launch(body, name, scalars, arrays, outs, scratch=(), after=(), hbm=(), flops=0, exps=0):
    counts = [len(scalars), len(arrays) + len(hbm), len(after), len(outs)]
    starts = [sum(counts[:i]) for i in range(5)]

    def kernel(*refs):
        body(
            refs[: starts[1]],
            refs[starts[1] : starts[2]],
            refs[starts[3] : starts[4]],
            *refs[starts[4] :],
        )

    return pl.pallas_call(
        kernel,
        in_specs=[pl.BlockSpec(memory_space=pltpu.SMEM)] * counts[0]
        + [pl.BlockSpec(memory_space=pltpu.VMEM)] * counts[1]
        + [pl.BlockSpec(memory_space=pl.ANY)] * counts[2],
        out_specs=[pl.BlockSpec(memory_space=pltpu.VMEM)] * counts[3],
        out_shape=[pltpu.VMEM(shape, F32) for shape in outs],
        scratch_shapes=[pltpu.VMEM(shape, F32) for shape in scratch],
        compiler_params=pltpu.CompilerParams(vmem_limit_bytes=VMEM_LIMIT),
        cost_estimate=pl.CostEstimate(flops=flops, bytes_accessed=0, transcendentals=exps),
        name=name,
    )(
        *scalars,
        *[pltpu.with_memory_space_constraint(x, pltpu.VMEM) for x in arrays],
        *hbm,
        *after,
    )


def split2(x):
    high = x.astype(BF)
    return high, (x - high.astype(F32)).astype(BF)


def split3(x):
    first = x.astype(BF)
    rest = x - first.astype(F32)
    second = rest.astype(BF)
    return first, second, (rest - second.astype(F32)).astype(BF)


def dot3(left, right, dims=(((1,), (0,)), ((), ()))):
    lh, ll = left
    rh, rl = right
    dot = functools.partial(lax.dot_general, dimension_numbers=dims, preferred_element_type=F32)
    return dot(lh, rh) + dot(lh, rl) + dot(ll, rh)


def layer_norm(values, gain_row):
    average = jnp.mean(values, axis=-1, keepdims=True)
    centered = values - average
    variance = jnp.mean(centered * centered, axis=-1, keepdims=True)
    return centered * lax.rsqrt(variance + EPSILON) * gain_row


def shift_by(k, count):
    return [(i, (i + k) % count) for i in range(count)]


def gather_slabs(piece):
    cols = lax.axis_size("col")
    reps = lax.axis_size("rep")
    far = [lax.ppermute(piece, "col", shift_by(k, cols)) for k in range(1, cols)]
    return [(p, lax.ppermute(p, "rep", shift_by(1, reps))) for p in [piece] + far]


def sliced(ref, scene, parts, part):
    size = ref.shape[1] // parts
    at = (scene * (parts // 2) + part) * size
    return ref[:, pl.ds(pl.multiple_of(at, size), size), :]


def prepare(place, w_qkv, w_out, w_up, w_down):
    width = w_out.shape[-1]
    features, hidden = w_out.shape[1], w_down.shape[1]

    def body(scalars, ins, outs):
        (place,) = scalars
        qkv, out, up, down = ins
        for layer in range(2):
            heads, units = outs[2 * layer], outs[2 * layer + 1]
            for j in range(3):
                heads[j] = qkv[layer, j].T
            heads[3] = out[layer]
            units[0] = up[layer].T
            units[1] = down[layer]
        for i in range(2):
            outs[4 + i][...] = sliced(outs[1], place[5], 4, i)

    per_layer = [(4, features, width), (2, hidden, width)]
    return launch(
        body,
        "prepare",
        [place],
        [],
        per_layer * 2 + [(2, hidden // 4, width)] * 2,
        hbm=[w_qkv, w_out, w_up, w_down],
    )


def project(place, slabs, gain, units, halves, after=()):
    cols = len(slabs)
    rows = slabs[0][0].shape[0]
    width = units[0].shape[-1]
    features = sum(u.shape[1] for u in units)
    half = rows // lax.axis_size(halves)

    def body(scalars, ins, outs, x_all):
        (place,) = scalars
        pieces, gain, units = ins[: 2 * cols], ins[2 * cols], ins[2 * cols + 1 :]
        q_t, k_t, v_t, x_half = outs
        col, rep = place[0], place[1]
        slab = width // cols
        for k in range(cols):
            near, other = pieces[2 * k][...], pieces[2 * k + 1][...]
            low = jnp.where(rep == 0, near, other)
            high = jnp.where(rep == 0, other, near)
            at = pl.multiple_of(lax.rem(col + cols - k, cols) * slab, 128)
            x_all[:, pl.ds(at, slab)] = jnp.concatenate([low, high], axis=1)
        weights = [split2(jnp.concatenate([u[j] for u in units], axis=0)) for j in range(3)]
        dims = (((1,), (1,)), ((), ()))
        chunk = 256
        for start in range(0, rows, chunk):
            normed = split2(layer_norm(x_all[start : start + chunk, :], gain[...]))
            k_t[:, start : start + chunk] = dot3(weights[1], normed, dims)
            v_t[:, start : start + chunk] = dot3(weights[2], normed, dims)
        first = (rep if halves == "rep" else col) * half
        chunk = min(chunk, half)
        for start in range(0, half, chunk):
            values = x_all[pl.ds(pl.multiple_of(first + start, chunk), chunk), :]
            x_half[start : start + chunk, :] = values
            normed = split2(layer_norm(values, gain[...]))
            q_t[:, start : start + chunk] = dot3(weights[0], normed, dims) * (LOG2E * HD**-0.5)

    return launch(
        body,
        "project",
        [place],
        [p for pair in slabs for p in pair] + [gain] + units,
        [(features, half), (features, rows), (features, rows), (half, width)],
        [(rows, width)],
        after,
    )


def attention(projected, heads_per_step=4):
    q_t, k_t, v_t = projected
    features, half = q_t.shape
    rows = k_t.shape[1]
    chunk = min(256, half)

    def body(scalars, ins, outs):
        q_t, k_t, v_t = ins
        (attended,) = outs

        def group(step, carry):
            def head_rows(h):
                return pl.ds(pl.multiple_of((step * heads_per_step + h) * HD, HD), HD)

            keys, values = [], []
            for h in range(heads_per_step):
                k1, k2, k3 = split3(k_t[head_rows(h), :])
                keys.append(jnp.concatenate([k1, k2, k1, k3, k2, k1], axis=0))
                v1, v2 = split2(v_t[head_rows(h), :])
                ones = jnp.ones_like(v1)
                values.append(
                    (jnp.concatenate([v1, v2, ones], axis=0), jnp.concatenate([v1, ones], axis=0))
                )

            def scores(h, at):
                q1, q2, q3 = split3(q_t[head_rows(h), at : at + chunk])
                queries = jnp.concatenate([q1, q1, q2, q1, q2, q3], axis=0)
                return lax.dot_general(
                    keys[h], queries, (((0,), (0,)), ((), ())), preferred_element_type=F32
                )

            items = [(h, at) for h in range(heads_per_step) for at in range(0, half, chunk)]
            current = scores(*items[0])
            for i, (h, at) in enumerate(items):
                following = scores(*items[i + 1]) if i + 1 < len(items) else None
                weights = jnp.exp2(current - jnp.max(current, axis=0, keepdims=True))
                high, low = split2(weights)
                first = jnp.dot(values[h][0], high, preferred_element_type=F32)
                second = jnp.dot(values[h][1], low, preferred_element_type=F32)
                total = first[:HD] + first[HD : 2 * HD] + second[:HD]
                norm = first[2 * HD : 2 * HD + 1] + second[HD : HD + 1]
                attended[head_rows(h), at : at + chunk] = total / norm
                current = following
            return carry

        lax.fori_loop(0, features // HD // heads_per_step, group, 0)

    (attended,) = launch(
        body,
        "attention",
        [],
        projected,
        [(features, half)],
        flops=16 * 10**9,
        exps=features // HD * rows * half,
    )
    return attended


def output_rows(place, attended, x_half, units, scatter, after=()):
    parts = lax.axis_size("col" if scatter else "rep")
    half, width = x_half.shape
    part = half // parts

    def body(scalars, ins, outs):
        (place,) = scalars
        attended, x_half, *units = ins
        w_out = split2(jnp.concatenate([u[3] for u in units], axis=0))
        mine = place[0] if scatter else place[1]
        for k in range(parts):
            at = pl.multiple_of(lax.rem(mine + k, parts) * part, 128)
            result = dot3(split2(attended[:, pl.ds(at, part)].T), w_out)
            if k == 0:
                result = result + x_half[pl.ds(at, part), :]
            if scatter:
                outs[k][...] = result
            else:
                outs[0][pl.ds(at, part), :] = result

    return launch(
        body,
        "output_rows",
        [place],
        [attended, x_half] + units,
        [(part, width)] * parts if scatter else [(half, width)],
        after=after,
    )


def sum_rows(place, keep, received, unit, after=()):
    def body(scalars, ins, outs):
        (place,) = scalars
        total = ins[0][...]
        for ref in ins[1:-1]:
            total = total + ref[...]
        outs[0][...] = total
        outs[1][...] = sliced(ins[-1], place[5], 2, 0)

    kinds, count, width = unit.shape
    return launch(
        body,
        "sum_rows",
        [place],
        [keep] + received + [unit],
        [keep.shape, (kinds, count // 2, width)],
        after=after,
    )


def sum_pairs(own, received, after=()):
    def body(scalars, ins, outs):
        for k, out in enumerate(outs):
            out[...] = ins[k][...] + ins[len(own) + k][...]

    return launch(body, "sum_pairs", [], own + received, [x.shape for x in own], after=after)


def slice_unit(place, unit, part, after=()):
    def body(scalars, ins, outs):
        outs[0][...] = sliced(ins[0], scalars[0][5], 4, part)

    kinds, count, width = unit.shape
    (out,) = launch(
        body, "slice_unit", [place], [unit], [(kinds, count // 4, width)], after=after
    )
    return out


def mlp_rows(values, gain_row, up, down):
    normed = split2(layer_norm(values, gain_row))
    hidden = dot3(normed, up, (((1,), (1,)), ((), ())))
    hidden = split2(hidden * (0.5 + 0.5 * lax.erf(hidden * 0.5**0.5)))
    return dot3(hidden, down)


def mlp(place, pieces, gain, units):
    cols, reps = lax.axis_size("col"), len(pieces)
    part, width = pieces[0].shape
    rows = part * reps
    feature = width // (cols * reps)
    hidden = sum(u.shape[1] for u in units)

    def body(scalars, ins, outs, partial):
        (place,) = scalars
        pieces, gain, units = ins[:reps], ins[reps], ins[reps + 1 :]
        col, rep = place[0], place[1]
        up, down = (split2(jnp.concatenate([u[j] for u in units], axis=0)) for j in range(2))
        for k in range(reps):
            at = pl.multiple_of(lax.rem(rep + reps - k, reps) * part, 128)
            values = pieces[k][...]
            result = mlp_rows(values, gain[...], up, down)
            partial[pl.ds(at, part), :] = result + values if k == 0 else result
        for k in range(cols):
            for j in range(reps):
                to_rep = lax.rem(rep + j, reps)
                to_col = lax.rem(col + k, cols)
                out = outs[k * reps + j]
                if feature % 128 == 0:
                    at = pl.multiple_of((to_col * reps + to_rep) * feature, 128)
                    out[...] = partial[:, pl.ds(at, feature)]
                else:
                    at = pl.multiple_of(to_col * reps * feature, 128)
                    slab = partial[:, pl.ds(at, reps * feature)]
                    out[...] = jnp.where(to_rep == 0, slab[:, :feature], slab[:, feature:])

    return launch(
        body,
        "mlp",
        [place],
        pieces + [gain] + units,
        [(rows, feature)] * (cols * reps),
        [(rows, width)],
        flops=4 * rows * width * hidden * 3,
    )


def pooled_mlp(place, near, other, pillar, cells, gain, units):
    cols = lax.axis_size("col")
    half, width = near.shape
    count = cells.shape[1]
    hidden = sum(u.shape[1] for u in units)

    def body(scalars, ins, outs):
        (place,) = scalars
        near, other, pillar, cells, gain, *units = ins
        col, rep = place[0], place[1]
        part = half // 2
        up, down = (split2(jnp.concatenate([u[j] for u in units], axis=0)) for j in range(2))
        totals = [None] * (2 * cols)
        for k in range(2):
            source = lax.rem(rep + k, 2) * part
            tokens_cells = pillar[:, pl.ds(pl.multiple_of(col * half + source, 128), part)]
            here = pl.ds(pl.multiple_of(source, 128), part)
            values = near[here, :] + other[here, :]
            result = mlp_rows(values, gain[...], up, down)
            if k == 0:
                result = result + values
            high, low = split2(result)
            for i in range(2 * cols):
                chosen = jnp.where(cells[i] == tokens_cells, 1.0, 0.0).astype(BF)
                term = jnp.dot(chosen, high, preferred_element_type=F32) + jnp.dot(
                    chosen, low, preferred_element_type=F32
                )
                totals[i] = term if totals[i] is None else totals[i] + term
        for i in range(2 * cols):
            outs[i][...] = totals[i]

    outs = launch(
        body,
        "mlp_pool",
        [place],
        [near, other, pillar, cells, gain] + units,
        [(count, width)] * (2 * cols),
        flops=4 * half * width * hidden * 3,
    )
    return outs[::2], outs[1::2]


def pick_blocks(place, sources, index, outs, each, unit=None, after=()):
    counts = [s.shape[0] for s in sources]
    shape = sources[0].shape[1:]

    def body(scalars, ins, targets, blocks):
        place, index = scalars
        start = 0
        for ref, count in zip(ins, counts):
            blocks[start : start + count] = ref[...]
            start += count
        for o in range(outs):
            for j in range(each):
                targets[o][j] = blocks[index[o * each + j]]
        if unit is not None:
            targets[-1][...] = sliced(ins[-1], place[5], 4, 0)

    more = [] if unit is None else [unit]
    return launch(
        body,
        "pick_blocks",
        [place, index],
        list(sources) + more,
        [(each,) + shape] * outs + [(2, u.shape[1] // 4, u.shape[2]) for u in more],
        [(sum(counts),) + shape],
        after,
    )


def routes(dest_device, dest_slot):
    count = dest_device.shape[0]
    peers = lax.axis_size("tok")
    capacity = max(2, (count + peers - 4) // (peers - 1))
    order = jnp.arange(count, dtype=jnp.int32)
    earlier = (dest_device[:, None] == dest_device[None, :]) & (order[None, :] < order[:, None])
    rank = jnp.sum(earlier.astype(jnp.int32), axis=1)
    shifts = jnp.arange(peers, dtype=jnp.int32)
    targets = (lax.axis_index("tok") + shifts) % peers
    places = jnp.arange(capacity, dtype=jnp.int32)
    chosen = (
        (targets[:, None, None] == dest_device[None, None, :])
        & (places[None, :, None] == rank[None, None, :])
    ).astype(jnp.int32)
    blocks = jnp.sum(chosen * order, axis=-1)
    slots = jnp.sum(chosen * (dest_slot + 1), axis=-1)
    arrived = jnp.stack(
        [slots[0]]
        + [lax.ppermute(slots[k], "tok", shift_by(k, peers)) for k in range(1, peers)]
    ).reshape(-1)
    matches = (arrived[None, :] == order[:, None] + 1).astype(jnp.int32)
    sources = jnp.sum(matches * jnp.arange(peers * capacity, dtype=jnp.int32), axis=1)
    return blocks, sources


def raster_kernel(reps, scalars, ins, outs, cells, normed):
    (place,) = scalars
    tile, halo, depth, gain, point = ins
    (out_ref,) = outs
    tok, col, rep, height, full_width = (place[i] for i in (2, 0, 1, 3, 4))
    tile_rows = out_ref.shape[0]
    tile_cols = out_ref.shape[1]
    width = out_ref.shape[2]
    wide = tile_cols + 2 * BORDER
    kept = tile_rows + BORDER
    padded = cells.shape[1]
    cells[...] = jnp.zeros_like(cells)
    normed[...] = jnp.zeros_like(normed)
    first = BORDER * (1 - rep)
    for i in range(kept):
        cells[first + i, 0:wide, :] = tile[i * wide : (i + 1) * wide, :]
    other = (tile_rows + BORDER) * rep
    for i in range(BORDER):
        cells[other + i, 0:wide, :] = halo[i * wide : (i + 1) * wide, :]
    lead = 8
    row_zero = tok * (tile_rows * reps) + rep * tile_rows - BORDER
    col_zero = col * tile_cols - BORDER
    for layer in range(2):
        rim = layer + 1
        grid_rows = tile_rows + 2 * BORDER - 2 * rim
        low_col, span = (0, padded) if layer == 0 else (BORDER, tile_cols)
        values = cells[...]
        mean = jnp.mean(values * values, axis=-1, keepdims=True)
        normed[:, lead : lead + padded, :] = values * lax.rsqrt(mean + EPSILON) * gain[layer : layer + 1]
        mixed = None
        for a in range(3):
            for b in range(3):
                start = lead + low_col + b - 1
                term = (
                    normed[rim - 1 + a : rim - 1 + a + grid_rows, start : start + span, :]
                    * depth[layer, a, b][None, None, :]
                )
                mixed = term if mixed is None else mixed + term
        left = split2(mixed.reshape(grid_rows * span, width))
        value = dot3(left, split2(point[layer, :, :width]))
        gate = dot3(left, split2(point[layer, :, width:]))
        change = (value * jax.nn.sigmoid(gate)).reshape(grid_rows, span, width)
        centre = cells[rim : rim + grid_rows, low_col : low_col + span, :]
        if layer == 0:
            row = row_zero + rim + lax.broadcasted_iota(jnp.int32, (grid_rows, span, 1), 0)
            column = col_zero + lax.broadcasted_iota(jnp.int32, (grid_rows, span, 1), 1)
            inside = (row >= 0) & (row < height) & (column >= 0) & (column < full_width)
            cells[rim : rim + grid_rows, :, :] = jnp.where(inside, centre + change, 0.0)
        else:
            out_ref[...] = centre + change


def raster_layers(place, tile, halo, depth_weight, point_weight, raster_gain, tile_rows):
    reps = lax.axis_size("rep")
    width = tile.shape[-1]
    padded = -(-(TC + 2 * BORDER) // 8) * 8
    kernel = functools.partial(raster_kernel, reps)
    arrays = [place, tile, halo, depth_weight, raster_gain, point_weight]
    return pl.pallas_call(
        lambda *refs: kernel(refs[:1], refs[1:6], refs[6:7], *refs[7:]),
        in_specs=[pl.BlockSpec(memory_space=pltpu.SMEM)]
        + [pl.BlockSpec(memory_space=pltpu.VMEM)] * 5,
        out_specs=pl.BlockSpec(memory_space=pltpu.VMEM),
        out_shape=jax.ShapeDtypeStruct((tile_rows, TC, width), F32),
        scratch_shapes=[
            pltpu.VMEM((tile_rows + 2 * BORDER, padded, width), F32),
            pltpu.VMEM((tile_rows + 2 * BORDER, padded + 16, width), F32),
        ],
        compiler_params=pltpu.CompilerParams(vmem_limit_bytes=VMEM_LIMIT),
        name="raster",
    )(*arrays[:1], *[pltpu.with_memory_space_constraint(x, pltpu.VMEM) for x in arrays[1:]])


def tile_cells(tile_rows):
    cols = lax.axis_size("col")
    tok, col, rep = (lax.axis_index(a) for a in ("tok", "col", "rep"))
    full_width = TC * cols
    wide = TC + 2 * BORDER
    flat = jnp.arange((tile_rows + BORDER) * wide, dtype=jnp.int32)
    row, column = flat // wide, flat % wide
    tables = []
    for k in range(cols):
        for r in (rep, 1 - rep):
            x = ((col + k) % cols) * TC - BORDER + column
            y = tok * TR + r * (tile_rows - BORDER) + row
            tables.append(jnp.where((x >= 0) & (x < full_width), y * full_width + x, -2))
    return jnp.stack(tables)[:, :, None]


def on_device(
    tokens,
    w_qkv,
    w_out,
    w_up,
    w_down,
    attn_gain,
    mlp_gain,
    dest_device,
    dest_slot,
    pillar,
    depth_weight,
    point_weight,
    raster_gain,
):
    cols, reps, toks = (lax.axis_size(a) for a in ("col", "rep", "tok"))
    tok, col, rep = (lax.axis_index(a) for a in ("tok", "col", "rep"))
    swap = shift_by(1, reps)
    scene_swap = shift_by(1, lax.axis_size("scene"))
    numbers = [col, rep, tok, TR * toks, TC * cols, lax.axis_index("scene")]
    place = jnp.stack([jnp.int32(n) for n in numbers])
    to_cols = lambda x: [lax.ppermute(x, "col", shift_by(k, cols)) for k in range(1, cols)]
    to_scene = lambda xs: [lax.ppermute(x, "scene", scene_swap) for x in xs]

    slabs = gather_slabs(tokens)
    heads0, hidden0, heads1, hidden1, *own_hidden0 = prepare(place, w_qkv, w_out, w_up, w_down)
    blocks_out, blocks_in = routes(dest_device, dest_slot)
    count = dest_device.shape[0]
    each = count // (reps * cols)
    of_rep, of_col = blocks_out // (each * cols), blocks_out // each % cols
    picks = ((col - of_col) % cols * reps + of_rep) * each + blocks_out % each
    capacity = picks.shape[1]
    picks = picks.reshape(-1)
    tile_rows = TR // reps
    cells = tile_cells(tile_rows)

    units = [heads0, lax.ppermute(heads0, "rep", swap)]
    direct = [to_cols(x) for x in own_hidden0]
    *projected, x_half = project(
        place, slabs, attn_gain[:1], units, "rep", (picks, blocks_in, cells)
    )
    passed = [to_scene(x) for x in direct]
    attended = attention(projected)
    keep, *sends = output_rows(place, attended, x_half, units, True, passed[0])
    received = [
        lax.ppermute(part, "col", shift_by(k + 1, cols)) for k, part in enumerate(sends)
    ]
    keep, own_heads1 = sum_rows(place, keep, received, heads1)
    far_heads1 = to_cols(own_heads1)
    outs = mlp(
        place,
        [keep, lax.ppermute(keep, "rep", swap)],
        mlp_gain[:1],
        [hidden0] + [u for x in direct + passed for u in x],
    )
    others = [lax.ppermute(x, "rep", swap) for x in outs[1::2]]
    parts = sum_pairs(list(outs[::2]), others, far_heads1)
    gathered = [parts[0]] + [
        lax.ppermute(parts[k], "col", shift_by(k, cols)) for k in range(1, cols)
    ]
    feature = parts[0].shape[1]
    *outgoing, own_hidden1 = pick_blocks(
        place,
        [g.reshape(reps * each, -1, feature) for g in gathered],
        picks,
        toks,
        capacity,
        hidden1,
    )
    incoming = [outgoing[0]] + [
        lax.ppermute(outgoing[k], "tok", shift_by(k, toks)) for k in range(1, toks)
    ]
    direct = to_cols(own_hidden1)
    (moved,) = pick_blocks(place, incoming, blocks_in, 1, count, None, direct)
    moved = moved.reshape(-1, feature)
    slabs = gather_slabs(moved)
    more = to_cols(slice_unit(place, hidden1, 1, (slabs[0][1],)))

    units = [heads1] + far_heads1 + to_scene(far_heads1)
    *projected, x_half = project(place, slabs, attn_gain[1:], units, "col")
    attended = attention(projected)
    more_passed = to_scene(more)
    (near,) = output_rows(place, attended, x_half, units, False, more_passed)
    own, other = pooled_mlp(
        place,
        near,
        lax.ppermute(near, "rep", swap),
        pillar[None],
        cells,
        mlp_gain[1:],
        [hidden1] + direct + to_scene(direct) + more + more_passed,
    )
    sums = [own[k] + lax.ppermute(other[k], "rep", swap) for k in range(cols)]
    tile = sums[0]
    for k in range(1, cols):
        tile = tile + lax.ppermute(sums[k], "col", shift_by(k, cols))
    edge = BORDER * (TC + 2 * BORDER)
    edge_rows = jnp.where(rep == 0, tile[:edge], tile[-edge:])
    pairs = [(i * reps + reps - 1, (i + 1) * reps) for i in range(toks - 1)]
    halo = lax.ppermute(edge_rows, ("tok", "rep"), pairs + [(b, a) for a, b in pairs])
    return raster_layers(place, tile, halo, depth_weight, point_weight, raster_gain, tile_rows)


def solution(mesh):
    placed = (
        P(("scene", "tok"), ("col", "rep")),
        P(None, None, None, ("col", "rep")),
        P(None, ("col", "rep"), None),
        P(None, None, ("col", "rep")),
        P(None, ("col", "rep"), None),
        P(),
        P(),
        P(("scene", "tok")),
        P(("scene", "tok")),
        P(("scene", "tok")),
        P(),
        P(),
        P(),
    )
    return jax.shard_map(
        on_device,
        mesh=mesh,
        in_specs=placed,
        out_specs=P(("scene", "tok", "rep"), "col", None),
        check_vma=False,
    )
```

```python
import functools

import jax
import jax.numpy as jnp
from jax import lax
from jax.experimental import pallas as pl
from jax.experimental.pallas import tpu as pltpu
from jax.sharding import PartitionSpec as P

PATCH = 1024
TR = 16
TC = 16
HD = 16
EPSILON = 1e-05
LOG2E = 1.4426950408889634
BF = jnp.bfloat16
F32 = jnp.float32
VMEM_LIMIT = 32 * 2**20
BORDER = 2


def launch(body, name, scalars, arrays, outs, scratch=(), after=(), hbm=(), flops=0, exps=0, kind=F32):
    counts = [len(scalars), len(arrays) + len(hbm), len(after), len(outs)]
    starts = [sum(counts[:i]) for i in range(5)]

    def kernel(*refs):
        body(
            refs[: starts[1]],
            refs[starts[1] : starts[2]],
            refs[starts[3] : starts[4]],
            *refs[starts[4] :],
        )

    return pl.pallas_call(
        kernel,
        in_specs=[pl.BlockSpec(memory_space=pltpu.SMEM)] * counts[0]
        + [pl.BlockSpec(memory_space=pltpu.VMEM)] * counts[1]
        + [pl.BlockSpec(memory_space=pl.ANY)] * counts[2],
        out_specs=[pl.BlockSpec(memory_space=pltpu.VMEM)] * counts[3],
        out_shape=[pltpu.VMEM(shape, kind) for shape in outs],
        scratch_shapes=[pltpu.VMEM(shape, F32) for shape in scratch],
        compiler_params=pltpu.CompilerParams(vmem_limit_bytes=VMEM_LIMIT),
        cost_estimate=pl.CostEstimate(flops=flops, bytes_accessed=0, transcendentals=exps),
        name=name,
    )(
        *scalars,
        *[pltpu.with_memory_space_constraint(x, pltpu.VMEM) for x in arrays],
        *hbm,
        *after,
    )


def split2(x):
    high = x.astype(BF)
    return high, (x - high.astype(F32)).astype(BF)


def split3(x):
    first = x.astype(BF)
    rest = x - first.astype(F32)
    second = rest.astype(BF)
    return first, second, (rest - second.astype(F32)).astype(BF)


def dot3(left, right, dims=(((1,), (0,)), ((), ()))):
    lh, ll = left
    rh, rl = right
    dot = functools.partial(lax.dot_general, dimension_numbers=dims, preferred_element_type=F32)
    return dot(lh, rh) + dot(lh, rl) + dot(ll, rh)


def layer_norm(values, gain_row):
    average = jnp.mean(values, axis=-1, keepdims=True)
    centered = values - average
    variance = jnp.mean(centered * centered, axis=-1, keepdims=True)
    return centered * lax.rsqrt(variance + EPSILON) * gain_row


def shift_by(k, count):
    return [(i, (i + k) % count) for i in range(count)]


def gather_slabs(piece):
    cols = lax.axis_size("col")
    reps = lax.axis_size("rep")
    far = [lax.ppermute(piece, "col", shift_by(k, cols)) for k in range(1, cols)]
    return [(p, lax.ppermute(p, "rep", shift_by(1, reps))) for p in [piece] + far]


def sliced(ref, part, parts):
    size = ref.shape[1] // parts
    return ref[:, pl.ds(pl.multiple_of(part * size, size), size), :]


def prepare(place, w_qkv, w_out, w_up, w_down, depth_weight):
    width = w_out.shape[-1]
    features, hidden = w_out.shape[1], w_down.shape[1]

    def body(scalars, ins, outs):
        (place,) = scalars
        qkv, out, up, down, depth = ins
        for layer in range(2):
            for a in range(3):
                for b in range(3):
                    i = layer * 9 + a * 3 + b
                    outs[6][i : i + 1, :] = depth[layer, a, b : b + 1, :]
        for layer in range(2):
            heads, units = outs[2 * layer], outs[2 * layer + 1]
            for j in range(3):
                heads[j] = qkv[layer, j].T
            heads[3] = out[layer]
            units[0] = up[layer].T
            units[1] = down[layer]
        for i in range(2):
            outs[4 + i][...] = sliced(outs[1], place[5] * 2 + i, 4)

    per_layer = [(4, features, width), (2, hidden, width)]
    return launch(
        body,
        "prepare",
        [place],
        [],
        per_layer * 2 + [(2, hidden // 4, width)] * 2 + [(18, width)],
        hbm=[w_qkv, w_out, w_up, w_down, depth_weight],
    )


def project(place, slabs, gain, layer, units, halves, after=()):
    cols = len(slabs)
    rows = slabs[0][0].shape[0]
    width = units[0].shape[-1]
    features = sum(u.shape[1] for u in units)
    half = rows // lax.axis_size(halves)
    parts = cols if halves == "rep" else lax.axis_size("rep")
    part = half // parts

    def body(scalars, ins, outs, x_all):
        (place,) = scalars
        pieces, units = ins[: 2 * cols], ins[2 * cols + 1 :]
        gain = ins[2 * cols][layer : layer + 1, :]
        q_parts, (k_t, v_t, x_keep) = outs[:parts], outs[parts:]
        col, rep = place[0], place[1]
        slab = width // cols
        for k in range(cols):
            near, other = pieces[2 * k][...], pieces[2 * k + 1][...]
            low = jnp.where(rep == 0, near, other)
            high = jnp.where(rep == 0, other, near)
            at = pl.multiple_of(lax.rem(col + cols - k, cols) * slab, 128)
            x_all[:, pl.ds(at, slab)] = jnp.concatenate([low, high], axis=1)
        weights = [split2(jnp.concatenate([u[j] for u in units], axis=0)) for j in range(3)]
        dims = (((1,), (1,)), ((), ()))
        chunk = 256
        for start in range(0, rows, chunk):
            normed = split2(layer_norm(x_all[start : start + chunk, :], gain))
            k_t[:, start : start + chunk] = dot3(weights[1], normed, dims)
            v_t[:, start : start + chunk] = dot3(weights[2], normed, dims)
        outer, inner = (rep, col) if halves == "rep" else (col, rep)
        for k in range(parts):
            at = outer * half + lax.rem(inner + k, parts) * part
            values = x_all[pl.ds(pl.multiple_of(at, part), part), :]
            if k == 0:
                x_keep[...] = values
            normed = split2(layer_norm(values, gain))
            q_parts[k][...] = dot3(weights[0], normed, dims) * (LOG2E * HD**-0.5)

    *q_parts, k_t, v_t, x_keep = launch(
        body,
        "project",
        [place],
        [p for pair in slabs for p in pair] + [gain] + units,
        [(features, part)] * parts + [(features, rows)] * 2 + [(part, width)],
        [(rows, width)],
        after,
        flops=6 * rows * width * features * 3,
    )
    return q_parts, k_t, v_t, x_keep


def attention(q_t, k_t, v_t, heads_per_step=16):
    features, count = q_t.shape
    rows = k_t.shape[1]
    chunk = min(256, count)
    heads_per_step = min(heads_per_step, features // HD)

    def body(scalars, ins, outs):
        q_t, k_t, v_t = ins
        (attended,) = outs

        def group(step, carry):
            def head_rows(h):
                return pl.ds(pl.multiple_of((step * heads_per_step + h) * HD, HD), HD)

            def scores(h, at):
                k1, k2, k3 = split3(k_t[head_rows(h), :])
                q1, q2, q3 = split3(q_t[head_rows(h), at : at + chunk])
                return lax.dot_general(
                    jnp.concatenate([k1, k2, k1, k3, k2, k1], axis=0),
                    jnp.concatenate([q1, q1, q2, q1, q2, q3], axis=0),
                    (((0,), (0,)), ((), ())),
                    preferred_element_type=F32,
                )

            items = [(h, at) for h in range(heads_per_step) for at in range(0, count, chunk)]
            current = scores(*items[0])
            for i, (h, at) in enumerate(items):
                following = scores(*items[i + 1]) if i + 1 < len(items) else None
                v1, v2 = split2(v_t[head_rows(h), :])
                ones = jnp.ones_like(v1)
                weights = jnp.exp2(current - jnp.max(current, axis=0, keepdims=True))
                high, low = split2(weights)
                first = jnp.dot(
                    jnp.concatenate([v1, v2, ones], axis=0), high, preferred_element_type=F32
                )
                second = jnp.dot(
                    jnp.concatenate([v1, ones], axis=0), low, preferred_element_type=F32
                )
                total = first[:HD] + first[HD : 2 * HD] + second[:HD]
                norm = first[2 * HD : 2 * HD + 1] + second[HD : HD + 1]
                attended[head_rows(h), at : at + chunk] = total / norm
                current = following
            return carry

        steps = features // HD // heads_per_step
        if steps == 1:
            group(0, 0)
        else:
            lax.fori_loop(0, steps, group, 0)

    (attended,) = launch(
        body,
        "attention",
        [],
        [q_t, k_t, v_t],
        [(features, count)],
        flops=8 * 10**9,
        exps=features // HD * rows * count,
    )
    return attended


def output_rows(attended, units, residual=None, after=()):
    width = units[0].shape[-1]
    count = attended.shape[1]
    more = [] if residual is None else [residual]

    def body(scalars, ins, outs):
        attended, units = ins[0], ins[1 : 1 + len(units_in)]
        w_out = split2(jnp.concatenate([u[3] for u in units], axis=0))
        result = dot3(split2(attended[...].T), w_out)
        if more:
            result = result + ins[-1][...]
        outs[0][...] = result

    units_in = units
    (out,) = launch(
        body, "output_rows", [], [attended] + units + more, [(count, width)], after=after
    )
    return out


def sum_rows(place, keep, received, unit, after=()):
    def body(scalars, ins, outs):
        (place,) = scalars
        total = ins[0][...]
        for ref in ins[1:-1]:
            total = total + ref[...]
        outs[0][...] = total
        outs[1][...] = sliced(ins[-1], place[6], 4)

    kinds, count, width = unit.shape
    return launch(
        body,
        "sum_rows",
        [place],
        [keep] + received + [unit],
        [keep.shape, (kinds, count // 4, width)],
        after=after,
    )


def sum_pairs(own, received, after=()):
    def body(scalars, ins, outs):
        for k, out in enumerate(outs):
            out[...] = ins[k][...] + ins[len(own) + k][...]

    return launch(body, "sum_pairs", [], own + received, [x.shape for x in own], after=after)


def join_units(first, second):
    def body(scalars, ins, outs):
        count = first.shape[1]
        outs[0][:, :count, :] = ins[0][...]
        outs[0][:, count:, :] = ins[1][...]

    kinds, count, width = first.shape
    (out,) = launch(body, "join_units", [], [first, second], [(kinds, 2 * count, width)])
    return out


def relay(arrays, after):
    def body(scalars, ins, outs):
        for x, out in zip(ins, outs):
            out[...] = x[...]

    return launch(body, "relay", [], arrays, [x.shape for x in arrays], after=after)


def split_weights(weights, after):
    def body(scalars, ins, outs):
        for out, part in zip(outs, split2(ins[0][...])):
            out[...] = part

    return launch(
        body, "split_weights", [], [], [weights.shape] * 2, after=after, hbm=[weights], kind=BF
    )


def mlp_rows(values, gain_row, up, down):
    normed = split2(layer_norm(values, gain_row))
    hidden = dot3(normed, up, (((1,), (1,)), ((), ())))
    hidden = split2(hidden * (0.5 + 0.5 * lax.erf(hidden * 0.5**0.5)))
    return dot3(hidden, down)


def mlp(place, pieces, gain, layer, units):
    cols, reps = lax.axis_size("col"), len(pieces)
    part, width = pieces[0].shape
    rows = part * reps
    feature = width // (cols * reps)
    hidden = sum(u.shape[1] for u in units)

    def body(scalars, ins, outs, partial):
        (place,) = scalars
        pieces, units = ins[:reps], ins[reps + 1 :]
        gain = ins[reps][layer : layer + 1, :]
        col, rep = place[0], place[1]
        up, down = (split2(jnp.concatenate([u[j] for u in units], axis=0)) for j in range(2))
        for k in range(reps):
            at = pl.multiple_of(lax.rem(rep + reps - k, reps) * part, 128)
            values = pieces[k][...]
            result = mlp_rows(values, gain, up, down)
            partial[pl.ds(at, part), :] = result + values if k == 0 else result
        for k in range(cols):
            for j in range(reps):
                to_rep = lax.rem(rep + j, reps)
                to_col = lax.rem(col + k, cols)
                out = outs[k * reps + j]
                if feature % 128 == 0:
                    at = pl.multiple_of((to_col * reps + to_rep) * feature, 128)
                    out[...] = partial[:, pl.ds(at, feature)]
                else:
                    at = pl.multiple_of(to_col * reps * feature, 128)
                    slab = partial[:, pl.ds(at, reps * feature)]
                    out[...] = jnp.where(to_rep == 0, slab[:, :feature], slab[:, feature:])

    return launch(
        body,
        "mlp",
        [place],
        pieces + [gain] + units,
        [(rows, feature)] * (cols * reps),
        [(rows, width)],
        flops=4 * rows * width * hidden * 3,
    )


def pooled_mlp(place, pieces, pillar, gain, layer, units):
    cols = lax.axis_size("col")
    part, width = pieces[0][0].shape
    half = 2 * part
    wide = TC + 2 * BORDER
    tile_rows = TR // lax.axis_size("rep")
    count = (tile_rows + BORDER) * wide
    hidden = sum(u.shape[1] for u in units)

    def body(scalars, ins, outs):
        (place,) = scalars
        pieces, (pillar, gains), units = ins[:4], ins[4:6], ins[6:]
        gain = gains[layer : layer + 1, :]
        col, rep, tok, full_width = (place[i] for i in (0, 1, 2, 4))
        flat = lax.broadcasted_iota(jnp.int32, (count, 1), 0)
        row = (flat * (-(-(2**16) // wide))) >> 16
        column = flat - row * wide - BORDER
        cells = []
        for k in range(cols):
            for j in range(2):
                x = lax.rem(col + k, cols) * TC + column
                y = tok * TR + lax.rem(rep + j, 2) * (tile_rows - BORDER) + row
                cells.append(jnp.where((x >= 0) & (x < full_width), y * full_width + x, -2))
        up, down = (split2(jnp.concatenate([u[j] for u in units], axis=0)) for j in range(2))
        totals = [None] * (2 * cols)
        for k in range(2):
            source = lax.rem(rep + k, 2) * part
            tokens_cells = pillar[:, pl.ds(pl.multiple_of(col * half + source, 128), part)]
            values = pieces[2 * k][...] + pieces[2 * k + 1][...]
            result = mlp_rows(values, gain, up, down)
            if k == 0:
                result = result + values
            high, low = split2(result)
            for i in range(2 * cols):
                chosen = jnp.where(cells[i] == tokens_cells, 1.0, 0.0).astype(BF)
                term = jnp.dot(chosen, high, preferred_element_type=F32) + jnp.dot(
                    chosen, low, preferred_element_type=F32
                )
                totals[i] = term if totals[i] is None else totals[i] + term
        for i in range(2 * cols):
            outs[i][...] = totals[i]

    outs = launch(
        body,
        "mlp_pool",
        [place],
        [x for pair in pieces for x in pair] + [pillar, gain] + units,
        [(count, width)] * (2 * cols),
        flops=4 * half * width * hidden * 3,
    )
    return outs[::2], outs[1::2]


def block_capacity(count, peers):
    return max(2, (count + peers - 4) // (peers - 1))


def pack_blocks(place, gathered, dest_device, dest_slot, unit, after=()):
    cols, reps, toks = (lax.axis_size(a) for a in ("col", "rep", "tok"))
    count = dest_device.shape[0]
    each = count // (reps * cols)
    rows, feature = gathered[0].shape
    size = rows // (reps * each)
    capacity = block_capacity(count, toks)
    codes = capacity * size
    length = codes + -(-capacity // 8) * 8

    def body(scalars, ins, outs, blocks, packed):
        place, device, slot = scalars
        col, tok = place[0], place[2]
        for k in range(cols):
            blocks[k * rows : (k + 1) * rows, :] = ins[k][...]
        for k in range(toks):
            packed[k * length + codes : (k + 1) * length, :] = jnp.zeros(
                (length - codes, feature), F32
            )
        targets = [device[b] for b in range(count)]
        for b in range(count):
            rank = jnp.int32(0)
            for earlier in targets[:b]:
                rank = rank + (earlier == targets[b]).astype(jnp.int32)
            shift = lax.rem(targets[b] - tok + toks, toks)
            of_rep, of_col = b // (each * cols), b // each % cols
            position = (lax.rem(col - of_col + cols, cols) * reps + of_rep) * each + b % each
            start = shift * length
            packed[pl.ds(pl.multiple_of(start + rank * size, 8), size), :] = blocks[
                pl.ds(pl.multiple_of(position * size, 8), size), :
            ]
            code = jnp.full((1, feature), (slot[b] + 1).astype(F32))
            packed[pl.ds(start + codes + rank, 1), :] = code
        for k in range(toks):
            outs[k][...] = packed[k * length : (k + 1) * length, :]
        outs[toks][...] = sliced(ins[cols], place[6], 4)

    return launch(
        body,
        "pack_blocks",
        [place, dest_device, dest_slot],
        list(gathered) + [unit],
        [(length, feature)] * toks + [(unit.shape[0], unit.shape[1] // 4, unit.shape[2])],
        [(cols * rows, feature), (toks * length, feature)],
        after,
    )


def place_blocks(incoming, count, size, after=()):
    feature = incoming[0].shape[1]
    capacity = block_capacity(count, len(incoming))

    def body(scalars, ins, outs):
        codes = [
            [jnp.max(x[capacity * size + j : capacity * size + j + 1, :]) for j in range(capacity)]
            for x in ins
        ]
        for x, slots in zip(ins, codes):
            for j, code in enumerate(slots):
                slot = code.astype(jnp.int32) - 1

                @pl.when(slot >= 0)
                def _(x=x, j=j, slot=slot):
                    at = pl.multiple_of(slot * size, 8)
                    outs[0][pl.ds(at, size), :] = x[j * size : (j + 1) * size, :]

    (placed,) = launch(
        body, "place_blocks", [], list(incoming), [(count * size, feature)], after=after
    )
    return placed


def sum_tiles(place, own, received):
    count = len(own)
    edge = BORDER * (TC + 2 * BORDER)
    width = own[0].shape[1]

    def body(scalars, ins, outs):
        rep = scalars[0][1]
        for k in range(count):
            total = ins[k][...] + ins[count + k][...]
            outs[k][...] = total
            outs[count + k][...] = jnp.where(rep == 0, total[:edge], total[-edge:])

    outs = launch(
        body,
        "sum_tiles",
        [place],
        list(own) + received,
        [x.shape for x in own] + [(edge, width)] * count,
    )
    return list(outs[:count]), list(outs[count:])


def raster_kernel(reps, cols, scalars, ins, outs, cells, normed):
    (place,) = scalars
    tiles, halos = ins[:cols], ins[cols : 2 * cols]
    depth, gain, point_high, point_low = ins[2 * cols :]
    (out_ref,) = outs
    tok, col, rep, height, full_width = (place[i] for i in (2, 0, 1, 3, 4))
    tile_rows = out_ref.shape[0]
    tile_cols = out_ref.shape[1]
    width = out_ref.shape[2]
    wide = tile_cols + 2 * BORDER
    kept = tile_rows + BORDER
    padded = cells.shape[1]
    cells[...] = jnp.zeros_like(cells)
    normed[...] = jnp.zeros_like(normed)
    first = BORDER * (1 - rep)
    for i in range(kept):
        parts = [x[i * wide : (i + 1) * wide, :] for x in tiles]
        cells[first + i, 0:wide, :] = functools.reduce(jnp.add, parts)
    other = (tile_rows + BORDER) * rep
    for i in range(BORDER):
        parts = [x[i * wide : (i + 1) * wide, :] for x in halos]
        cells[other + i, 0:wide, :] = functools.reduce(jnp.add, parts)
    lead = 8
    row_zero = tok * (tile_rows * reps) + rep * tile_rows - BORDER
    col_zero = col * tile_cols - BORDER
    for layer in range(2):
        rim = layer + 1
        grid_rows = tile_rows + 2 * BORDER - 2 * rim
        low_col, span = (0, padded) if layer == 0 else (BORDER, tile_cols)
        values = cells[...]
        mean = jnp.mean(values * values, axis=-1, keepdims=True)
        normed[:, lead : lead + padded, :] = values * lax.rsqrt(mean + EPSILON) * gain[layer : layer + 1]
        mixed = None
        for a in range(3):
            for b in range(3):
                start = lead + low_col + b - 1
                term = (
                    normed[rim - 1 + a : rim - 1 + a + grid_rows, start : start + span, :]
                    * depth[layer * 9 + a * 3 + b : layer * 9 + a * 3 + b + 1, :][None]
                )
                mixed = term if mixed is None else mixed + term
        left = split2(mixed.reshape(grid_rows * span, width))
        value = dot3(left, (point_high[layer, :, :width], point_low[layer, :, :width]))
        gate = dot3(left, (point_high[layer, :, width:], point_low[layer, :, width:]))
        change = (value * jax.nn.sigmoid(gate)).reshape(grid_rows, span, width)
        centre = cells[rim : rim + grid_rows, low_col : low_col + span, :]
        if layer == 0:
            row = row_zero + rim + lax.broadcasted_iota(jnp.int32, (grid_rows, span, 1), 0)
            column = col_zero + lax.broadcasted_iota(jnp.int32, (grid_rows, span, 1), 1)
            inside = (row >= 0) & (row < height) & (column >= 0) & (column < full_width)
            cells[rim : rim + grid_rows, :, :] = jnp.where(inside, centre + change, 0.0)
        else:
            out_ref[...] = centre + change


def raster_layers(place, tiles, halos, depth, point, gain, tile_rows):
    reps = lax.axis_size("rep")
    width = depth.shape[-1]
    padded = -(-(TC + 2 * BORDER) // 8) * 8
    kernel = functools.partial(raster_kernel, reps, len(tiles))
    arrays = [*tiles, *halos, depth, gain, *point]
    count = 1 + len(arrays)
    return pl.pallas_call(
        lambda *refs: kernel(refs[:1], refs[1:count], refs[count : count + 1], *refs[count + 1 :]),
        in_specs=[pl.BlockSpec(memory_space=pltpu.SMEM)]
        + [pl.BlockSpec(memory_space=pltpu.VMEM)] * len(arrays),
        out_specs=pl.BlockSpec(memory_space=pltpu.VMEM),
        out_shape=jax.ShapeDtypeStruct((tile_rows, TC, width), F32),
        scratch_shapes=[
            pltpu.VMEM((tile_rows + 2 * BORDER, padded, width), F32),
            pltpu.VMEM((tile_rows + 2 * BORDER, padded + 16, width), F32),
        ],
        compiler_params=pltpu.CompilerParams(vmem_limit_bytes=VMEM_LIMIT),
        name="raster",
    )(place, *[pltpu.with_memory_space_constraint(x, pltpu.VMEM) for x in arrays])


def on_device(
    tokens,
    w_qkv,
    w_out,
    w_up,
    w_down,
    attn_gain,
    mlp_gain,
    dest_device,
    dest_slot,
    pillar,
    depth_weight,
    point_weight,
    raster_gain,
):
    cols, reps, toks = (lax.axis_size(a) for a in ("col", "rep", "tok"))
    tok, col, rep = (lax.axis_index(a) for a in ("tok", "col", "rep"))
    swap = shift_by(1, reps)
    scene_swap = shift_by(1, lax.axis_size("scene"))
    scene = lax.axis_index("scene")
    numbers = [col, rep, tok, TR * toks, TC * cols, scene, scene * 2 + tok % 2]
    place = jnp.stack([jnp.int32(n) for n in numbers])
    to_cols = lambda x: [lax.ppermute(x, "col", shift_by(k, cols)) for k in range(1, cols)]
    to_next = lambda xs: [lax.ppermute(x, "tok", [(i, i ^ 1) for i in range(toks)]) for x in xs]
    to_scene = lambda xs: [lax.ppermute(x, "scene", scene_swap) for x in xs]

    slabs = gather_slabs(tokens)
    heads0, hidden0, heads1, hidden1, *own_hidden0, depth = prepare(
        place, w_qkv, w_out, w_up, w_down, depth_weight
    )
    units = [heads0, lax.ppermute(heads0, "rep", swap)]
    q_parts, k_t, v_t, x_keep = project(place, slabs, attn_gain, 0, units, "rep")
    later = relay(own_hidden0[1:], [k_t])
    direct0 = [to_cols(x) for x in (own_hidden0[0], *later)]
    received = []
    for k in range(1, cols):
        part = output_rows(attention(q_parts[k], k_t, v_t), units)
        received.append(lax.ppermute(part, "col", shift_by(k, cols)))
    first_passed = to_scene(relay(direct0[0], [part]))
    keep = output_rows(attention(q_parts[0], k_t, v_t), units, x_keep)
    second_passed = to_scene(relay(direct0[1], [keep]))
    point = split_weights(point_weight, [keep])
    keep, own_heads1 = sum_rows(place, keep, received, heads1, [*point, *first_passed])
    far_heads1 = to_cols(own_heads1)
    next_heads1 = to_next(far_heads1)
    outs = mlp(
        place,
        [keep, lax.ppermute(keep, "rep", swap)],
        mlp_gain,
        0,
        [hidden0] + direct0[0] + first_passed + direct0[1] + second_passed,
    )
    others = [lax.ppermute(x, "rep", swap) for x in outs[1::2]]
    parts = sum_pairs(list(outs[::2]), others, far_heads1)
    gathered = [parts[0]] + [
        lax.ppermute(parts[k], "col", shift_by(k, cols)) for k in range(1, cols)
    ]
    *outgoing, own_hidden1 = pack_blocks(
        place, gathered, dest_device, dest_slot, hidden1, next_heads1
    )
    incoming = [outgoing[0]] + [
        lax.ppermute(outgoing[k], "tok", shift_by(k, toks)) for k in range(1, toks)
    ]
    direct1 = to_cols(own_hidden1)
    far_heads1 = [join_units(*pair) for pair in zip(far_heads1, next_heads1)]
    passed_heads1 = to_scene(far_heads1)
    count = dest_device.shape[0]
    moved = place_blocks(incoming, count, tokens.shape[0] // count, direct1 + passed_heads1)
    slabs = gather_slabs(moved)
    direct1 = relay(direct1, [moved])
    next1 = to_next(direct1)
    passed1 = to_scene(direct1)
    next_passed1 = to_scene(next1)

    units = [heads1] + far_heads1 + passed_heads1
    q_parts, k_t, v_t, x_keep = project(place, slabs, attn_gain, 1, units, "col", passed1)
    other_part = output_rows(attention(q_parts[1], k_t, v_t), units, after=next_passed1)
    own_part = output_rows(attention(q_parts[0], k_t, v_t), units, x_keep)
    from_rep = lambda x: lax.ppermute(x, "rep", swap)
    own, other = pooled_mlp(
        place,
        [(own_part, from_rep(other_part)), (other_part, from_rep(own_part))],
        pillar[None],
        mlp_gain,
        1,
        [hidden1, *direct1, *passed1, *next1, *next_passed1],
    )
    sums, edges = sum_tiles(place, own, [from_rep(x) for x in other])
    tiles = [sums[0]] + [lax.ppermute(sums[k], "col", shift_by(k, cols)) for k in range(1, cols)]
    at = lambda t, c, r: (t * cols + c % cols) * reps + r
    halos = [
        lax.ppermute(
            edges[k],
            ("tok", "col", "rep"),
            [(at(t, c, reps - 1), at(t + 1, c + k, 0)) for t in range(toks - 1) for c in range(cols)]
            + [(at(t + 1, c, 0), at(t, c + k, reps - 1)) for t in range(toks - 1) for c in range(cols)],
        )
        for k in range(cols)
    ]
    return raster_layers(place, tiles, halos, depth, point, raster_gain, TR // reps)


def solution(mesh):
    placed = (
        P(("scene", "tok"), ("col", "rep")),
        P(None, None, None, ("col", "rep")),
        P(None, ("col", "rep"), None),
        P(None, None, ("col", "rep")),
        P(None, ("col", "rep"), None),
        P(),
        P(),
        P(("scene", "tok")),
        P(("scene", "tok")),
        P(("scene", "tok")),
        P(),
        P(),
        P(),
    )
    return jax.shard_map(
        on_device,
        mesh=mesh,
        in_specs=placed,
        out_specs=P(("scene", "tok", "rep"), "col", None),
        check_vma=False,
    )
```

```python
import functools

import jax
import jax.numpy as jnp
from jax import lax
from jax.experimental import pallas as pl
from jax.experimental.pallas import tpu as pltpu
from jax.sharding import PartitionSpec as P

PATCH = 1024
TR = 16
TC = 16
HD = 16
EPSILON = 1e-05
LOG2E = 1.4426950408889634
BF = jnp.bfloat16
F32 = jnp.float32
VMEM_LIMIT = 32 * 2**20
BORDER = 2


def launch(body, name, scalars, arrays, outs, scratch=(), after=(), hbm=(), flops=0, exps=0, kind=F32):
    counts = [len(scalars), len(arrays) + len(hbm), len(after), len(outs)]
    starts = [sum(counts[:i]) for i in range(5)]

    def kernel(*refs):
        body(
            refs[: starts[1]],
            refs[starts[1] : starts[2]],
            refs[starts[3] : starts[4]],
            *refs[starts[4] :],
        )

    return pl.pallas_call(
        kernel,
        in_specs=[pl.BlockSpec(memory_space=pltpu.SMEM)] * counts[0]
        + [pl.BlockSpec(memory_space=pltpu.VMEM)] * counts[1]
        + [pl.BlockSpec(memory_space=pl.ANY)] * counts[2],
        out_specs=[pl.BlockSpec(memory_space=pltpu.VMEM)] * counts[3],
        out_shape=[pltpu.VMEM(shape, kind) for shape in outs],
        scratch_shapes=[pltpu.VMEM(shape, F32) for shape in scratch],
        compiler_params=pltpu.CompilerParams(vmem_limit_bytes=VMEM_LIMIT),
        cost_estimate=pl.CostEstimate(flops=flops, bytes_accessed=0, transcendentals=exps),
        name=name,
    )(
        *scalars,
        *[pltpu.with_memory_space_constraint(x, pltpu.VMEM) for x in arrays],
        *hbm,
        *after,
    )


def split2(x):
    high = x.astype(BF)
    return high, (x - high.astype(F32)).astype(BF)


def split3(x):
    first = x.astype(BF)
    rest = x - first.astype(F32)
    second = rest.astype(BF)
    return first, second, (rest - second.astype(F32)).astype(BF)


def dot3(left, right, dims=(((1,), (0,)), ((), ()))):
    lh, ll = left
    rh, rl = right
    dot = functools.partial(lax.dot_general, dimension_numbers=dims, preferred_element_type=F32)
    return dot(lh, rh) + dot(lh, rl) + dot(ll, rh)


def layer_norm(values, gain_row):
    average = jnp.mean(values, axis=-1, keepdims=True)
    centered = values - average
    variance = jnp.mean(centered * centered, axis=-1, keepdims=True)
    return centered * lax.rsqrt(variance + EPSILON) * gain_row


def shift_by(k, count):
    return [(i, (i + k) % count) for i in range(count)]


def gather_slabs(piece):
    cols = lax.axis_size("col")
    reps = lax.axis_size("rep")
    far = [lax.ppermute(piece, "col", shift_by(k, cols)) for k in range(1, cols)]
    return [(p, lax.ppermute(p, "rep", shift_by(1, reps))) for p in [piece] + far]


def sliced(ref, part, parts):
    size = ref.shape[1] // parts
    return ref[:, pl.ds(pl.multiple_of(part * size, size), size), :]


def prepare(place, w_qkv, w_out, w_up, w_down, depth_weight):
    width = w_out.shape[-1]
    features, hidden = w_out.shape[1], w_down.shape[1]

    def body(scalars, ins, outs):
        (place,) = scalars
        qkv, out, up, down, depth = ins
        for layer in range(2):
            for a in range(3):
                for b in range(3):
                    i = layer * 9 + a * 3 + b
                    outs[5][i : i + 1, :] = depth[layer, a, b : b + 1, :]
        for layer in range(2):
            heads, units = outs[2 * layer], outs[2 * layer + 1]
            for j in range(3):
                heads[j] = qkv[layer, j].T
            heads[3] = out[layer]
            units[0] = up[layer].T
            units[1] = down[layer]
        outs[4][...] = sliced(outs[1], place[6], 4)

    per_layer = [(4, features, width), (2, hidden, width)]
    return launch(
        body,
        "prepare",
        [place],
        [],
        per_layer * 2 + [(2, hidden // 4, width), (18, width)],
        hbm=[w_qkv, w_out, w_up, w_down, depth_weight],
        flops=8 * 10**9,
    )


def project(place, slabs, gain, layer, units, halves, after=()):
    cols = len(slabs)
    rows = slabs[0][0].shape[0]
    width = units[0].shape[-1]
    features = sum(u.shape[1] for u in units)
    half = rows // lax.axis_size(halves)
    parts = cols if halves == "rep" else lax.axis_size("rep")
    part = half // parts

    def body(scalars, ins, outs, x_all):
        (place,) = scalars
        pieces, units = ins[: 2 * cols], ins[2 * cols + 1 :]
        gain = ins[2 * cols][layer : layer + 1, :]
        q_parts, (k_t, v_t, x_keep) = outs[:parts], outs[parts:]
        col, rep = place[0], place[1]
        slab = width // cols
        for k in range(cols):
            near, other = pieces[2 * k][...], pieces[2 * k + 1][...]
            low = jnp.where(rep == 0, near, other)
            high = jnp.where(rep == 0, other, near)
            at = pl.multiple_of(lax.rem(col + cols - k, cols) * slab, 128)
            x_all[:, pl.ds(at, slab)] = jnp.concatenate([low, high], axis=1)
        weights = [split2(jnp.concatenate([u[j] for u in units], axis=0)) for j in range(3)]
        dims = (((1,), (1,)), ((), ()))
        chunk = 256
        for start in range(0, rows, chunk):
            normed = split2(layer_norm(x_all[start : start + chunk, :], gain))
            k_t[:, start : start + chunk] = dot3(weights[1], normed, dims)
            v_t[:, start : start + chunk] = dot3(weights[2], normed, dims)
        outer, inner = (rep, col) if halves == "rep" else (col, rep)
        for k in range(parts):
            at = outer * half + lax.rem(inner + k, parts) * part
            values = x_all[pl.ds(pl.multiple_of(at, part), part), :]
            if k == 0:
                x_keep[...] = values
            normed = split2(layer_norm(values, gain))
            q_parts[k][...] = dot3(weights[0], normed, dims) * (LOG2E * HD**-0.5)

    *q_parts, k_t, v_t, x_keep = launch(
        body,
        "project",
        [place],
        [p for pair in slabs for p in pair] + [gain] + units,
        [(features, part)] * parts + [(features, rows)] * 2 + [(part, width)],
        [(rows, width)],
        after,
    )
    return q_parts, k_t, v_t, x_keep


def attention(q_t, k_t, v_t, after=(), heads_per_step=16):
    features, count = q_t.shape
    rows = k_t.shape[1]
    chunk = min(256, count)
    heads_per_step = min(heads_per_step, features // HD)

    def body(scalars, ins, outs):
        q_t, k_t, v_t = ins
        (attended,) = outs

        def group(step, carry):
            def head_rows(h):
                return pl.ds(pl.multiple_of((step * heads_per_step + h) * HD, HD), HD)

            def scores(h, at):
                k1, k2, k3 = split3(k_t[head_rows(h), :])
                q1, q2, q3 = split3(q_t[head_rows(h), at : at + chunk])
                return lax.dot_general(
                    jnp.concatenate([k1, k2, k1, k3, k2, k1], axis=0),
                    jnp.concatenate([q1, q1, q2, q1, q2, q3], axis=0),
                    (((0,), (0,)), ((), ())),
                    preferred_element_type=F32,
                )

            items = [(h, at) for h in range(heads_per_step) for at in range(0, count, chunk)]
            current = scores(*items[0])
            for i, (h, at) in enumerate(items):
                following = scores(*items[i + 1]) if i + 1 < len(items) else None
                v1, v2 = split2(v_t[head_rows(h), :])
                ones = jnp.ones_like(v1)
                weights = jnp.exp2(current - jnp.max(current, axis=0, keepdims=True))
                high, low = split2(weights)
                first = jnp.dot(
                    jnp.concatenate([v1, v2, ones], axis=0), high, preferred_element_type=F32
                )
                second = jnp.dot(
                    jnp.concatenate([v1, ones], axis=0), low, preferred_element_type=F32
                )
                total = first[:HD] + first[HD : 2 * HD] + second[:HD]
                norm = first[2 * HD : 2 * HD + 1] + second[HD : HD + 1]
                attended[head_rows(h), at : at + chunk] = total / norm
                current = following
            return carry

        steps = features // HD // heads_per_step
        if steps == 1:
            group(0, 0)
        else:
            lax.fori_loop(0, steps, group, 0)

    (attended,) = launch(
        body,
        "attention",
        [],
        [q_t, k_t, v_t],
        [(features, count)],
        after=after,
        flops=10**9,
        exps=features // HD * rows * count,
    )
    return attended


def output_rows(attended, units, residual=None, after=()):
    width = units[0].shape[-1]
    count = attended.shape[1]
    more = [] if residual is None else [residual]

    def body(scalars, ins, outs):
        attended, units = ins[0], ins[1 : 1 + len(units_in)]
        w_out = split2(jnp.concatenate([u[3] for u in units], axis=0))
        result = dot3(split2(attended[...].T), w_out)
        if more:
            result = result + ins[-1][...]
        outs[0][...] = result

    units_in = units
    (out,) = launch(
        body, "output_rows", [], [attended] + units + more, [(count, width)], after=after
    )
    return out


def sum_rows(keep, received, after=()):
    def body(scalars, ins, outs):
        outs[0][...] = functools.reduce(jnp.add, [x[...] for x in ins])

    (out,) = launch(body, "sum_rows", [], [keep] + received, [keep.shape], after=after)
    return out


def cut_units(firsts, seconds, after=()):
    kinds, count, width = firsts[0].shape
    size = count // 2
    total = len(firsts)

    def body(scalars, ins, outs):
        for x, out in zip(ins[:total], outs[:total]):
            out[...] = x[:, :size, :]
        for x, out in zip(ins[total:], outs[total:]):
            out[...] = x[:, size:, :]

    arrays = [*firsts, *seconds]
    halves = launch(
        body, "cut_units", [], arrays, [(kinds, size, width)] * len(arrays), after=after
    )
    return halves[:total], halves[total:]


def sum_pairs(own, received, after=()):
    def body(scalars, ins, outs):
        for k, out in enumerate(outs):
            out[...] = ins[k][...] + ins[len(own) + k][...]

    return launch(body, "sum_pairs", [], own + received, [x.shape for x in own], after=after)


def join_units(first, second, after=()):
    def body(scalars, ins, outs):
        count = first.shape[1]
        outs[0][:, :count, :] = ins[0][...]
        outs[0][:, count:, :] = ins[1][...]

    kinds, count, width = first.shape
    (out,) = launch(
        body, "join_units", [], [first, second], [(kinds, 2 * count, width)], after=after
    )
    return out


def quarter_rows(place, units, after=()):
    width = units[0].shape[-1]
    sizes = [u.shape[1] // 4 for u in units]

    def body(scalars, ins, outs):
        at = 0
        for ref, size in zip(ins, sizes):
            start = pl.multiple_of(scalars[0][6] * size, size)
            for j in range(ref.shape[0]):
                outs[0][at : at + size, :] = ref[j, pl.ds(start, size), :]
                at += size

    total = sum(u.shape[0] * size for u, size in zip(units, sizes))
    (out,) = launch(body, "quarter_rows", [place], units, [(total, width)], after=after)
    return out


def units_of_rows(rows, units, after=()):
    shapes = [(u.shape[0], u.shape[1] // 4, u.shape[2]) for u in units]

    def body(scalars, ins, outs):
        at = 0
        for out in outs:
            size = out.shape[1]
            for j in range(out.shape[0]):
                out[j] = ins[0][at : at + size, :]
                at += size

    return launch(body, "units_of_rows", [], [rows], shapes, after=after)


def relay(arrays, after):
    def body(scalars, ins, outs):
        for x, out in zip(ins, outs):
            out[...] = x[...]

    return launch(body, "relay", [], arrays, [x.shape for x in arrays], after=after)


def split_weights(weights, after):
    def body(scalars, ins, outs):
        for out, part in zip(outs, split2(ins[0][...])):
            out[...] = part

    return launch(
        body, "split_weights", [], [], [weights.shape] * 2, after=after, hbm=[weights], kind=BF
    )


def mlp_rows(values, gain_row, up, down):
    normed = split2(layer_norm(values, gain_row))
    hidden = dot3(normed, up, (((1,), (1,)), ((), ())))
    hidden = split2(hidden * (0.5 + 0.5 * lax.erf(hidden * 0.5**0.5)))
    return dot3(hidden, down)


def mlp(place, pieces, gain, layer, units, base=()):
    cols, reps = lax.axis_size("col"), len(pieces)
    part, width = pieces[0].shape
    rows = part * reps
    feature = width // (cols * reps)
    hidden = sum(u.shape[1] for u in units)
    first = reps + 1 + len(base)

    def body(scalars, ins, outs, partial):
        (place,) = scalars
        pieces, base, units = ins[:reps], ins[reps + 1 : first], ins[first:]
        gain = ins[reps][layer : layer + 1, :]
        col, rep = place[0], place[1]
        up, down = (split2(jnp.concatenate([u[j] for u in units], axis=0)) for j in range(2))
        for k in range(reps):
            at = pl.multiple_of(lax.rem(rep + reps - k, reps) * part, 128)
            values = pieces[k][...]
            result = mlp_rows(values, gain, up, down)
            partial[pl.ds(at, part), :] = result + values if k == 0 and not base else result
        for k in range(cols):
            for j in range(reps):
                to_rep = lax.rem(rep + j, reps)
                to_col = lax.rem(col + k, cols)
                out = outs[k * reps + j]
                if feature % 128 == 0:
                    at = pl.multiple_of((to_col * reps + to_rep) * feature, 128)
                    values = partial[:, pl.ds(at, feature)]
                else:
                    at = pl.multiple_of(to_col * reps * feature, 128)
                    slab = partial[:, pl.ds(at, reps * feature)]
                    values = jnp.where(to_rep == 0, slab[:, :feature], slab[:, feature:])
                out[...] = values + base[k * reps + j][...] if base else values

    return launch(
        body,
        "mlp",
        [place],
        pieces + [gain] + list(base) + units,
        [(rows, feature)] * (cols * reps),
        [(rows, width)],
        flops=4 * rows * width * hidden * 3,
    )


def pooled_mlp(place, pieces, pillar, gain, layer, units):
    cols = lax.axis_size("col")
    part, width = pieces[0][0].shape
    half = 2 * part
    wide = TC + 2 * BORDER
    tile_rows = TR // lax.axis_size("rep")
    count = (tile_rows + BORDER) * wide
    hidden = sum(u.shape[1] for u in units)

    def body(scalars, ins, outs):
        (place,) = scalars
        pieces, (pillar, gains), units = ins[:4], ins[4:6], ins[6:]
        gain = gains[layer : layer + 1, :]
        col, rep, tok, full_width = (place[i] for i in (0, 1, 2, 4))
        flat = lax.broadcasted_iota(jnp.int32, (count, 1), 0)
        row = (flat * (-(-(2**16) // wide))) >> 16
        column = flat - row * wide - BORDER
        cells = []
        for k in range(cols):
            for j in range(2):
                x = lax.rem(col + k, cols) * TC + column
                y = tok * TR + lax.rem(rep + j, 2) * (tile_rows - BORDER) + row
                cells.append(jnp.where((x >= 0) & (x < full_width), y * full_width + x, -2))
        up, down = (split2(jnp.concatenate([u[j] for u in units], axis=0)) for j in range(2))
        totals = [None] * (2 * cols)
        for k in range(2):
            source = lax.rem(rep + k, 2) * part
            tokens_cells = pillar[:, pl.ds(pl.multiple_of(col * half + source, 128), part)]
            values = pieces[2 * k][...] + pieces[2 * k + 1][...]
            result = mlp_rows(values, gain, up, down)
            if k == 0:
                result = result + values
            high, low = split2(result)
            for i in range(2 * cols):
                chosen = jnp.where(cells[i] == tokens_cells, 1.0, 0.0).astype(BF)
                term = jnp.dot(chosen, high, preferred_element_type=F32) + jnp.dot(
                    chosen, low, preferred_element_type=F32
                )
                totals[i] = term if totals[i] is None else totals[i] + term
        for i in range(2 * cols):
            outs[i][...] = totals[i]

    outs = launch(
        body,
        "mlp_pool",
        [place],
        [x for pair in pieces for x in pair] + [pillar, gain] + units,
        [(count, width)] * (2 * cols),
        flops=4 * half * width * hidden * 3,
    )
    return outs[::2], outs[1::2]


def block_capacity(count, peers):
    return max(2, (count + peers - 4) // (peers - 1))


def pack_blocks(place, gathered, dest_device, dest_slot, after=()):
    cols, reps, toks = (lax.axis_size(a) for a in ("col", "rep", "tok"))
    count = dest_device.shape[0]
    each = count // (reps * cols)
    rows, feature = gathered[0].shape
    size = rows // (reps * each)
    capacity = block_capacity(count, toks)
    codes = capacity * size
    length = codes + -(-capacity // 8) * 8

    def body(scalars, ins, outs, blocks, packed):
        place, device, slot = scalars
        col, tok = place[0], place[2]
        for k in range(cols):
            blocks[k * rows : (k + 1) * rows, :] = ins[k][...]
        for k in range(toks):
            packed[k * length + codes : (k + 1) * length, :] = jnp.zeros(
                (length - codes, feature), F32
            )
        targets = [device[b] for b in range(count)]
        for b in range(count):
            rank = jnp.int32(0)
            for earlier in targets[:b]:
                rank = rank + (earlier == targets[b]).astype(jnp.int32)
            shift = lax.rem(targets[b] - tok + toks, toks)
            of_rep, of_col = b // (each * cols), b // each % cols
            position = (lax.rem(col - of_col + cols, cols) * reps + of_rep) * each + b % each
            start = shift * length
            packed[pl.ds(pl.multiple_of(start + rank * size, 8), size), :] = blocks[
                pl.ds(pl.multiple_of(position * size, 8), size), :
            ]
            code = jnp.full((1, feature), (slot[b] + 1).astype(F32))
            packed[pl.ds(start + codes + rank, 1), :] = code
        for k in range(toks):
            outs[k][...] = packed[k * length : (k + 1) * length, :]

    return launch(
        body,
        "pack_blocks",
        [place, dest_device, dest_slot],
        list(gathered),
        [(length, feature)] * toks,
        [(cols * rows, feature), (toks * length, feature)],
        after,
    )


def place_blocks(incoming, count, size, after=()):
    feature = incoming[0].shape[1]
    capacity = block_capacity(count, len(incoming))

    def body(scalars, ins, outs):
        codes = [
            [jnp.max(x[capacity * size + j : capacity * size + j + 1, :]) for j in range(capacity)]
            for x in ins
        ]
        for x, slots in zip(ins, codes):
            for j, code in enumerate(slots):
                slot = code.astype(jnp.int32) - 1

                @pl.when(slot >= 0)
                def _(x=x, j=j, slot=slot):
                    at = pl.multiple_of(slot * size, 8)
                    outs[0][pl.ds(at, size), :] = x[j * size : (j + 1) * size, :]

    (placed,) = launch(
        body, "place_blocks", [], list(incoming), [(count * size, feature)], after=after
    )
    return placed


def sum_tiles(place, own, received):
    count = len(own)
    edge = BORDER * (TC + 2 * BORDER)
    width = own[0].shape[1]

    def body(scalars, ins, outs):
        rep = scalars[0][1]
        for k in range(count):
            total = ins[k][...] + ins[count + k][...]
            outs[k][...] = total
            outs[count + k][...] = jnp.where(rep == 0, total[:edge], total[-edge:])

    outs = launch(
        body,
        "sum_tiles",
        [place],
        list(own) + received,
        [x.shape for x in own] + [(edge, width)] * count,
    )
    return list(outs[:count]), list(outs[count:])


def raster_kernel(reps, cols, scalars, ins, outs, cells, normed):
    (place,) = scalars
    tiles, halos = ins[:cols], ins[cols : 2 * cols]
    depth, gain, point_high, point_low = ins[2 * cols :]
    (out_ref,) = outs
    tok, col, rep, height, full_width = (place[i] for i in (2, 0, 1, 3, 4))
    tile_rows = out_ref.shape[0]
    tile_cols = out_ref.shape[1]
    width = out_ref.shape[2]
    wide = tile_cols + 2 * BORDER
    kept = tile_rows + BORDER
    padded = cells.shape[1]
    cells[...] = jnp.zeros_like(cells)
    normed[...] = jnp.zeros_like(normed)
    first = BORDER * (1 - rep)
    for i in range(kept):
        parts = [x[i * wide : (i + 1) * wide, :] for x in tiles]
        cells[first + i, 0:wide, :] = functools.reduce(jnp.add, parts)
    other = (tile_rows + BORDER) * rep
    for i in range(BORDER):
        parts = [x[i * wide : (i + 1) * wide, :] for x in halos]
        cells[other + i, 0:wide, :] = functools.reduce(jnp.add, parts)
    lead = 8
    row_zero = tok * (tile_rows * reps) + rep * tile_rows - BORDER
    col_zero = col * tile_cols - BORDER
    for layer in range(2):
        rim = layer + 1
        grid_rows = tile_rows + 2 * BORDER - 2 * rim
        low_col, span = (0, padded) if layer == 0 else (BORDER, tile_cols)
        values = cells[...]
        mean = jnp.mean(values * values, axis=-1, keepdims=True)
        normed[:, lead : lead + padded, :] = values * lax.rsqrt(mean + EPSILON) * gain[layer : layer + 1]
        mixed = None
        for a in range(3):
            for b in range(3):
                start = lead + low_col + b - 1
                term = (
                    normed[rim - 1 + a : rim - 1 + a + grid_rows, start : start + span, :]
                    * depth[layer * 9 + a * 3 + b : layer * 9 + a * 3 + b + 1, :][None]
                )
                mixed = term if mixed is None else mixed + term
        left = split2(mixed.reshape(grid_rows * span, width))
        value = dot3(left, (point_high[layer, :, :width], point_low[layer, :, :width]))
        gate = dot3(left, (point_high[layer, :, width:], point_low[layer, :, width:]))
        change = (value * jax.nn.sigmoid(gate)).reshape(grid_rows, span, width)
        centre = cells[rim : rim + grid_rows, low_col : low_col + span, :]
        if layer == 0:
            row = row_zero + rim + lax.broadcasted_iota(jnp.int32, (grid_rows, span, 1), 0)
            column = col_zero + lax.broadcasted_iota(jnp.int32, (grid_rows, span, 1), 1)
            inside = (row >= 0) & (row < height) & (column >= 0) & (column < full_width)
            cells[rim : rim + grid_rows, :, :] = jnp.where(inside, centre + change, 0.0)
        else:
            out_ref[...] = centre + change


def raster_layers(place, tiles, halos, depth, point, gain, tile_rows):
    reps = lax.axis_size("rep")
    width = depth.shape[-1]
    padded = -(-(TC + 2 * BORDER) // 8) * 8
    kernel = functools.partial(raster_kernel, reps, len(tiles))
    arrays = [*tiles, *halos, depth, gain, *point]
    count = 1 + len(arrays)
    return pl.pallas_call(
        lambda *refs: kernel(refs[:1], refs[1:count], refs[count : count + 1], *refs[count + 1 :]),
        in_specs=[pl.BlockSpec(memory_space=pltpu.SMEM)]
        + [pl.BlockSpec(memory_space=pltpu.VMEM)] * len(arrays),
        out_specs=pl.BlockSpec(memory_space=pltpu.VMEM),
        out_shape=jax.ShapeDtypeStruct((tile_rows, TC, width), F32),
        scratch_shapes=[
            pltpu.VMEM((tile_rows + 2 * BORDER, padded, width), F32),
            pltpu.VMEM((tile_rows + 2 * BORDER, padded + 16, width), F32),
        ],
        compiler_params=pltpu.CompilerParams(vmem_limit_bytes=VMEM_LIMIT),
        name="raster",
    )(place, *[pltpu.with_memory_space_constraint(x, pltpu.VMEM) for x in arrays])


def on_device(
    tokens,
    w_qkv,
    w_out,
    w_up,
    w_down,
    attn_gain,
    mlp_gain,
    dest_device,
    dest_slot,
    pillar,
    depth_weight,
    point_weight,
    raster_gain,
):
    cols, reps, toks = (lax.axis_size(a) for a in ("col", "rep", "tok"))
    tok, col, rep = (lax.axis_index(a) for a in ("tok", "col", "rep"))
    swap = shift_by(1, reps)
    scene_swap = shift_by(1, lax.axis_size("scene"))
    scene = lax.axis_index("scene")
    numbers = [col, rep, tok, TR * toks, TC * cols, scene, scene * 2 + tok % 2]
    place = jnp.stack([jnp.int32(n) for n in numbers])
    to_cols = lambda x: [lax.ppermute(x, "col", shift_by(k, cols)) for k in range(1, cols)]
    to_next = lambda xs: [lax.ppermute(x, "tok", [(i, i ^ 1) for i in range(toks)]) for x in xs]
    to_scene = lambda xs: [lax.ppermute(x, "scene", scene_swap) for x in xs]

    slabs = gather_slabs(tokens)
    heads0, hidden0, heads1, hidden1, own_hidden0, depth = prepare(
        place, w_qkv, w_out, w_up, w_down, depth_weight
    )
    units = [heads0, lax.ppermute(heads0, "rep", swap)]
    direct0 = to_cols(own_hidden0)
    q_parts, k_t, v_t, x_keep = project(place, slabs, attn_gain, 0, units, "rep")
    received = []
    for k in range(1, cols):
        part = output_rows(attention(q_parts[k], k_t, v_t), units)
        received.append(lax.ppermute(part, "col", shift_by(k, cols)))
    direct0 = relay(direct0, [part])
    next0, passed0 = to_next(direct0), to_scene(direct0)
    keep = output_rows(attention(q_parts[0], k_t, v_t, direct0), units, x_keep)
    point = split_weights(point_weight, [keep])
    keep = sum_rows(keep, received, point)
    far_rows = to_cols(
        quarter_rows(place, [heads1, hidden1], [keep, *next0, *passed0])
    )
    next_half, passed_half = cut_units(next0, passed0, [keep])
    pieces = [keep, lax.ppermute(keep, "rep", swap)]
    last0 = to_scene(next_half) + to_next(passed_half)
    outs = mlp(place, pieces, mlp_gain, 0, [hidden0, *direct0, *passed0, *next0])
    outs = mlp(place, pieces, mlp_gain, 0, last0, outs)
    others = [lax.ppermute(x, "rep", swap) for x in outs[1::2]]
    parts = sum_pairs(list(outs[::2]), others, far_rows)
    divided = [units_of_rows(x, [heads1, hidden1], parts[:1]) for x in far_rows]
    passed_rows = to_scene(relay(far_rows, parts[:1]))
    next_heads1 = to_next([x[0] for x in divided])
    gathered = [parts[0]] + [
        lax.ppermute(parts[k], "col", shift_by(k, cols)) for k in range(1, cols)
    ]
    outgoing = pack_blocks(place, gathered, dest_device, dest_slot, next_heads1)
    incoming = [outgoing[0]] + [
        lax.ppermute(outgoing[k], "tok", shift_by(k, toks)) for k in range(1, toks)
    ]
    passed = [units_of_rows(x, [heads1, hidden1]) for x in passed_rows]
    passed_heads1 = to_scene(next_heads1)
    far_heads1 = [x[0] for x in divided + passed] + next_heads1 + passed_heads1
    count = dest_device.shape[0]
    moved = place_blocks(incoming, count, tokens.shape[0] // count, [x[1] for x in passed] + passed_heads1)
    slabs = gather_slabs(moved)
    far_hidden1 = [join_units(x[1], y[1], [moved]) for x, y in zip(divided, passed)]
    next1 = to_next(far_hidden1)

    units = [heads1] + far_heads1
    q_parts, k_t, v_t, x_keep = project(place, slabs, attn_gain, 1, units, "col")
    other_part = output_rows(attention(q_parts[1], k_t, v_t), units)
    own_part = output_rows(attention(q_parts[0], k_t, v_t), units, x_keep, next1)
    from_rep = lambda x: lax.ppermute(x, "rep", swap)
    own, other = pooled_mlp(
        place,
        [(own_part, from_rep(other_part)), (other_part, from_rep(own_part))],
        pillar[None],
        mlp_gain,
        1,
        [hidden1, *far_hidden1, *next1],
    )
    sums, edges = sum_tiles(place, own, [from_rep(x) for x in other])
    tiles = [sums[0]] + [lax.ppermute(sums[k], "col", shift_by(k, cols)) for k in range(1, cols)]
    at = lambda t, c, r: (t * cols + c % cols) * reps + r
    halos = [
        lax.ppermute(
            edges[k],
            ("tok", "col", "rep"),
            [(at(t, c, reps - 1), at(t + 1, c + k, 0)) for t in range(toks - 1) for c in range(cols)]
            + [(at(t + 1, c, 0), at(t, c + k, reps - 1)) for t in range(toks - 1) for c in range(cols)],
        )
        for k in range(cols)
    ]
    return raster_layers(place, tiles, halos, depth, point, raster_gain, TR // reps)


def solution(mesh):
    placed = (
        P(("scene", "tok"), ("col", "rep")),
        P(None, None, None, ("col", "rep")),
        P(None, ("col", "rep"), None),
        P(None, None, ("col", "rep")),
        P(None, ("col", "rep"), None),
        P(),
        P(),
        P(("scene", "tok")),
        P(("scene", "tok")),
        P(("scene", "tok")),
        P(),
        P(),
        P(),
    )
    return jax.shard_map(
        on_device,
        mesh=mesh,
        in_specs=placed,
        out_specs=P(("scene", "tok", "rep"), "col", None),
        check_vma=False,
    )
```

```python
import functools

import jax
import jax.numpy as jnp
from jax import lax
from jax.experimental import pallas as pl
from jax.experimental.pallas import tpu as pltpu
from jax.sharding import PartitionSpec as P

PATCH = 1024
TR = 16
TC = 16
HD = 16
EPSILON = 1e-05
LOG2E = 1.4426950408889634
BF = jnp.bfloat16
F32 = jnp.float32
VMEM_LIMIT = 32 * 2**20
BORDER = 2


def typed(shape, kind):
    return shape if isinstance(shape[0], tuple) else (shape, kind)


def launch(body, name, scalars, arrays, outs, scratch=(), after=(), hbm=(), flops=0, exps=0, kind=F32):
    counts = [len(scalars), len(arrays) + len(hbm), len(after), len(outs)]
    starts = [sum(counts[:i]) for i in range(5)]

    def kernel(*refs):
        body(
            refs[: starts[1]],
            refs[starts[1] : starts[2]],
            refs[starts[3] : starts[4]],
            *refs[starts[4] :],
        )

    return pl.pallas_call(
        kernel,
        in_specs=[pl.BlockSpec(memory_space=pltpu.SMEM)] * counts[0]
        + [pl.BlockSpec(memory_space=pltpu.VMEM)] * counts[1]
        + [pl.BlockSpec(memory_space=pl.ANY)] * counts[2],
        out_specs=[pl.BlockSpec(memory_space=pltpu.VMEM)] * counts[3],
        out_shape=[pltpu.VMEM(*typed(x, kind)) for x in outs],
        scratch_shapes=[pltpu.VMEM(*typed(x, F32)) for x in scratch],
        compiler_params=pltpu.CompilerParams(vmem_limit_bytes=VMEM_LIMIT),
        cost_estimate=pl.CostEstimate(flops=flops, bytes_accessed=0, transcendentals=exps),
        name=name,
    )(
        *scalars,
        *[pltpu.with_memory_space_constraint(x, pltpu.VMEM) for x in arrays],
        *hbm,
        *after,
    )


def split2(x):
    high = x.astype(BF)
    return high, (x - high.astype(F32)).astype(BF)


def split3(x):
    first = x.astype(BF)
    rest = x - first.astype(F32)
    second = rest.astype(BF)
    return first, second, (rest - second.astype(F32)).astype(BF)


def dot3(left, right, dims=(((1,), (0,)), ((), ()))):
    lh, ll = left
    rh, rl = right
    dot = functools.partial(lax.dot_general, dimension_numbers=dims, preferred_element_type=F32)
    if lh.shape[1] % 128:
        return dot(lh, rh) + dot(lh, rl) + dot(ll, rh)
    lefts = jnp.concatenate([lh, lh, ll], axis=1)
    return dot(lefts, jnp.concatenate([rh, rl, rh], axis=dims[0][1][0]))


def layer_norm(values, gain_row):
    average = jnp.mean(values, axis=-1, keepdims=True)
    centered = values - average
    variance = jnp.mean(centered * centered, axis=-1, keepdims=True)
    return centered * lax.rsqrt(variance + EPSILON) * gain_row


def shift_by(k, count):
    return [(i, (i + k) % count) for i in range(count)]


def gather_slabs(piece):
    cols = lax.axis_size("col")
    reps = lax.axis_size("rep")
    far = [lax.ppermute(piece, "col", shift_by(k, cols)) for k in range(1, cols)]
    return [(p, lax.ppermute(p, "rep", shift_by(1, reps))) for p in [piece] + far]


def sliced(ref, part, parts):
    size = ref.shape[1] // parts
    return ref[:, pl.ds(pl.multiple_of(part * size, size), size), :]


def prepare(place, w_qkv, w_out, w_up, w_down, depth_weight):
    width = w_out.shape[-1]
    features, hidden = w_out.shape[1], w_down.shape[1]

    def body(scalars, ins, outs):
        (place,) = scalars
        qkv, out, up, down, depth = ins
        for layer in range(2):
            for a in range(3):
                for b in range(3):
                    i = layer * 9 + a * 3 + b
                    outs[5][i : i + 1, :] = depth[layer, a, b : b + 1, :]
        for layer in range(2):
            heads, units = outs[2 * layer], outs[2 * layer + 1]
            for j in range(3):
                heads[j] = qkv[layer, j].T
            heads[3] = out[layer]
            units[0] = up[layer].T
            units[1] = down[layer]
        outs[4][...] = sliced(outs[1], place[6], 4)

    per_layer = [(4, features, width), (2, hidden, width)]
    return launch(
        body,
        "prepare",
        [place],
        [],
        per_layer * 2 + [(2, hidden // 4, width), (18, width)],
        hbm=[w_qkv, w_out, w_up, w_down, depth_weight],
        flops=8 * 10**9,
    )


def project(place, slabs, gain, layer, units, halves, after=()):
    cols = len(slabs)
    rows = slabs[0][0].shape[0]
    width = units[0].shape[-1]
    features = sum(u.shape[1] for u in units)
    half = rows // lax.axis_size(halves)
    parts = cols if halves == "rep" else lax.axis_size("rep")
    part = half // parts

    def body(scalars, ins, outs, x_all, norm_high, norm_low):
        (place,) = scalars
        pieces, units = ins[: 2 * cols], ins[2 * cols + 1 :]
        gain = ins[2 * cols][layer : layer + 1, :]
        q_parts, (k_t, v_t, x_keep) = outs[:parts], outs[parts:]
        col, rep = place[0], place[1]
        slab = width // cols
        for k in range(cols):
            near, other = pieces[2 * k][...], pieces[2 * k + 1][...]
            low = jnp.where(rep == 0, near, other)
            high = jnp.where(rep == 0, other, near)
            at = pl.multiple_of(lax.rem(col + cols - k, cols) * slab, 128)
            x_all[:, pl.ds(at, slab)] = jnp.concatenate([low, high], axis=1)
        weights = [split2(jnp.concatenate([u[j] for u in units], axis=0)) for j in range(3)]
        dims = (((1,), (1,)), ((), ()))
        chunk = 256
        for start in range(0, rows, chunk):
            here = slice(start, start + chunk)
            high, low = split2(layer_norm(x_all[here, :], gain))
            norm_high[here, :] = high
            norm_low[here, :] = low
            k_t[:, here] = dot3(weights[1], (high, low), dims)
            v_t[:, here] = dot3(weights[2], (high, low), dims)
        outer, inner = (rep, col) if halves == "rep" else (col, rep)
        for k in range(parts):
            at = outer * half + lax.rem(inner + k, parts) * part
            here = pl.ds(pl.multiple_of(at, part), part)
            if k == 0:
                x_keep[...] = x_all[here, :]
            normed = norm_high[here, :], norm_low[here, :]
            q_parts[k][...] = dot3(weights[0], normed, dims) * (LOG2E * HD**-0.5)

    *q_parts, k_t, v_t, x_keep = launch(
        body,
        "project",
        [place],
        [p for pair in slabs for p in pair] + [gain] + units,
        [(features, part)] * parts + [(features, rows)] * 2 + [(part, width)],
        [(rows, width)] + [((rows, width), BF)] * 2,
        after,
    )
    return q_parts, k_t, v_t, x_keep


def attention(q_t, k_t, v_t, after=(), heads_per_step=16):
    features, count = q_t.shape
    rows = k_t.shape[1]
    chunk = min(256, count)
    heads_per_step = min(heads_per_step, features // HD)

    def body(scalars, ins, outs):
        q_t, k_t, v_t = ins
        (attended,) = outs

        def group(step, carry):
            def head_rows(h):
                return pl.ds(pl.multiple_of((step * heads_per_step + h) * HD, HD), HD)

            def scores(h, at):
                k1, k2, k3 = split3(k_t[head_rows(h), :])
                q1, q2, q3 = split3(q_t[head_rows(h), at : at + chunk])
                return lax.dot_general(
                    jnp.concatenate([k1, k2, k1, k3, k2, k1], axis=0),
                    jnp.concatenate([q1, q1, q2, q1, q2, q3], axis=0),
                    (((0,), (0,)), ((), ())),
                    preferred_element_type=F32,
                )

            items = [(h, at) for h in range(heads_per_step) for at in range(0, count, chunk)]
            current = scores(*items[0])
            for i, (h, at) in enumerate(items):
                following = scores(*items[i + 1]) if i + 1 < len(items) else None
                v1, v2 = split2(v_t[head_rows(h), :])
                ones = jnp.ones_like(v1)
                weights = jnp.exp2(current - jnp.max(current, axis=0, keepdims=True))
                high, low = split2(weights)
                first = jnp.dot(
                    jnp.concatenate([v1, v2, ones], axis=0), high, preferred_element_type=F32
                )
                second = jnp.dot(
                    jnp.concatenate([v1, ones], axis=0), low, preferred_element_type=F32
                )
                total = first[:HD] + first[HD : 2 * HD] + second[:HD]
                norm = first[2 * HD : 2 * HD + 1] + second[HD : HD + 1]
                attended[head_rows(h), at : at + chunk] = total / norm
                current = following
            return carry

        steps = features // HD // heads_per_step
        if steps == 1:
            group(0, 0)
        else:
            lax.fori_loop(0, steps, group, 0)

    (attended,) = launch(
        body,
        "attention",
        [],
        [q_t, k_t, v_t],
        [(features, count)],
        after=after,
        flops=10**9,
        exps=features // HD * rows * count,
    )
    return attended


def output_rows(attended, units, residual=None, after=()):
    width = units[0].shape[-1]
    count = attended.shape[1]
    more = [] if residual is None else [residual]

    def body(scalars, ins, outs):
        attended, units = ins[0], ins[1 : 1 + len(units_in)]
        w_out = split2(jnp.concatenate([u[3] for u in units], axis=0))
        result = dot3(split2(attended[...].T), w_out)
        if more:
            result = result + ins[-1][...]
        outs[0][...] = result

    units_in = units
    (out,) = launch(
        body, "output_rows", [], [attended] + units + more, [(count, width)], after=after
    )
    return out


def sum_rows(keep, received, after=()):
    def body(scalars, ins, outs):
        outs[0][...] = functools.reduce(jnp.add, [x[...] for x in ins])

    (out,) = launch(body, "sum_rows", [], [keep] + received, [keep.shape], after=after)
    return out


def cut_units(firsts, seconds, after=()):
    kinds, count, width = firsts[0].shape
    size = count // 2
    total = len(firsts)

    def body(scalars, ins, outs):
        for x, out in zip(ins[:total], outs[:total]):
            out[...] = x[:, :size, :]
        for x, out in zip(ins[total:], outs[total:]):
            out[...] = x[:, size:, :]

    arrays = [*firsts, *seconds]
    halves = launch(
        body, "cut_units", [], arrays, [(kinds, size, width)] * len(arrays), after=after
    )
    return halves[:total], halves[total:]


def sum_pairs(own, received, after=()):
    def body(scalars, ins, outs):
        for k, out in enumerate(outs):
            out[...] = ins[k][...] + ins[len(own) + k][...]

    return launch(body, "sum_pairs", [], own + received, [x.shape for x in own], after=after)


def join_units(units, after=()):
    kinds, count, width = units[0].shape

    def body(scalars, ins, outs):
        for i, x in enumerate(ins):
            outs[0][:, i * count : (i + 1) * count, :] = x[...]

    shape = (kinds, len(units) * count, width)
    (out,) = launch(body, "join_units", [], units, [shape], after=after)
    return out


def share_rows(place, units, shares, after=()):
    width = units[0].shape[-1]
    sizes = [u.shape[1] // (4 * n) for u, n in zip(units, shares)]

    def body(scalars, ins, outs):
        at = 0
        for ref, size, n in zip(ins, sizes, shares):
            start = pl.multiple_of(scalars[0][6] * (n * size), size)
            for j in range(ref.shape[0]):
                outs[0][at : at + size, :] = ref[j, pl.ds(start, size), :]
                at += size

    total = sum(u.shape[0] * size for u, size in zip(units, sizes))
    (out,) = launch(body, "share_rows", [place], units, [(total, width)], after=after)
    return out


def second_share(place, unit, after=()):
    def body(scalars, ins, outs):
        outs[0][...] = sliced(ins[0], scalars[0][6] * 2 + 1, 8)

    kinds, count, width = unit.shape
    (out,) = launch(
        body, "second_share", [place], [unit], [(kinds, count // 8, width)], after=after
    )
    return out


def units_of_rows(rows, units, shares, after=()):
    shapes = [(u.shape[0], u.shape[1] // (4 * n), u.shape[2]) for u, n in zip(units, shares)]

    def body(scalars, ins, outs):
        at = 0
        for out in outs:
            size = out.shape[1]
            for j in range(out.shape[0]):
                out[j] = ins[0][at : at + size, :]
                at += size

    return launch(body, "units_of_rows", [], [rows], shapes, after=after)


def relay(arrays, after):
    def body(scalars, ins, outs):
        for x, out in zip(ins, outs):
            out[...] = x[...]

    return launch(body, "relay", [], arrays, [x.shape for x in arrays], after=after)


def split_weights(weights, after):
    def body(scalars, ins, outs):
        for out, part in zip(outs, split2(ins[0][...])):
            out[...] = part

    return launch(
        body, "split_weights", [], [], [weights.shape] * 2, after=after, hbm=[weights], kind=BF
    )


def hidden_units(normed, up, down):
    hidden = dot3(normed, up, (((1,), (1,)), ((), ())))
    hidden = split2(hidden * (0.5 + 0.5 * lax.erf(hidden * 0.5**0.5)))
    return dot3(hidden, down)


def features_of(partial, col, rep, cols, reps):
    feature = partial.shape[1] // (cols * reps)
    for k in range(cols):
        for j in range(reps):
            to_rep = lax.rem(rep + j, reps)
            to_col = lax.rem(col + k, cols)
            if feature % 128 == 0:
                at = pl.multiple_of((to_col * reps + to_rep) * feature, 128)
                yield partial[:, pl.ds(at, feature)]
            else:
                at = pl.multiple_of(to_col * reps * feature, 128)
                slab = partial[:, pl.ds(at, reps * feature)]
                yield jnp.where(to_rep == 0, slab[:, :feature], slab[:, feature:])


def mlp(place, pieces, gain, layer, units):
    cols, reps = lax.axis_size("col"), len(pieces)
    part, width = pieces[0].shape
    rows = part * reps
    hidden = sum(u.shape[1] for u in units)

    def body(scalars, ins, outs, partial):
        (place,) = scalars
        pieces, units = ins[:reps], ins[reps + 1 :]
        gain = ins[reps][layer : layer + 1, :]
        col, rep = place[0], place[1]
        up, down = (split2(jnp.concatenate([u[j] for u in units], axis=0)) for j in range(2))
        for k in range(reps):
            here = pl.ds(pl.multiple_of(lax.rem(rep + reps - k, reps) * part, 128), part)
            values = pieces[k][...]
            high, low = split2(layer_norm(values, gain))
            outs[-2][here, :] = high
            outs[-1][here, :] = low
            result = hidden_units((high, low), up, down)
            partial[here, :] = result + values if k == 0 else result
        for out, values in zip(outs, features_of(partial, col, rep, cols, reps)):
            out[...] = values

    *outs, high, low = launch(
        body,
        "mlp",
        [place],
        pieces + [gain] + units,
        [(rows, width // (cols * reps))] * (cols * reps) + [((rows, width), BF)] * 2,
        [(rows, width)],
        flops=4 * rows * width * hidden * 3,
    )
    return outs, (high, low)


def mlp_rest(place, normed, units, base):
    cols, reps = lax.axis_size("col"), lax.axis_size("rep")
    rows, width = normed[0].shape

    def body(scalars, ins, outs, partial):
        (place,) = scalars
        base, units = ins[2 : 2 + len(outs)], ins[2 + len(outs) :]
        up, down = (split2(jnp.concatenate([u[j] for u in units], axis=0)) for j in range(2))
        partial[...] = hidden_units((ins[0][...], ins[1][...]), up, down)
        shares = features_of(partial, place[0], place[1], cols, reps)
        for out, values, before in zip(outs, shares, base):
            out[...] = before[...] + values

    return launch(
        body,
        "mlp_rest",
        [place],
        [*normed, *base, *units],
        [x.shape for x in base],
        [(rows, width)],
        flops=10**9,
    )


def pooled_mlp(place, pieces, pillar, gain, layer, units):
    cols = lax.axis_size("col")
    part, width = pieces[0][0].shape
    half = 2 * part
    wide, lead, lead_step = tile_border(cols)
    tile_rows = TR // lax.axis_size("rep")
    count = -(-(tile_rows + BORDER) * wide // 8) * 8
    hidden = sum(u.shape[1] for u in units)

    def body(scalars, ins, outs):
        (place,) = scalars
        pieces, (pillar, gains), units = ins[:4], ins[4:6], ins[6:]
        gain = gains[layer : layer + 1, :]
        col, rep, tok, full_width = (place[i] for i in (0, 1, 2, 4))
        flat = lax.broadcasted_iota(jnp.int32, (count, 1), 0)
        row = (flat * (-(-(2**16) // wide))) >> 16
        column = flat - row * wide - lead
        cells = []
        for k in range(cols):
            for j in range(2):
                x = lax.rem(col + k, cols) * (TC - lead_step) + column
                y = tok * TR + lax.rem(rep + j, 2) * (tile_rows - BORDER) + row
                cells.append(jnp.where((x >= 0) & (x < full_width), y * full_width + x, -2))
        up, down = (split2(jnp.concatenate([u[j] for u in units], axis=0)) for j in range(2))
        totals = [None] * (2 * cols)
        for k in range(2):
            source = lax.rem(rep + k, 2) * part
            tokens_cells = pillar[:, pl.ds(pl.multiple_of(col * half + source, 128), part)]
            values = pieces[2 * k][...] + pieces[2 * k + 1][...]
            result = hidden_units(split2(layer_norm(values, gain)), up, down)
            if k == 0:
                result = result + values
            high, low = split2(result)
            for i in range(2 * cols):
                chosen = jnp.where(cells[i] == tokens_cells, 1.0, 0.0).astype(BF)
                term = jnp.dot(chosen, high, preferred_element_type=F32) + jnp.dot(
                    chosen, low, preferred_element_type=F32
                )
                totals[i] = term if totals[i] is None else totals[i] + term
        for i in range(2 * cols):
            outs[i][...] = totals[i]

    outs = launch(
        body,
        "mlp_pool",
        [place],
        [x for pair in pieces for x in pair] + [pillar, gain] + units,
        [(count, width)] * (2 * cols),
        flops=4 * half * width * hidden * 3,
    )
    return outs[::2], outs[1::2]


def tile_border(cols):
    return (TC + BORDER, 0, BORDER) if cols == 2 else (TC + 2 * BORDER, BORDER, 0)


def block_capacity(count, peers):
    return max(2, (count + peers - 4) // (peers - 1))


def pack_blocks(place, gathered, dest_device, dest_slot, after=()):
    cols, reps, toks = (lax.axis_size(a) for a in ("col", "rep", "tok"))
    count = dest_device.shape[0]
    each = count // (reps * cols)
    rows, feature = gathered[0].shape
    size = rows // (reps * each)
    capacity = block_capacity(count, toks)
    codes = capacity * size
    length = codes + -(-capacity // 8) * 8

    def body(scalars, ins, outs, blocks, packed):
        place, device, slot = scalars
        col, tok = place[0], place[2]
        for k in range(cols):
            blocks[k * rows : (k + 1) * rows, :] = ins[k][...]
        for k in range(toks):
            packed[k * length + codes : (k + 1) * length, :] = jnp.zeros(
                (length - codes, feature), F32
            )
        targets = [device[b] for b in range(count)]
        for b in range(count):
            rank = jnp.int32(0)
            for earlier in targets[:b]:
                rank = rank + (earlier == targets[b]).astype(jnp.int32)
            shift = lax.rem(targets[b] - tok + toks, toks)
            of_rep, of_col = b // (each * cols), b // each % cols
            position = (lax.rem(col - of_col + cols, cols) * reps + of_rep) * each + b % each
            start = shift * length
            packed[pl.ds(pl.multiple_of(start + rank * size, 8), size), :] = blocks[
                pl.ds(pl.multiple_of(position * size, 8), size), :
            ]
            code = jnp.full((1, feature), (slot[b] + 1).astype(F32))
            packed[pl.ds(start + codes + rank, 1), :] = code
        for k in range(toks):
            outs[k][...] = packed[k * length : (k + 1) * length, :]

    return launch(
        body,
        "pack_blocks",
        [place, dest_device, dest_slot],
        list(gathered),
        [(length, feature)] * toks,
        [(cols * rows, feature), (toks * length, feature)],
        after,
    )


def place_blocks(incoming, count, size, after=()):
    feature = incoming[0].shape[1]
    capacity = block_capacity(count, len(incoming))

    def body(scalars, ins, outs):
        codes = [
            [jnp.max(x[capacity * size + j : capacity * size + j + 1, :]) for j in range(capacity)]
            for x in ins
        ]
        for x, slots in zip(ins, codes):
            for j, code in enumerate(slots):
                slot = code.astype(jnp.int32) - 1

                @pl.when(slot >= 0)
                def _(x=x, j=j, slot=slot):
                    at = pl.multiple_of(slot * size, 8)
                    outs[0][pl.ds(at, size), :] = x[j * size : (j + 1) * size, :]

    (placed,) = launch(
        body, "place_blocks", [], list(incoming), [(count * size, feature)], after=after
    )
    return placed


def sum_tiles(place, own, received):
    count = len(own)
    wide = tile_border(count)[0]
    edge = BORDER * wide
    last = TR // lax.axis_size("rep") * wide
    width = own[0].shape[1]

    def body(scalars, ins, outs):
        rep = scalars[0][1]
        for k in range(count):
            total = ins[k][...] + ins[count + k][...]
            outs[k][...] = total
            outs[count + k][...] = jnp.where(
                rep == 0, total[:edge], total[last : last + edge]
            )

    outs = launch(
        body,
        "sum_tiles",
        [place],
        list(own) + received,
        [x.shape for x in own] + [(edge, width)] * count,
    )
    return list(outs[:count]), list(outs[count:])


def raster_kernel(reps, cols, scalars, ins, outs, cells, normed):
    (place,) = scalars
    tiles, halos = ins[:cols], ins[cols : 2 * cols]
    depth, gain, point_high, point_low = ins[2 * cols :]
    (out_ref,) = outs
    tok, col, rep, height, full_width = (place[i] for i in (2, 0, 1, 3, 4))
    tile_rows = out_ref.shape[0]
    tile_cols = out_ref.shape[1]
    width = out_ref.shape[2]
    wide = tile_border(cols)[0]
    kept = tile_rows + BORDER
    padded = cells.shape[1]
    cells[...] = jnp.zeros_like(cells)
    normed[...] = jnp.zeros_like(normed)
    full = tile_cols + 2 * BORDER

    def row_of(arrays, i):
        values = functools.reduce(jnp.add, [x[i * wide : (i + 1) * wide, :] for x in arrays])
        if wide < full:
            none = jnp.zeros((full - wide, width), F32)
            values = jnp.where(
                col == 0,
                jnp.concatenate([none, values], axis=0),
                jnp.concatenate([values, none], axis=0),
            )
        return values

    first = BORDER * (1 - rep)
    for i in range(kept):
        cells[first + i, 0:full, :] = row_of(tiles, i)
    other = (tile_rows + BORDER) * rep
    for i in range(BORDER):
        cells[other + i, 0:full, :] = row_of(halos, i)
    lead = 8
    row_zero = tok * (tile_rows * reps) + rep * tile_rows - BORDER
    col_zero = col * tile_cols - BORDER
    for layer in range(2):
        rim = layer + 1
        grid_rows = tile_rows + 2 * BORDER - 2 * rim
        low_col, span = (0, padded) if layer == 0 else (BORDER, tile_cols)
        values = cells[...]
        mean = jnp.mean(values * values, axis=-1, keepdims=True)
        normed[:, lead : lead + padded, :] = values * lax.rsqrt(mean + EPSILON) * gain[layer : layer + 1]
        mixed = None
        for b in range(3):
            start = lead + low_col + b - 1
            shifted = normed[rim - 1 : rim + 1 + grid_rows, start : start + span, :]
            for a in range(3):
                i = layer * 9 + a * 3 + b
                term = shifted[a : a + grid_rows] * depth[i : i + 1, :][None]
                mixed = term if mixed is None else mixed + term
        left = split2(mixed.reshape(grid_rows * span, width))
        value = dot3(left, (point_high[layer, :, :width], point_low[layer, :, :width]))
        gate = dot3(left, (point_high[layer, :, width:], point_low[layer, :, width:]))
        change = (value * jax.nn.sigmoid(gate)).reshape(grid_rows, span, width)
        centre = cells[rim : rim + grid_rows, low_col : low_col + span, :]
        if layer == 0:
            row = row_zero + rim + lax.broadcasted_iota(jnp.int32, (grid_rows, span, 1), 0)
            column = col_zero + lax.broadcasted_iota(jnp.int32, (grid_rows, span, 1), 1)
            inside = (row >= 0) & (row < height) & (column >= 0) & (column < full_width)
            cells[rim : rim + grid_rows, :, :] = jnp.where(inside, centre + change, 0.0)
        else:
            out_ref[...] = centre + change


def raster_layers(place, tiles, halos, depth, point, gain, tile_rows):
    reps = lax.axis_size("rep")
    width = depth.shape[-1]
    padded = -(-(TC + 2 * BORDER) // 8) * 8
    kernel = functools.partial(raster_kernel, reps, len(tiles))
    arrays = [*tiles, *halos, depth, gain, *point]
    count = 1 + len(arrays)
    return pl.pallas_call(
        lambda *refs: kernel(refs[:1], refs[1:count], refs[count : count + 1], *refs[count + 1 :]),
        in_specs=[pl.BlockSpec(memory_space=pltpu.SMEM)]
        + [pl.BlockSpec(memory_space=pltpu.VMEM)] * len(arrays),
        out_specs=pl.BlockSpec(memory_space=pltpu.VMEM),
        out_shape=jax.ShapeDtypeStruct((tile_rows, TC, width), F32),
        scratch_shapes=[
            pltpu.VMEM((tile_rows + 2 * BORDER, padded, width), F32),
            pltpu.VMEM((tile_rows + 2 * BORDER, padded + 16, width), F32),
        ],
        compiler_params=pltpu.CompilerParams(vmem_limit_bytes=VMEM_LIMIT),
        name="raster",
    )(place, *[pltpu.with_memory_space_constraint(x, pltpu.VMEM) for x in arrays])


def on_device(
    tokens,
    w_qkv,
    w_out,
    w_up,
    w_down,
    attn_gain,
    mlp_gain,
    dest_device,
    dest_slot,
    pillar,
    depth_weight,
    point_weight,
    raster_gain,
):
    cols, reps, toks = (lax.axis_size(a) for a in ("col", "rep", "tok"))
    tok, col, rep = (lax.axis_index(a) for a in ("tok", "col", "rep"))
    swap = shift_by(1, reps)
    scene_swap = shift_by(1, lax.axis_size("scene"))
    scene = lax.axis_index("scene")
    numbers = [col, rep, tok, TR * toks, TC * cols, scene, scene * 2 + tok % 2]
    place = jnp.stack([jnp.int32(n) for n in numbers])
    to_cols = lambda x: [lax.ppermute(x, "col", shift_by(k, cols)) for k in range(1, cols)]
    to_next = lambda xs: [lax.ppermute(x, "tok", [(i, i ^ 1) for i in range(toks)]) for x in xs]
    to_scene = lambda xs: [lax.ppermute(x, "scene", scene_swap) for x in xs]

    slabs = gather_slabs(tokens)
    heads0, hidden0, heads1, hidden1, own_hidden0, depth = prepare(
        place, w_qkv, w_out, w_up, w_down, depth_weight
    )
    units = [heads0, lax.ppermute(heads0, "rep", swap)]
    direct0 = to_cols(own_hidden0)
    q_parts, k_t, v_t, x_keep = project(place, slabs, attn_gain, 0, units, "rep")
    received = []
    for k in range(1, cols):
        part = output_rows(attention(q_parts[k], k_t, v_t), units)
        received.append(lax.ppermute(part, "col", shift_by(k, cols)))
    direct0 = relay(direct0, [part])
    next0, passed0 = to_next(direct0), to_scene(direct0)
    keep = output_rows(attention(q_parts[0], k_t, v_t, direct0), units, x_keep)
    point = split_weights(point_weight, [keep])
    keep = sum_rows(keep, received, point)
    far_rows = to_cols(
        share_rows(place, [heads1, hidden1], (1, 2), [keep, *next0, *passed0])
    )
    next_half, passed_half = cut_units(next0, passed0, [keep])
    pieces = [keep, lax.ppermute(keep, "rep", swap)]
    last0 = to_scene(next_half) + to_next(passed_half)
    outs, normed = mlp(place, pieces, mlp_gain, 0, [hidden0, *direct0, *passed0, *next0])
    outs = mlp_rest(place, normed, last0, outs)
    others = [lax.ppermute(x, "rep", swap) for x in outs[1::2]]
    parts = sum_pairs(list(outs[::2]), others)
    divided = [units_of_rows(x, [heads1, hidden1], (1, 2), parts[:1]) for x in far_rows]
    passed_rows = to_scene(relay(far_rows, parts[:1]))
    next_heads1 = to_next([x[0] for x in divided])
    gathered = [parts[0]] + [
        lax.ppermute(parts[k], "col", shift_by(k, cols)) for k in range(1, cols)
    ]
    outgoing = pack_blocks(place, gathered, dest_device, dest_slot, next_heads1)
    rest = to_cols(second_share(place, hidden1, divided[0][:1]))
    passed_rest = to_scene(rest)
    incoming = [outgoing[0]] + [
        lax.ppermute(outgoing[k], "tok", shift_by(k, toks)) for k in range(1, toks)
    ]
    passed = [units_of_rows(x, [heads1, hidden1], (1, 2)) for x in passed_rows]
    passed_heads1 = to_scene(next_heads1)
    far_heads1 = [x[0] for x in divided + passed] + next_heads1 + passed_heads1
    count = dest_device.shape[0]
    moved = place_blocks(incoming, count, tokens.shape[0] // count, [x[1] for x in passed] + passed_heads1 + rest)
    slabs = gather_slabs(moved)
    far_hidden1 = [
        join_units([x[1], y[1], z, w], [moved])
        for x, y, z, w in zip(divided, passed, rest, passed_rest)
    ]
    next1 = to_next(far_hidden1)

    units = [heads1] + far_heads1
    q_parts, k_t, v_t, x_keep = project(place, slabs, attn_gain, 1, units, "col")
    other_part = output_rows(attention(q_parts[1], k_t, v_t), units)
    own_part = output_rows(attention(q_parts[0], k_t, v_t), units, x_keep, next1)
    from_rep = lambda x: lax.ppermute(x, "rep", swap)
    own, other = pooled_mlp(
        place,
        [(own_part, from_rep(other_part)), (other_part, from_rep(own_part))],
        pillar[None],
        mlp_gain,
        1,
        [hidden1, *far_hidden1, *next1],
    )
    sums, edges = sum_tiles(place, own, [from_rep(x) for x in other])
    tiles = [sums[0]] + [lax.ppermute(sums[k], "col", shift_by(k, cols)) for k in range(1, cols)]
    at = lambda t, c, r: (t * cols + c % cols) * reps + r
    halos = [
        lax.ppermute(
            edges[k],
            ("tok", "col", "rep"),
            [(at(t, c, reps - 1), at(t + 1, c + k, 0)) for t in range(toks - 1) for c in range(cols)]
            + [(at(t + 1, c, 0), at(t, c + k, reps - 1)) for t in range(toks - 1) for c in range(cols)],
        )
        for k in range(cols)
    ]
    return raster_layers(place, tiles, halos, depth, point, raster_gain, TR // reps)


def solution(mesh):
    placed = (
        P(("scene", "tok"), ("col", "rep")),
        P(None, None, None, ("col", "rep")),
        P(None, ("col", "rep"), None),
        P(None, None, ("col", "rep")),
        P(None, ("col", "rep"), None),
        P(),
        P(),
        P(("scene", "tok")),
        P(("scene", "tok")),
        P(("scene", "tok")),
        P(),
        P(),
        P(),
    )
    return jax.shard_map(
        on_device,
        mesh=mesh,
        in_specs=placed,
        out_specs=P(("scene", "tok", "rep"), "col", None),
        check_vma=False,
    )
```

```python
import functools

import jax
import jax.numpy as jnp
from jax import lax
from jax.experimental import pallas as pl
from jax.experimental.pallas import tpu as pltpu
from jax.sharding import PartitionSpec as P

PATCH = 1024
TR = 16
TC = 16
HD = 16
EPSILON = 1e-05
LOG2E = 1.4426950408889634
BF = jnp.bfloat16
F32 = jnp.float32
VMEM_LIMIT = 32 * 2**20
BORDER = 2


def typed(shape, kind):
    return shape if isinstance(shape[0], tuple) else (shape, kind)


def launch(body, name, scalars, arrays, outs, scratch=(), after=(), hbm=(), flops=0, exps=0, kind=F32):
    counts = [len(scalars), len(arrays) + len(hbm), len(after), len(outs)]
    starts = [sum(counts[:i]) for i in range(5)]

    def kernel(*refs):
        body(
            refs[: starts[1]],
            refs[starts[1] : starts[2]],
            refs[starts[3] : starts[4]],
            *refs[starts[4] :],
        )

    return pl.pallas_call(
        kernel,
        in_specs=[pl.BlockSpec(memory_space=pltpu.SMEM)] * counts[0]
        + [pl.BlockSpec(memory_space=pltpu.VMEM)] * counts[1]
        + [pl.BlockSpec(memory_space=pl.ANY)] * counts[2],
        out_specs=[pl.BlockSpec(memory_space=pltpu.VMEM)] * counts[3],
        out_shape=[pltpu.VMEM(*typed(x, kind)) for x in outs],
        scratch_shapes=[pltpu.VMEM(*typed(x, F32)) for x in scratch],
        compiler_params=pltpu.CompilerParams(vmem_limit_bytes=VMEM_LIMIT),
        cost_estimate=pl.CostEstimate(flops=flops, bytes_accessed=0, transcendentals=exps),
        name=name,
    )(
        *scalars,
        *[pltpu.with_memory_space_constraint(x, pltpu.VMEM) for x in arrays],
        *hbm,
        *after,
    )


def split2(x):
    high = x.astype(BF)
    return high, (x - high.astype(F32)).astype(BF)


def split3(x):
    first = x.astype(BF)
    rest = x - first.astype(F32)
    second = rest.astype(BF)
    return first, second, (rest - second.astype(F32)).astype(BF)


def dot3(left, right, dims=(((1,), (0,)), ((), ()))):
    lh, ll = left
    rh, rl = right
    dot = functools.partial(lax.dot_general, dimension_numbers=dims, preferred_element_type=F32)
    if lh.shape[1] % 128:
        return dot(lh, rh) + dot(lh, rl) + dot(ll, rh)
    lefts = jnp.concatenate([lh, lh, ll], axis=1)
    return dot(lefts, jnp.concatenate([rh, rl, rh], axis=dims[0][1][0]))


def layer_norm(values, gain_row):
    average = jnp.mean(values, axis=-1, keepdims=True)
    centered = values - average
    variance = jnp.mean(centered * centered, axis=-1, keepdims=True)
    return centered * lax.rsqrt(variance + EPSILON) * gain_row


def shift_by(k, count):
    return [(i, (i + k) % count) for i in range(count)]


def gather_slabs(piece):
    cols = lax.axis_size("col")
    reps = lax.axis_size("rep")
    far = [lax.ppermute(piece, "col", shift_by(k, cols)) for k in range(1, cols)]
    return [(p, lax.ppermute(p, "rep", shift_by(1, reps))) for p in [piece] + far]


def sliced(ref, part, parts):
    size = ref.shape[1] // parts
    return ref[:, pl.ds(pl.multiple_of(part * size, size), size), :]


def prepare(place, w_qkv, w_out, w_up, w_down, depth_weight):
    width = w_out.shape[-1]
    features, hidden = w_out.shape[1], w_down.shape[1]

    def body(scalars, ins, outs):
        (place,) = scalars
        qkv, out, up, down, depth = ins
        for layer in range(2):
            for a in range(3):
                for b in range(3):
                    i = layer * 9 + a * 3 + b
                    outs[5][i : i + 1, :] = depth[layer, a, b : b + 1, :]
        for layer in range(2):
            heads, units = outs[2 * layer], outs[2 * layer + 1]
            for j in range(3):
                heads[j] = qkv[layer, j].T
            heads[3] = out[layer]
            units[0] = up[layer].T
            units[1] = down[layer]
        outs[4][...] = sliced(outs[1], place[6], 4)

    per_layer = [(4, features, width), (2, hidden, width)]
    return launch(
        body,
        "prepare",
        [place],
        [],
        per_layer * 2 + [(2, hidden // 4, width), (18, width)],
        hbm=[w_qkv, w_out, w_up, w_down, depth_weight],
        flops=8 * 10**9,
    )


def project(place, slabs, gain, layer, units, halves, after=()):
    cols = len(slabs)
    rows = slabs[0][0].shape[0]
    width = units[0].shape[-1]
    features = sum(u.shape[1] for u in units)
    half = rows // lax.axis_size(halves)
    parts = cols if halves == "rep" else lax.axis_size("rep")
    part = half // parts

    def body(scalars, ins, outs, x_all, norm_high, norm_low):
        (place,) = scalars
        pieces, units = ins[: 2 * cols], ins[2 * cols + 1 :]
        gain = ins[2 * cols][layer : layer + 1, :]
        q_parts, (k_t, v_t, x_keep) = outs[:parts], outs[parts:]
        col, rep = place[0], place[1]
        slab = width // cols
        for k in range(cols):
            near, other = pieces[2 * k][...], pieces[2 * k + 1][...]
            low = jnp.where(rep == 0, near, other)
            high = jnp.where(rep == 0, other, near)
            at = pl.multiple_of(lax.rem(col + cols - k, cols) * slab, 128)
            x_all[:, pl.ds(at, slab)] = jnp.concatenate([low, high], axis=1)
        weights = [split2(jnp.concatenate([u[j] for u in units], axis=0)) for j in range(3)]
        dims = (((1,), (1,)), ((), ()))
        chunk = 256
        for start in range(0, rows, chunk):
            here = slice(start, start + chunk)
            high, low = split2(layer_norm(x_all[here, :], gain))
            norm_high[here, :] = high
            norm_low[here, :] = low
            k_t[:, here] = dot3(weights[1], (high, low), dims)
            v_t[:, here] = dot3(weights[2], (high, low), dims)
        outer, inner = (rep, col) if halves == "rep" else (col, rep)
        for k in range(parts):
            at = outer * half + lax.rem(inner + k, parts) * part
            here = pl.ds(pl.multiple_of(at, part), part)
            if k == 0:
                x_keep[...] = x_all[here, :]
            normed = norm_high[here, :], norm_low[here, :]
            q_parts[k][...] = dot3(weights[0], normed, dims) * (LOG2E * HD**-0.5)

    *q_parts, k_t, v_t, x_keep = launch(
        body,
        "project",
        [place],
        [p for pair in slabs for p in pair] + [gain] + units,
        [(features, part)] * parts + [(features, rows)] * 2 + [(part, width)],
        [(rows, width)] + [((rows, width), BF)] * 2,
        after,
    )
    return q_parts, k_t, v_t, x_keep


def attention(q_t, k_t, v_t, after=(), heads_per_step=16):
    features, count = q_t.shape
    rows = k_t.shape[1]
    chunk = min(256, count)
    heads_per_step = min(heads_per_step, features // HD)

    def body(scalars, ins, outs):
        q_t, k_t, v_t = ins
        (attended,) = outs

        def group(step, carry):
            def head_rows(h):
                return pl.ds(pl.multiple_of((step * heads_per_step + h) * HD, HD), HD)

            def scores(h, at):
                k1, k2, k3 = split3(k_t[head_rows(h), :])
                q1, q2, q3 = split3(q_t[head_rows(h), at : at + chunk])
                return lax.dot_general(
                    jnp.concatenate([k1, k2, k1, k3, k2, k1], axis=0),
                    jnp.concatenate([q1, q1, q2, q1, q2, q3], axis=0),
                    (((0,), (0,)), ((), ())),
                    preferred_element_type=F32,
                )

            items = [(h, at) for h in range(heads_per_step) for at in range(0, count, chunk)]
            current = scores(*items[0])
            for i, (h, at) in enumerate(items):
                following = scores(*items[i + 1]) if i + 1 < len(items) else None
                v1, v2 = split2(v_t[head_rows(h), :])
                ones = jnp.ones_like(v1)
                weights = jnp.exp2(current - jnp.max(current, axis=0, keepdims=True))
                high, low = split2(weights)
                first = jnp.dot(
                    jnp.concatenate([v1, v2, ones], axis=0), high, preferred_element_type=F32
                )
                second = jnp.dot(
                    jnp.concatenate([v1, ones], axis=0), low, preferred_element_type=F32
                )
                total = first[:HD] + first[HD : 2 * HD] + second[:HD]
                norm = first[2 * HD : 2 * HD + 1] + second[HD : HD + 1]
                attended[head_rows(h), at : at + chunk] = total / norm
                current = following
            return carry

        steps = features // HD // heads_per_step
        if steps == 1:
            group(0, 0)
        else:
            lax.fori_loop(0, steps, group, 0)

    (attended,) = launch(
        body,
        "attention",
        [],
        [q_t, k_t, v_t],
        [(features, count)],
        after=after,
        flops=10**9,
        exps=features // HD * rows * count,
    )
    return attended


def output_rows(attended, units, residual=None, after=()):
    width = units[0].shape[-1]
    count = attended.shape[1]
    more = [] if residual is None else [residual]

    def body(scalars, ins, outs):
        attended, units = ins[0], ins[1 : 1 + len(units_in)]
        w_out = split2(jnp.concatenate([u[3] for u in units], axis=0))
        result = dot3(split2(attended[...].T), w_out)
        if more:
            result = result + ins[-1][...]
        outs[0][...] = result

    units_in = units
    (out,) = launch(
        body, "output_rows", [], [attended] + units + more, [(count, width)], after=after
    )
    return out


def sum_rows(keep, received, after=()):
    def body(scalars, ins, outs):
        outs[0][...] = functools.reduce(jnp.add, [x[...] for x in ins])

    (out,) = launch(body, "sum_rows", [], [keep] + received, [keep.shape], after=after)
    return out


def cut_units(firsts, seconds, after=()):
    kinds, count, width = firsts[0].shape
    size = count // 2
    total = len(firsts)

    def body(scalars, ins, outs):
        for x, out in zip(ins[:total], outs[:total]):
            out[...] = x[:, :size, :]
        for x, out in zip(ins[total:], outs[total:]):
            out[...] = x[:, size:, :]

    arrays = [*firsts, *seconds]
    halves = launch(
        body, "cut_units", [], arrays, [(kinds, size, width)] * len(arrays), after=after
    )
    return halves[:total], halves[total:]


def sum_pairs(own, received, after=()):
    def body(scalars, ins, outs):
        for k, out in enumerate(outs):
            out[...] = ins[k][...] + ins[len(own) + k][...]

    return launch(body, "sum_pairs", [], own + received, [x.shape for x in own], after=after)


def join_units(units, after=()):
    kinds, count, width = units[0].shape

    def body(scalars, ins, outs):
        for i, x in enumerate(ins):
            outs[0][:, i * count : (i + 1) * count, :] = x[...]

    shape = (kinds, len(units) * count, width)
    (out,) = launch(body, "join_units", [], units, [shape], after=after)
    return out


def share_rows(place, units, shares, after=()):
    width = units[0].shape[-1]
    sizes = [u.shape[1] // (4 * n) for u, n in zip(units, shares)]

    def body(scalars, ins, outs):
        at = 0
        for ref, size, n in zip(ins, sizes, shares):
            start = pl.multiple_of(scalars[0][6] * (n * size), size)
            for j in range(ref.shape[0]):
                outs[0][at : at + size, :] = ref[j, pl.ds(start, size), :]
                at += size

    total = sum(u.shape[0] * size for u, size in zip(units, sizes))
    (out,) = launch(body, "share_rows", [place], units, [(total, width)], after=after)
    return out


def second_share(place, unit, after=()):
    def body(scalars, ins, outs):
        outs[0][...] = sliced(ins[0], scalars[0][6] * 2 + 1, 8)

    kinds, count, width = unit.shape
    (out,) = launch(
        body, "second_share", [place], [unit], [(kinds, count // 8, width)], after=after
    )
    return out


def units_of_rows(rows, units, shares, after=()):
    shapes = [(u.shape[0], u.shape[1] // (4 * n), u.shape[2]) for u, n in zip(units, shares)]

    def body(scalars, ins, outs):
        at = 0
        for out in outs:
            size = out.shape[1]
            for j in range(out.shape[0]):
                out[j] = ins[0][at : at + size, :]
                at += size

    return launch(body, "units_of_rows", [], [rows], shapes, after=after)


def relay(arrays, after):
    def body(scalars, ins, outs):
        for x, out in zip(ins, outs):
            out[...] = x[...]

    return launch(body, "relay", [], arrays, [x.shape for x in arrays], after=after)


def split_weights(weights, after):
    def body(scalars, ins, outs):
        for out, part in zip(outs, split2(ins[0][...])):
            out[...] = part

    return launch(
        body, "split_weights", [], [], [weights.shape] * 2, after=after, hbm=[weights], kind=BF
    )


def hidden_units(normed, up, down):
    hidden = dot3(normed, up, (((1,), (1,)), ((), ())))
    hidden = split2(hidden * (0.5 + 0.5 * lax.erf(hidden * 0.5**0.5)))
    return dot3(hidden, down)


def features_of(partial, col, rep, cols, reps):
    feature = partial.shape[1] // (cols * reps)
    for k in range(cols):
        for j in range(reps):
            to_rep = lax.rem(rep + j, reps)
            to_col = lax.rem(col + k, cols)
            if feature % 128 == 0:
                at = pl.multiple_of((to_col * reps + to_rep) * feature, 128)
                yield partial[:, pl.ds(at, feature)]
            else:
                at = pl.multiple_of(to_col * reps * feature, 128)
                slab = partial[:, pl.ds(at, reps * feature)]
                yield jnp.where(to_rep == 0, slab[:, :feature], slab[:, feature:])


def mlp(place, pieces, gain, layer, units):
    cols, reps = lax.axis_size("col"), len(pieces)
    part, width = pieces[0].shape
    rows = part * reps
    hidden = sum(u.shape[1] for u in units)

    def body(scalars, ins, outs, partial):
        (place,) = scalars
        pieces, units = ins[:reps], ins[reps + 1 :]
        gain = ins[reps][layer : layer + 1, :]
        col, rep = place[0], place[1]
        up, down = (split2(jnp.concatenate([u[j] for u in units], axis=0)) for j in range(2))
        for k in range(reps):
            here = pl.ds(pl.multiple_of(lax.rem(rep + reps - k, reps) * part, 128), part)
            values = pieces[k][...]
            high, low = split2(layer_norm(values, gain))
            outs[-2][here, :] = high
            outs[-1][here, :] = low
            result = hidden_units((high, low), up, down)
            partial[here, :] = result + values if k == 0 else result
        for out, values in zip(outs, features_of(partial, col, rep, cols, reps)):
            out[...] = values

    *outs, high, low = launch(
        body,
        "mlp",
        [place],
        pieces + [gain] + units,
        [(rows, width // (cols * reps))] * (cols * reps) + [((rows, width), BF)] * 2,
        [(rows, width)],
        flops=4 * rows * width * hidden * 3,
    )
    return outs, (high, low)


def mlp_rest(place, normed, units, base):
    cols, reps = lax.axis_size("col"), lax.axis_size("rep")
    rows, width = normed[0].shape

    def body(scalars, ins, outs, partial):
        (place,) = scalars
        base, units = ins[2 : 2 + len(outs)], ins[2 + len(outs) :]
        up, down = (split2(jnp.concatenate([u[j] for u in units], axis=0)) for j in range(2))
        partial[...] = hidden_units((ins[0][...], ins[1][...]), up, down)
        shares = features_of(partial, place[0], place[1], cols, reps)
        for out, values, before in zip(outs, shares, base):
            out[...] = before[...] + values

    return launch(
        body,
        "mlp_rest",
        [place],
        [*normed, *base, *units],
        [x.shape for x in base],
        [(rows, width)],
        flops=10**9,
    )


def pooled_mlp(place, pieces, pillar, gain, layer, units):
    cols = lax.axis_size("col")
    part, width = pieces[0][0].shape
    half = 2 * part
    wide, lead, lead_step = tile_border(cols)
    tile_rows = TR // lax.axis_size("rep")
    count = -(-(tile_rows + BORDER) * wide // 8) * 8
    hidden = sum(u.shape[1] for u in units)

    def body(scalars, ins, outs):
        (place,) = scalars
        pieces, (pillar, gains), units = ins[:4], ins[4:6], ins[6:]
        gain = gains[layer : layer + 1, :]
        col, rep, tok, full_width = (place[i] for i in (0, 1, 2, 4))
        flat = lax.broadcasted_iota(jnp.int32, (count, 1), 0)
        row = (flat * (-(-(2**16) // wide))) >> 16
        column = flat - row * wide - lead
        cells = []
        for k in range(cols):
            for j in range(2):
                x = lax.rem(col + k, cols) * (TC - lead_step) + column
                y = tok * TR + lax.rem(rep + j, 2) * (tile_rows - BORDER) + row
                cells.append(jnp.where((x >= 0) & (x < full_width), y * full_width + x, -2))
        up, down = (split2(jnp.concatenate([u[j] for u in units], axis=0)) for j in range(2))
        cells = jnp.concatenate(cells, axis=0)
        chosen, summed = [], []
        for k in range(2):
            source = lax.rem(rep + k, 2) * part
            tokens_cells = pillar[:, pl.ds(pl.multiple_of(col * half + source, 128), part)]
            values = pieces[2 * k][...] + pieces[2 * k + 1][...]
            result = hidden_units(split2(layer_norm(values, gain)), up, down)
            if k == 0:
                result = result + values
            summed += split2(result)
            chosen += [jnp.where(cells == tokens_cells, 1.0, 0.0).astype(BF)] * 2
        totals = jnp.dot(
            jnp.concatenate(chosen, axis=1),
            jnp.concatenate(summed, axis=0),
            preferred_element_type=F32,
        )
        for i in range(2 * cols):
            outs[i][...] = totals[i * count : (i + 1) * count]

    outs = launch(
        body,
        "mlp_pool",
        [place],
        [x for pair in pieces for x in pair] + [pillar, gain] + units,
        [(count, width)] * (2 * cols),
        flops=4 * half * width * hidden * 3,
    )
    return outs[::2], outs[1::2]


def tile_border(cols):
    return (TC + BORDER, 0, BORDER) if cols == 2 else (TC + 2 * BORDER, BORDER, 0)


def block_capacity(count, peers):
    return max(2, (count + peers - 4) // (peers - 1))


def pack_blocks(place, gathered, dest_device, dest_slot, after=()):
    cols, reps, toks = (lax.axis_size(a) for a in ("col", "rep", "tok"))
    count = dest_device.shape[0]
    each = count // (reps * cols)
    rows, feature = gathered[0].shape
    size = rows // (reps * each)
    capacity = block_capacity(count, toks)
    codes = capacity * size
    length = codes + -(-capacity // 8) * 8

    def body(scalars, ins, outs, blocks, packed):
        place, device, slot = scalars
        col, tok = place[0], place[2]
        for k in range(cols):
            blocks[k * rows : (k + 1) * rows, :] = ins[k][...]
        for k in range(toks):
            packed[k * length + codes : (k + 1) * length, :] = jnp.zeros(
                (length - codes, feature), F32
            )
        targets = [device[b] for b in range(count)]
        for b in range(count):
            rank = jnp.int32(0)
            for earlier in targets[:b]:
                rank = rank + (earlier == targets[b]).astype(jnp.int32)
            shift = lax.rem(targets[b] - tok + toks, toks)
            of_rep, of_col = b // (each * cols), b // each % cols
            position = (lax.rem(col - of_col + cols, cols) * reps + of_rep) * each + b % each
            start = shift * length
            packed[pl.ds(pl.multiple_of(start + rank * size, 8), size), :] = blocks[
                pl.ds(pl.multiple_of(position * size, 8), size), :
            ]
            code = jnp.full((1, feature), (slot[b] + 1).astype(F32))
            packed[pl.ds(start + codes + rank, 1), :] = code
        for k in range(toks):
            outs[k][...] = packed[k * length : (k + 1) * length, :]

    return launch(
        body,
        "pack_blocks",
        [place, dest_device, dest_slot],
        list(gathered),
        [(length, feature)] * toks,
        [(cols * rows, feature), (toks * length, feature)],
        after,
    )


def place_blocks(incoming, count, size, after=()):
    feature = incoming[0].shape[1]
    capacity = block_capacity(count, len(incoming))

    def body(scalars, ins, outs):
        codes = [
            [jnp.max(x[capacity * size + j : capacity * size + j + 1, :]) for j in range(capacity)]
            for x in ins
        ]
        for x, slots in zip(ins, codes):
            for j, code in enumerate(slots):
                slot = code.astype(jnp.int32) - 1

                @pl.when(slot >= 0)
                def _(x=x, j=j, slot=slot):
                    at = pl.multiple_of(slot * size, 8)
                    outs[0][pl.ds(at, size), :] = x[j * size : (j + 1) * size, :]

    (placed,) = launch(
        body, "place_blocks", [], list(incoming), [(count * size, feature)], after=after
    )
    return placed


def sum_tiles(place, own, received):
    count = len(own)
    wide = tile_border(count)[0]
    edge = BORDER * wide
    last = TR // lax.axis_size("rep") * wide
    width = own[0].shape[1]

    def body(scalars, ins, outs):
        rep = scalars[0][1]
        for k in range(count):
            total = ins[k][...] + ins[count + k][...]
            outs[k][...] = total
            outs[count + k][...] = jnp.where(
                rep == 0, total[:edge], total[last : last + edge]
            )

    outs = launch(
        body,
        "sum_tiles",
        [place],
        list(own) + received,
        [x.shape for x in own] + [(edge, width)] * count,
    )
    return list(outs[:count]), list(outs[count:])


def raster_kernel(reps, cols, scalars, ins, outs, cells, normed):
    (place,) = scalars
    tiles, halos = ins[:cols], ins[cols : 2 * cols]
    depth, gain, point_high, point_low = ins[2 * cols :]
    (out_ref,) = outs
    tok, col, rep, height, full_width = (place[i] for i in (2, 0, 1, 3, 4))
    tile_rows = out_ref.shape[0]
    tile_cols = out_ref.shape[1]
    width = out_ref.shape[2]
    wide = tile_border(cols)[0]
    kept = tile_rows + BORDER
    padded = cells.shape[1]
    cells[...] = jnp.zeros_like(cells)
    normed[:, :8, :] = jnp.zeros((normed.shape[0], 8, width), F32)
    normed[:, 8 + padded :, :] = jnp.zeros((normed.shape[0], 8, width), F32)
    full = tile_cols + 2 * BORDER

    def row_of(arrays, i):
        values = functools.reduce(jnp.add, [x[i * wide : (i + 1) * wide, :] for x in arrays])
        if wide < full:
            none = jnp.zeros((full - wide, width), F32)
            values = jnp.where(
                col == 0,
                jnp.concatenate([none, values], axis=0),
                jnp.concatenate([values, none], axis=0),
            )
        return values

    first = BORDER * (1 - rep)
    for i in range(kept):
        cells[first + i, 0:full, :] = row_of(tiles, i)
    other = (tile_rows + BORDER) * rep
    for i in range(BORDER):
        cells[other + i, 0:full, :] = row_of(halos, i)
    lead = 8
    row_zero = tok * (tile_rows * reps) + rep * tile_rows - BORDER
    col_zero = col * tile_cols - BORDER
    for layer in range(2):
        rim = layer + 1
        grid_rows = tile_rows + 2 * BORDER - 2 * rim
        low_col, span = (0, padded) if layer == 0 else (BORDER, tile_cols)
        values = cells[...]
        mean = jnp.mean(values * values, axis=-1, keepdims=True)
        normed[:, lead : lead + padded, :] = values * lax.rsqrt(mean + EPSILON) * gain[layer : layer + 1]
        mixed = None
        for b in range(3):
            start = lead + low_col + b - 1
            shifted = normed[rim - 1 : rim + 1 + grid_rows, start : start + span, :]
            for a in range(3):
                i = layer * 9 + a * 3 + b
                term = shifted[a : a + grid_rows] * depth[i : i + 1, :][None]
                mixed = term if mixed is None else mixed + term
        left = split2(mixed.reshape(grid_rows * span, width))
        value = dot3(left, (point_high[layer, :, :width], point_low[layer, :, :width]))
        gate = dot3(left, (point_high[layer, :, width:], point_low[layer, :, width:]))
        change = (value * jax.nn.sigmoid(gate)).reshape(grid_rows, span, width)
        centre = cells[rim : rim + grid_rows, low_col : low_col + span, :]
        if layer == 0:
            row = row_zero + rim + lax.broadcasted_iota(jnp.int32, (grid_rows, span, 1), 0)
            column = col_zero + lax.broadcasted_iota(jnp.int32, (grid_rows, span, 1), 1)
            inside = (row >= 0) & (row < height) & (column >= 0) & (column < full_width)
            cells[rim : rim + grid_rows, :, :] = jnp.where(inside, centre + change, 0.0)
        else:
            out_ref[...] = centre + change


def raster_layers(place, tiles, halos, depth, point, gain, tile_rows):
    reps = lax.axis_size("rep")
    width = depth.shape[-1]
    padded = -(-(TC + 2 * BORDER) // 8) * 8
    kernel = functools.partial(raster_kernel, reps, len(tiles))
    arrays = [*tiles, *halos, depth, gain, *point]
    count = 1 + len(arrays)
    return pl.pallas_call(
        lambda *refs: kernel(refs[:1], refs[1:count], refs[count : count + 1], *refs[count + 1 :]),
        in_specs=[pl.BlockSpec(memory_space=pltpu.SMEM)]
        + [pl.BlockSpec(memory_space=pltpu.VMEM)] * len(arrays),
        out_specs=pl.BlockSpec(memory_space=pltpu.VMEM),
        out_shape=jax.ShapeDtypeStruct((tile_rows, TC, width), F32),
        scratch_shapes=[
            pltpu.VMEM((tile_rows + 2 * BORDER, padded, width), F32),
            pltpu.VMEM((tile_rows + 2 * BORDER, padded + 16, width), F32),
        ],
        compiler_params=pltpu.CompilerParams(vmem_limit_bytes=VMEM_LIMIT),
        name="raster",
    )(place, *[pltpu.with_memory_space_constraint(x, pltpu.VMEM) for x in arrays])


def on_device(
    tokens,
    w_qkv,
    w_out,
    w_up,
    w_down,
    attn_gain,
    mlp_gain,
    dest_device,
    dest_slot,
    pillar,
    depth_weight,
    point_weight,
    raster_gain,
):
    cols, reps, toks = (lax.axis_size(a) for a in ("col", "rep", "tok"))
    tok, col, rep = (lax.axis_index(a) for a in ("tok", "col", "rep"))
    swap = shift_by(1, reps)
    scene_swap = shift_by(1, lax.axis_size("scene"))
    scene = lax.axis_index("scene")
    numbers = [col, rep, tok, TR * toks, TC * cols, scene, scene * 2 + tok % 2]
    place = jnp.stack([jnp.int32(n) for n in numbers])
    to_cols = lambda x: [lax.ppermute(x, "col", shift_by(k, cols)) for k in range(1, cols)]
    to_next = lambda xs: [lax.ppermute(x, "tok", [(i, i ^ 1) for i in range(toks)]) for x in xs]
    to_scene = lambda xs: [lax.ppermute(x, "scene", scene_swap) for x in xs]

    slabs = gather_slabs(tokens)
    heads0, hidden0, heads1, hidden1, own_hidden0, depth = prepare(
        place, w_qkv, w_out, w_up, w_down, depth_weight
    )
    units = [heads0, lax.ppermute(heads0, "rep", swap)]
    direct0 = to_cols(own_hidden0)
    q_parts, k_t, v_t, x_keep = project(place, slabs, attn_gain, 0, units, "rep")
    received = []
    for k in range(1, cols):
        part = output_rows(attention(q_parts[k], k_t, v_t), units)
        received.append(lax.ppermute(part, "col", shift_by(k, cols)))
    direct0 = relay(direct0, [part])
    next0, passed0 = to_next(direct0), to_scene(direct0)
    keep = output_rows(attention(q_parts[0], k_t, v_t, direct0), units, x_keep)
    point = split_weights(point_weight, [keep])
    keep = sum_rows(keep, received, point)
    far_rows = to_cols(
        share_rows(place, [heads1, hidden1], (1, 2), [keep, *next0, *passed0])
    )
    next_half, passed_half = cut_units(next0, passed0, [keep])
    pieces = [keep, lax.ppermute(keep, "rep", swap)]
    last0 = to_scene(next_half) + to_next(passed_half)
    outs, normed = mlp(place, pieces, mlp_gain, 0, [hidden0, *direct0, *passed0, *next0])
    outs = mlp_rest(place, normed, last0, outs)
    others = [lax.ppermute(x, "rep", swap) for x in outs[1::2]]
    parts = sum_pairs(list(outs[::2]), others)
    divided = [units_of_rows(x, [heads1, hidden1], (1, 2), parts[:1]) for x in far_rows]
    passed_rows = to_scene(relay(far_rows, parts[:1]))
    next_heads1 = to_next([x[0] for x in divided])
    gathered = [parts[0]] + [
        lax.ppermute(parts[k], "col", shift_by(k, cols)) for k in range(1, cols)
    ]
    outgoing = pack_blocks(place, gathered, dest_device, dest_slot, next_heads1)
    rest = to_cols(second_share(place, hidden1, divided[0][:1]))
    passed_rest = to_scene(rest)
    incoming = [outgoing[0]] + [
        lax.ppermute(outgoing[k], "tok", shift_by(k, toks)) for k in range(1, toks)
    ]
    passed = [units_of_rows(x, [heads1, hidden1], (1, 2)) for x in passed_rows]
    passed_heads1 = to_scene(next_heads1)
    far_heads1 = [x[0] for x in divided + passed] + next_heads1 + passed_heads1
    count = dest_device.shape[0]
    moved = place_blocks(incoming, count, tokens.shape[0] // count, [x[1] for x in passed] + passed_heads1 + rest)
    slabs = gather_slabs(moved)
    far_hidden1 = [
        join_units([x[1], y[1], z, w], [moved])
        for x, y, z, w in zip(divided, passed, rest, passed_rest)
    ]
    next1 = to_next(far_hidden1)

    units = [heads1] + far_heads1
    q_parts, k_t, v_t, x_keep = project(place, slabs, attn_gain, 1, units, "col")
    other_part = output_rows(attention(q_parts[1], k_t, v_t), units)
    own_part = output_rows(attention(q_parts[0], k_t, v_t), units, x_keep, next1)
    from_rep = lambda x: lax.ppermute(x, "rep", swap)
    own, other = pooled_mlp(
        place,
        [(own_part, from_rep(other_part)), (other_part, from_rep(own_part))],
        pillar[None],
        mlp_gain,
        1,
        [hidden1, *far_hidden1, *next1],
    )
    sums, edges = sum_tiles(place, own, [from_rep(x) for x in other])
    tiles = [sums[0]] + [lax.ppermute(sums[k], "col", shift_by(k, cols)) for k in range(1, cols)]
    at = lambda t, c, r: (t * cols + c % cols) * reps + r
    halos = [
        lax.ppermute(
            edges[k],
            ("tok", "col", "rep"),
            [(at(t, c, reps - 1), at(t + 1, c + k, 0)) for t in range(toks - 1) for c in range(cols)]
            + [(at(t + 1, c, 0), at(t, c + k, reps - 1)) for t in range(toks - 1) for c in range(cols)],
        )
        for k in range(cols)
    ]
    return raster_layers(place, tiles, halos, depth, point, raster_gain, TR // reps)


def solution(mesh):
    placed = (
        P(("scene", "tok"), ("col", "rep")),
        P(None, None, None, ("col", "rep")),
        P(None, ("col", "rep"), None),
        P(None, None, ("col", "rep")),
        P(None, ("col", "rep"), None),
        P(),
        P(),
        P(("scene", "tok")),
        P(("scene", "tok")),
        P(("scene", "tok")),
        P(),
        P(),
        P(),
    )
    return jax.shard_map(
        on_device,
        mesh=mesh,
        in_specs=placed,
        out_specs=P(("scene", "tok", "rep"), "col", None),
        check_vma=False,
    )
```

```python
import functools

import jax
import jax.numpy as jnp
from jax import lax
from jax.experimental import pallas as pl
from jax.experimental.pallas import tpu as pltpu
from jax.sharding import PartitionSpec as P

PATCH = 1024
TR = 16
TC = 16
HD = 16
EPSILON = 1e-05
LOG2E = 1.4426950408889634
BF = jnp.bfloat16
F32 = jnp.float32
VMEM_LIMIT = 32 * 2**20
BORDER = 2


def typed(shape, kind):
    return shape if isinstance(shape[0], tuple) else (shape, kind)


def launch(body, name, scalars, arrays, outs, scratch=(), after=(), hbm=(), flops=0, exps=0, kind=F32):
    counts = [len(scalars), len(arrays) + len(hbm), len(after), len(outs)]
    starts = [sum(counts[:i]) for i in range(5)]

    def kernel(*refs):
        body(
            refs[: starts[1]],
            refs[starts[1] : starts[2]],
            refs[starts[3] : starts[4]],
            *refs[starts[4] :],
        )

    return pl.pallas_call(
        kernel,
        in_specs=[pl.BlockSpec(memory_space=pltpu.SMEM)] * counts[0]
        + [pl.BlockSpec(memory_space=pltpu.VMEM)] * counts[1]
        + [pl.BlockSpec(memory_space=pl.ANY)] * counts[2],
        out_specs=[pl.BlockSpec(memory_space=pltpu.VMEM)] * counts[3],
        out_shape=[pltpu.VMEM(*typed(x, kind)) for x in outs],
        scratch_shapes=[pltpu.VMEM(*typed(x, F32)) for x in scratch],
        compiler_params=pltpu.CompilerParams(vmem_limit_bytes=VMEM_LIMIT),
        cost_estimate=pl.CostEstimate(flops=flops, bytes_accessed=0, transcendentals=exps),
        name=name,
    )(
        *scalars,
        *[pltpu.with_memory_space_constraint(x, pltpu.VMEM) for x in arrays],
        *hbm,
        *after,
    )


def split2(x):
    high = x.astype(BF)
    return high, (x - high.astype(F32)).astype(BF)


def split3(x):
    first = x.astype(BF)
    rest = x - first.astype(F32)
    second = rest.astype(BF)
    return first, second, (rest - second.astype(F32)).astype(BF)


def dot3(left, right, dims=(((1,), (0,)), ((), ()))):
    lh, ll = left
    rh, rl = right
    dot = functools.partial(lax.dot_general, dimension_numbers=dims, preferred_element_type=F32)
    if lh.shape[1] % 128:
        return dot(lh, rh) + dot(lh, rl) + dot(ll, rh)
    lefts = jnp.concatenate([lh, lh, ll], axis=1)
    return dot(lefts, jnp.concatenate([rh, rl, rh], axis=dims[0][1][0]))


def layer_norm(values, gain_row):
    average = jnp.mean(values, axis=-1, keepdims=True)
    centered = values - average
    variance = jnp.mean(centered * centered, axis=-1, keepdims=True)
    return centered * lax.rsqrt(variance + EPSILON) * gain_row


def shift_by(k, count):
    return [(i, (i + k) % count) for i in range(count)]


def gather_slabs(piece):
    cols = lax.axis_size("col")
    reps = lax.axis_size("rep")
    far = [lax.ppermute(piece, "col", shift_by(k, cols)) for k in range(1, cols)]
    return [(p, lax.ppermute(p, "rep", shift_by(1, reps))) for p in [piece] + far]


def sliced(ref, part, parts):
    size = ref.shape[1] // parts
    return ref[:, pl.ds(pl.multiple_of(part * size, size), size), :]


def prepare(place, w_qkv, w_out, w_up, w_down, depth_weight):
    width = w_out.shape[-1]
    features, hidden = w_out.shape[1], w_down.shape[1]

    def body(scalars, ins, outs):
        (place,) = scalars
        qkv, out, up, down, depth = ins
        for layer in range(2):
            for a in range(3):
                for b in range(3):
                    i = layer * 9 + a * 3 + b
                    outs[5][i : i + 1, :] = depth[layer, a, b : b + 1, :]
        for layer in range(2):
            heads, units = outs[2 * layer], outs[2 * layer + 1]
            for j in range(3):
                heads[j] = qkv[layer, j].T
            heads[3] = out[layer]
            units[0] = up[layer].T
            units[1] = down[layer]
        outs[4][...] = sliced(outs[1], place[6], 4)

    per_layer = [(4, features, width), (2, hidden, width)]
    return launch(
        body,
        "prepare",
        [place],
        [],
        per_layer * 2 + [(2, hidden // 4, width), (18, width)],
        hbm=[w_qkv, w_out, w_up, w_down, depth_weight],
        flops=8 * 10**9,
    )


def project(place, slabs, gain, layer, units, halves, after=()):
    cols = len(slabs)
    rows = slabs[0][0].shape[0]
    width = units[0].shape[-1]
    features = sum(u.shape[1] for u in units)
    half = rows // lax.axis_size(halves)
    parts = cols if halves == "rep" else lax.axis_size("rep")
    part = half // parts

    def body(scalars, ins, outs, x_all, norm_high, norm_low):
        (place,) = scalars
        pieces, units = ins[: 2 * cols], ins[2 * cols + 1 :]
        gain = ins[2 * cols][layer : layer + 1, :]
        q_parts, (k_t, v_t, x_keep) = outs[:parts], outs[parts:]
        col, rep = place[0], place[1]
        slab = width // cols
        for k in range(cols):
            near, other = pieces[2 * k][...], pieces[2 * k + 1][...]
            low = jnp.where(rep == 0, near, other)
            high = jnp.where(rep == 0, other, near)
            at = pl.multiple_of(lax.rem(col + cols - k, cols) * slab, 128)
            x_all[:, pl.ds(at, slab)] = jnp.concatenate([low, high], axis=1)
        weights = [split2(jnp.concatenate([u[j] for u in units], axis=0)) for j in range(3)]
        dims = (((1,), (1,)), ((), ()))
        chunk = 256
        for start in range(0, rows, chunk):
            here = slice(start, start + chunk)
            high, low = split2(layer_norm(x_all[here, :], gain))
            norm_high[here, :] = high
            norm_low[here, :] = low
            k_t[:, here] = dot3(weights[1], (high, low), dims)
            v_t[:, here] = dot3(weights[2], (high, low), dims)
        outer, inner = (rep, col) if halves == "rep" else (col, rep)
        for k in range(parts):
            at = outer * half + lax.rem(inner + k, parts) * part
            here = pl.ds(pl.multiple_of(at, part), part)
            if k == 0:
                x_keep[...] = x_all[here, :]
            normed = norm_high[here, :], norm_low[here, :]
            q_parts[k][...] = dot3(weights[0], normed, dims) * (LOG2E * HD**-0.5)

    *q_parts, k_t, v_t, x_keep = launch(
        body,
        "project",
        [place],
        [p for pair in slabs for p in pair] + [gain] + units,
        [(features, part)] * parts + [(features, rows)] * 2 + [(part, width)],
        [(rows, width)] + [((rows, width), BF)] * 2,
        after,
    )
    return q_parts, k_t, v_t, x_keep


def attention(q_t, k_t, v_t, after=(), heads_per_step=16):
    features, count = q_t.shape
    rows = k_t.shape[1]
    chunk = min(256, count)
    heads_per_step = min(heads_per_step, features // HD)

    def body(scalars, ins, outs):
        q_t, k_t, v_t = ins
        (attended,) = outs

        def group(step, carry):
            def head_rows(h):
                return pl.ds(pl.multiple_of((step * heads_per_step + h) * HD, HD), HD)

            def scores(h, at):
                k1, k2, k3 = split3(k_t[head_rows(h), :])
                q1, q2, q3 = split3(q_t[head_rows(h), at : at + chunk])
                return lax.dot_general(
                    jnp.concatenate([k1, k2, k1, k3, k2, k1], axis=0),
                    jnp.concatenate([q1, q1, q2, q1, q2, q3], axis=0),
                    (((0,), (0,)), ((), ())),
                    preferred_element_type=F32,
                )

            items = [(h, at) for h in range(heads_per_step) for at in range(0, count, chunk)]
            current = scores(*items[0])
            for i, (h, at) in enumerate(items):
                following = scores(*items[i + 1]) if i + 1 < len(items) else None
                v1, v2 = split2(v_t[head_rows(h), :])
                ones = jnp.ones_like(v1)
                weights = jnp.exp2(current - jnp.max(current, axis=0, keepdims=True))
                high, low = split2(weights)
                first = jnp.dot(
                    jnp.concatenate([v1, v2, ones], axis=0), high, preferred_element_type=F32
                )
                second = jnp.dot(
                    jnp.concatenate([v1, ones], axis=0), low, preferred_element_type=F32
                )
                total = first[:HD] + first[HD : 2 * HD] + second[:HD]
                norm = first[2 * HD : 2 * HD + 1] + second[HD : HD + 1]
                attended[head_rows(h), at : at + chunk] = total / norm
                current = following
            return carry

        steps = features // HD // heads_per_step
        if steps == 1:
            group(0, 0)
        else:
            lax.fori_loop(0, steps, group, 0)

    (attended,) = launch(
        body,
        "attention",
        [],
        [q_t, k_t, v_t],
        [(features, count)],
        after=after,
        flops=10**9,
        exps=features // HD * rows * count,
    )
    return attended


def output_rows(attended, units, residual=None, after=()):
    width = units[0].shape[-1]
    count = attended.shape[1]
    more = [] if residual is None else [residual]

    def body(scalars, ins, outs):
        attended, units = ins[0], ins[1 : 1 + len(units_in)]
        w_out = split2(jnp.concatenate([u[3] for u in units], axis=0))
        result = dot3(split2(attended[...].T), w_out)
        if more:
            result = result + ins[-1][...]
        outs[0][...] = result

    units_in = units
    (out,) = launch(
        body, "output_rows", [], [attended] + units + more, [(count, width)], after=after
    )
    return out


def sum_rows(keep, received, after=()):
    def body(scalars, ins, outs):
        outs[0][...] = functools.reduce(jnp.add, [x[...] for x in ins])

    (out,) = launch(body, "sum_rows", [], [keep] + received, [keep.shape], after=after)
    return out


def sum_pairs(own, received, after=()):
    def body(scalars, ins, outs):
        for k, out in enumerate(outs):
            out[...] = ins[k][...] + ins[len(own) + k][...]

    return launch(body, "sum_pairs", [], own + received, [x.shape for x in own], after=after)


def join_units(units, after=()):
    kinds, count, width = units[0].shape

    def body(scalars, ins, outs):
        for i, x in enumerate(ins):
            outs[0][:, i * count : (i + 1) * count, :] = x[...]

    shape = (kinds, len(units) * count, width)
    (out,) = launch(body, "join_units", [], units, [shape], after=after)
    return out


def share_rows(place, units, shares, firsts, seconds, after=()):
    width = units[0].shape[-1]
    sizes = [u.shape[1] // (4 * n) for u, n in zip(units, shares)]
    kinds, whole, _ = firsts[0].shape
    half = whole // 2
    total = len(firsts)

    def body(scalars, ins, outs):
        at = 0
        for ref, size, n in zip(ins, sizes, shares):
            start = pl.multiple_of(scalars[0][6] * (n * size), size)
            for j in range(ref.shape[0]):
                outs[0][at : at + size, :] = ref[j, pl.ds(start, size), :]
                at += size
        for i, (x, out) in enumerate(zip(ins[len(sizes) :], outs[1:])):
            out[...] = x[:, :half, :] if i < total else x[:, half:, :]

    count = sum(u.shape[0] * size for u, size in zip(units, sizes))
    arrays = [*units, *firsts, *seconds]
    halves = [(kinds, half, width)] * (len(firsts) + len(seconds))
    rows, *halves = launch(
        body, "share_rows", [place], arrays, [(count, width)] + halves, after=after
    )
    return rows, halves[:total], halves[total:]


def second_share(place, unit, after=()):
    def body(scalars, ins, outs):
        outs[0][...] = sliced(ins[0], scalars[0][6] * 2 + 1, 8)

    kinds, count, width = unit.shape
    (out,) = launch(
        body, "second_share", [place], [unit], [(kinds, count // 8, width)], after=after
    )
    return out


def units_of_rows(rows, units, shares, after=()):
    shapes = [(u.shape[0], u.shape[1] // (4 * n), u.shape[2]) for u, n in zip(units, shares)]

    def body(scalars, ins, outs):
        at = 0
        for out in outs:
            size = out.shape[1]
            for j in range(out.shape[0]):
                out[j] = ins[0][at : at + size, :]
                at += size

    return launch(body, "units_of_rows", [], [rows], shapes, after=after)


def relay(arrays, after):
    def body(scalars, ins, outs):
        for x, out in zip(ins, outs):
            out[...] = x[...]

    return launch(body, "relay", [], arrays, [x.shape for x in arrays], after=after)


def split_weights(weights, after):
    def body(scalars, ins, outs):
        for out, part in zip(outs, split2(ins[0][...])):
            out[...] = part

    return launch(
        body, "split_weights", [], [], [weights.shape] * 2, after=after, hbm=[weights], kind=BF
    )


def hidden_units(normed, up, down):
    hidden = dot3(normed, up, (((1,), (1,)), ((), ())))
    hidden = split2(hidden * (0.5 + 0.5 * lax.erf(hidden * 0.5**0.5)))
    return dot3(hidden, down)


def features_of(partial, col, rep, cols, reps):
    feature = partial.shape[1] // (cols * reps)
    for k in range(cols):
        for j in range(reps):
            to_rep = lax.rem(rep + j, reps)
            to_col = lax.rem(col + k, cols)
            if feature % 128 == 0:
                at = pl.multiple_of((to_col * reps + to_rep) * feature, 128)
                yield partial[:, pl.ds(at, feature)]
            else:
                at = pl.multiple_of(to_col * reps * feature, 128)
                slab = partial[:, pl.ds(at, reps * feature)]
                yield jnp.where(to_rep == 0, slab[:, :feature], slab[:, feature:])


def mlp(place, pieces, gain, layer, units):
    cols, reps = lax.axis_size("col"), len(pieces)
    part, width = pieces[0].shape
    rows = part * reps
    hidden = sum(u.shape[1] for u in units)

    def body(scalars, ins, outs, partial):
        (place,) = scalars
        pieces, units = ins[:reps], ins[reps + 1 :]
        gain = ins[reps][layer : layer + 1, :]
        col, rep = place[0], place[1]
        up, down = (split2(jnp.concatenate([u[j] for u in units], axis=0)) for j in range(2))
        for k in range(reps):
            here = pl.ds(pl.multiple_of(lax.rem(rep + reps - k, reps) * part, 128), part)
            values = pieces[k][...]
            high, low = split2(layer_norm(values, gain))
            outs[-2][here, :] = high
            outs[-1][here, :] = low
            result = hidden_units((high, low), up, down)
            partial[here, :] = result + values if k == 0 else result
        for out, values in zip(outs, features_of(partial, col, rep, cols, reps)):
            out[...] = values

    *outs, high, low = launch(
        body,
        "mlp",
        [place],
        pieces + [gain] + units,
        [(rows, width // (cols * reps))] * (cols * reps) + [((rows, width), BF)] * 2,
        [(rows, width)],
        flops=4 * rows * width * hidden * 3,
    )
    return outs, (high, low)


def mlp_rest(place, normed, units, base):
    cols, reps = lax.axis_size("col"), lax.axis_size("rep")
    rows, width = normed[0].shape

    def body(scalars, ins, outs, partial):
        (place,) = scalars
        base, units = ins[2 : 2 + len(outs)], ins[2 + len(outs) :]
        up, down = (split2(jnp.concatenate([u[j] for u in units], axis=0)) for j in range(2))
        partial[...] = hidden_units((ins[0][...], ins[1][...]), up, down)
        shares = features_of(partial, place[0], place[1], cols, reps)
        for out, values, before in zip(outs, shares, base):
            out[...] = before[...] + values

    return launch(
        body,
        "mlp_rest",
        [place],
        [*normed, *base, *units],
        [x.shape for x in base],
        [(rows, width)],
        flops=10**9,
    )


def pooled_mlp(place, pieces, pillar, gain, layer, units):
    cols = lax.axis_size("col")
    part, width = pieces[0][0].shape
    half = 2 * part
    wide, lead, lead_step = tile_border(cols)
    tile_rows = TR // lax.axis_size("rep")
    count = -(-(tile_rows + BORDER) * wide // 8) * 8
    hidden = sum(u.shape[1] for u in units)

    def body(scalars, ins, outs):
        (place,) = scalars
        pieces, (pillar, gains), units = ins[:4], ins[4:6], ins[6:]
        gain = gains[layer : layer + 1, :]
        col, rep, tok, full_width = (place[i] for i in (0, 1, 2, 4))
        flat = lax.broadcasted_iota(jnp.int32, (count, 1), 0)
        row = (flat * (-(-(2**16) // wide))) >> 16
        column = flat - row * wide - lead
        cells = []
        for k in range(cols):
            for j in range(2):
                x = lax.rem(col + k, cols) * (TC - lead_step) + column
                y = tok * TR + lax.rem(rep + j, 2) * (tile_rows - BORDER) + row
                cells.append(jnp.where((x >= 0) & (x < full_width), y * full_width + x, -2))
        up, down = (split2(jnp.concatenate([u[j] for u in units], axis=0)) for j in range(2))
        cells = jnp.concatenate(cells, axis=0)
        chosen, summed = [], []
        for k in range(2):
            source = lax.rem(rep + k, 2) * part
            tokens_cells = pillar[:, pl.ds(pl.multiple_of(col * half + source, 128), part)]
            values = pieces[2 * k][...] + pieces[2 * k + 1][...]
            result = hidden_units(split2(layer_norm(values, gain)), up, down)
            if k == 0:
                result = result + values
            summed += split2(result)
            chosen += [jnp.where(cells == tokens_cells, 1.0, 0.0).astype(BF)] * 2
        totals = jnp.dot(
            jnp.concatenate(chosen, axis=1),
            jnp.concatenate(summed, axis=0),
            preferred_element_type=F32,
        )
        for i in range(2 * cols):
            outs[i][...] = totals[i * count : (i + 1) * count]

    outs = launch(
        body,
        "mlp_pool",
        [place],
        [x for pair in pieces for x in pair] + [pillar, gain] + units,
        [(count, width)] * (2 * cols),
        flops=4 * half * width * hidden * 3,
    )
    return outs[::2], outs[1::2]


def tile_border(cols):
    return (TC + BORDER, 0, BORDER) if cols == 2 else (TC + 2 * BORDER, BORDER, 0)


def block_capacity(count, peers):
    return max(2, (count + peers - 4) // (peers - 1))


def pack_blocks(place, gathered, dest_device, dest_slot, after=()):
    cols, reps, toks = (lax.axis_size(a) for a in ("col", "rep", "tok"))
    count = dest_device.shape[0]
    each = count // (reps * cols)
    rows, feature = gathered[0].shape
    size = rows // (reps * each)
    capacity = block_capacity(count, toks)
    codes = capacity * size
    length = codes + -(-capacity // 8) * 8

    def body(scalars, ins, outs, blocks, packed):
        place, device, slot = scalars
        col, tok = place[0], place[2]
        for k in range(cols):
            blocks[k * rows : (k + 1) * rows, :] = ins[k][...]
        for k in range(toks):
            packed[k * length + codes : (k + 1) * length, :] = jnp.zeros(
                (length - codes, feature), F32
            )
        targets = [device[b] for b in range(count)]
        for b in range(count):
            rank = jnp.int32(0)
            for earlier in targets[:b]:
                rank = rank + (earlier == targets[b]).astype(jnp.int32)
            shift = lax.rem(targets[b] - tok + toks, toks)
            of_rep, of_col = b // (each * cols), b // each % cols
            position = (lax.rem(col - of_col + cols, cols) * reps + of_rep) * each + b % each
            start = shift * length
            packed[pl.ds(pl.multiple_of(start + rank * size, 8), size), :] = blocks[
                pl.ds(pl.multiple_of(position * size, 8), size), :
            ]
            code = jnp.full((1, feature), (slot[b] + 1).astype(F32))
            packed[pl.ds(start + codes + rank, 1), :] = code
        for k in range(toks):
            outs[k][...] = packed[k * length : (k + 1) * length, :]

    return launch(
        body,
        "pack_blocks",
        [place, dest_device, dest_slot],
        list(gathered),
        [(length, feature)] * toks,
        [(cols * rows, feature), (toks * length, feature)],
        after,
    )


def place_blocks(incoming, count, size, after=()):
    feature = incoming[0].shape[1]
    capacity = block_capacity(count, len(incoming))

    def body(scalars, ins, outs):
        codes = [
            [jnp.max(x[capacity * size + j : capacity * size + j + 1, :]) for j in range(capacity)]
            for x in ins
        ]
        for x, slots in zip(ins, codes):
            for j, code in enumerate(slots):
                slot = code.astype(jnp.int32) - 1

                @pl.when(slot >= 0)
                def _(x=x, j=j, slot=slot):
                    at = pl.multiple_of(slot * size, 8)
                    outs[0][pl.ds(at, size), :] = x[j * size : (j + 1) * size, :]

    (placed,) = launch(
        body, "place_blocks", [], list(incoming), [(count * size, feature)], after=after
    )
    return placed


def sum_tiles(place, own, received):
    count = len(own)
    wide = tile_border(count)[0]
    edge = BORDER * wide
    last = TR // lax.axis_size("rep") * wide
    width = own[0].shape[1]

    def body(scalars, ins, outs):
        rep = scalars[0][1]
        for k in range(count):
            total = ins[k][...] + ins[count + k][...]
            outs[k][...] = total
            outs[count + k][...] = jnp.where(
                rep == 0, total[:edge], total[last : last + edge]
            )

    outs = launch(
        body,
        "sum_tiles",
        [place],
        list(own) + received,
        [x.shape for x in own] + [(edge, width)] * count,
    )
    return list(outs[:count]), list(outs[count:])


def raster_kernel(reps, cols, scalars, ins, outs, cells, normed):
    (place,) = scalars
    tiles, halos = ins[:cols], ins[cols : 2 * cols]
    depth, gain, point_high, point_low = ins[2 * cols :]
    (out_ref,) = outs
    tok, col, rep, height, full_width = (place[i] for i in (2, 0, 1, 3, 4))
    tile_rows = out_ref.shape[0]
    tile_cols = out_ref.shape[1]
    width = out_ref.shape[2]
    wide = tile_border(cols)[0]
    kept = tile_rows + BORDER
    padded = cells.shape[1]
    cells[...] = jnp.zeros_like(cells)
    normed[:, :8, :] = jnp.zeros((normed.shape[0], 8, width), F32)
    normed[:, 8 + padded :, :] = jnp.zeros((normed.shape[0], 8, width), F32)
    full = tile_cols + 2 * BORDER

    def row_of(arrays, i):
        values = functools.reduce(jnp.add, [x[i * wide : (i + 1) * wide, :] for x in arrays])
        if wide < full:
            none = jnp.zeros((full - wide, width), F32)
            values = jnp.where(
                col == 0,
                jnp.concatenate([none, values], axis=0),
                jnp.concatenate([values, none], axis=0),
            )
        return values

    first = BORDER * (1 - rep)
    for i in range(kept):
        cells[first + i, 0:full, :] = row_of(tiles, i)
    other = (tile_rows + BORDER) * rep
    for i in range(BORDER):
        cells[other + i, 0:full, :] = row_of(halos, i)
    lead = 8
    row_zero = tok * (tile_rows * reps) + rep * tile_rows - BORDER
    col_zero = col * tile_cols - BORDER
    for layer in range(2):
        rim = layer + 1
        grid_rows = tile_rows + 2 * BORDER - 2 * rim
        low_col, span = (0, padded) if layer == 0 else (BORDER, tile_cols)
        values = cells[...]
        mean = jnp.mean(values * values, axis=-1, keepdims=True)
        normed[:, lead : lead + padded, :] = values * lax.rsqrt(mean + EPSILON) * gain[layer : layer + 1]
        mixed = None
        for b in range(3):
            start = lead + low_col + b - 1
            shifted = normed[rim - 1 : rim + 1 + grid_rows, start : start + span, :]
            for a in range(3):
                i = layer * 9 + a * 3 + b
                term = shifted[a : a + grid_rows] * depth[i : i + 1, :][None]
                mixed = term if mixed is None else mixed + term
        left = split2(mixed.reshape(grid_rows * span, width))
        value = dot3(left, (point_high[layer, :, :width], point_low[layer, :, :width]))
        gate = dot3(left, (point_high[layer, :, width:], point_low[layer, :, width:]))
        change = (value * jax.nn.sigmoid(gate)).reshape(grid_rows, span, width)
        centre = cells[rim : rim + grid_rows, low_col : low_col + span, :]
        if layer == 0:
            row = row_zero + rim + lax.broadcasted_iota(jnp.int32, (grid_rows, span, 1), 0)
            column = col_zero + lax.broadcasted_iota(jnp.int32, (grid_rows, span, 1), 1)
            inside = (row >= 0) & (row < height) & (column >= 0) & (column < full_width)
            cells[rim : rim + grid_rows, :, :] = jnp.where(inside, centre + change, 0.0)
        else:
            out_ref[...] = centre + change


def raster_layers(place, tiles, halos, depth, point, gain, tile_rows):
    reps = lax.axis_size("rep")
    width = depth.shape[-1]
    padded = -(-(TC + 2 * BORDER) // 8) * 8
    kernel = functools.partial(raster_kernel, reps, len(tiles))
    arrays = [*tiles, *halos, depth, gain, *point]
    count = 1 + len(arrays)
    return pl.pallas_call(
        lambda *refs: kernel(refs[:1], refs[1:count], refs[count : count + 1], *refs[count + 1 :]),
        in_specs=[pl.BlockSpec(memory_space=pltpu.SMEM)]
        + [pl.BlockSpec(memory_space=pltpu.VMEM)] * len(arrays),
        out_specs=pl.BlockSpec(memory_space=pltpu.VMEM),
        out_shape=jax.ShapeDtypeStruct((tile_rows, TC, width), F32),
        scratch_shapes=[
            pltpu.VMEM((tile_rows + 2 * BORDER, padded, width), F32),
            pltpu.VMEM((tile_rows + 2 * BORDER, padded + 16, width), F32),
        ],
        compiler_params=pltpu.CompilerParams(vmem_limit_bytes=VMEM_LIMIT),
        name="raster",
    )(place, *[pltpu.with_memory_space_constraint(x, pltpu.VMEM) for x in arrays])


def on_device(
    tokens,
    w_qkv,
    w_out,
    w_up,
    w_down,
    attn_gain,
    mlp_gain,
    dest_device,
    dest_slot,
    pillar,
    depth_weight,
    point_weight,
    raster_gain,
):
    cols, reps, toks = (lax.axis_size(a) for a in ("col", "rep", "tok"))
    tok, col, rep = (lax.axis_index(a) for a in ("tok", "col", "rep"))
    swap = shift_by(1, reps)
    scene_swap = shift_by(1, lax.axis_size("scene"))
    scene = lax.axis_index("scene")
    numbers = [col, rep, tok, TR * toks, TC * cols, scene, scene * 2 + tok % 2]
    place = jnp.stack([jnp.int32(n) for n in numbers])
    to_cols = lambda x: [lax.ppermute(x, "col", shift_by(k, cols)) for k in range(1, cols)]
    to_next = lambda xs: [lax.ppermute(x, "tok", [(i, i ^ 1) for i in range(toks)]) for x in xs]
    to_scene = lambda xs: [lax.ppermute(x, "scene", scene_swap) for x in xs]

    slabs = gather_slabs(tokens)
    heads0, hidden0, heads1, hidden1, own_hidden0, depth = prepare(
        place, w_qkv, w_out, w_up, w_down, depth_weight
    )
    units = [heads0, lax.ppermute(heads0, "rep", swap)]
    direct0 = to_cols(own_hidden0)
    q_parts, k_t, v_t, x_keep = project(place, slabs, attn_gain, 0, units, "rep")
    received = []
    for k in range(1, cols):
        part = output_rows(attention(q_parts[k], k_t, v_t), units)
        received.append(lax.ppermute(part, "col", shift_by(k, cols)))
    direct0 = relay(direct0, [part])
    next0, passed0 = to_next(direct0), to_scene(direct0)
    keep = output_rows(attention(q_parts[0], k_t, v_t, direct0), units, x_keep)
    point = split_weights(point_weight, [keep])
    keep = sum_rows(keep, received, point)
    own_rows, next_half, passed_half = share_rows(
        place, [heads1, hidden1], (1, 2), next0, passed0, [keep]
    )
    far_rows = to_cols(own_rows)
    pieces = [keep, lax.ppermute(keep, "rep", swap)]
    last0 = to_scene(next_half) + to_next(passed_half)
    outs, normed = mlp(place, pieces, mlp_gain, 0, [hidden0, *direct0, *passed0, *next0])
    outs = mlp_rest(place, normed, last0, outs)
    others = [lax.ppermute(x, "rep", swap) for x in outs[1::2]]
    parts = sum_pairs(list(outs[::2]), others)
    divided = [units_of_rows(x, [heads1, hidden1], (1, 2), parts[:1]) for x in far_rows]
    passed_rows = to_scene(relay(far_rows, parts[:1]))
    next_heads1 = to_next([x[0] for x in divided])
    gathered = [parts[0]] + [
        lax.ppermute(parts[k], "col", shift_by(k, cols)) for k in range(1, cols)
    ]
    outgoing = pack_blocks(place, gathered, dest_device, dest_slot, next_heads1)
    rest = to_cols(second_share(place, hidden1, divided[0][:1]))
    passed_rest = to_scene(rest)
    incoming = [outgoing[0]] + [
        lax.ppermute(outgoing[k], "tok", shift_by(k, toks)) for k in range(1, toks)
    ]
    passed = [units_of_rows(x, [heads1, hidden1], (1, 2)) for x in passed_rows]
    passed_heads1 = to_scene(next_heads1)
    far_heads1 = [x[0] for x in divided + passed] + next_heads1 + passed_heads1
    count = dest_device.shape[0]
    moved = place_blocks(incoming, count, tokens.shape[0] // count, [x[1] for x in passed] + passed_heads1 + rest)
    slabs = gather_slabs(moved)
    far_hidden1 = [
        join_units([x[1], y[1], z, w], [moved])
        for x, y, z, w in zip(divided, passed, rest, passed_rest)
    ]
    next1 = to_next(far_hidden1)

    units = [heads1] + far_heads1
    q_parts, k_t, v_t, x_keep = project(place, slabs, attn_gain, 1, units, "col")
    other_part = output_rows(attention(q_parts[1], k_t, v_t), units)
    own_part = output_rows(attention(q_parts[0], k_t, v_t), units, x_keep, next1)
    from_rep = lambda x: lax.ppermute(x, "rep", swap)
    own, other = pooled_mlp(
        place,
        [(own_part, from_rep(other_part)), (other_part, from_rep(own_part))],
        pillar[None],
        mlp_gain,
        1,
        [hidden1, *far_hidden1, *next1],
    )
    sums, edges = sum_tiles(place, own, [from_rep(x) for x in other])
    tiles = [sums[0]] + [lax.ppermute(sums[k], "col", shift_by(k, cols)) for k in range(1, cols)]
    at = lambda t, c, r: (t * cols + c % cols) * reps + r
    halos = [
        lax.ppermute(
            edges[k],
            ("tok", "col", "rep"),
            [(at(t, c, reps - 1), at(t + 1, c + k, 0)) for t in range(toks - 1) for c in range(cols)]
            + [(at(t + 1, c, 0), at(t, c + k, reps - 1)) for t in range(toks - 1) for c in range(cols)],
        )
        for k in range(cols)
    ]
    return raster_layers(place, tiles, halos, depth, point, raster_gain, TR // reps)


def solution(mesh):
    placed = (
        P(("scene", "tok"), ("col", "rep")),
        P(None, None, None, ("col", "rep")),
        P(None, ("col", "rep"), None),
        P(None, None, ("col", "rep")),
        P(None, ("col", "rep"), None),
        P(),
        P(),
        P(("scene", "tok")),
        P(("scene", "tok")),
        P(("scene", "tok")),
        P(),
        P(),
        P(),
    )
    return jax.shard_map(
        on_device,
        mesh=mesh,
        in_specs=placed,
        out_specs=P(("scene", "tok", "rep"), "col", None),
        check_vma=False,
    )
```
